512 devices in a mesh: dp: 128 (over z, y_lo, x), ctx: 4 (over y_hi, core).
Axes of the slice: x: 4, y: 4 (y_hi: 2, y_lo: 2; y = y_hi * 2 + y_lo), z: 16, core: 2. Of those that a mesh axis runs over, the one named last changes fastest.
Arguments:
- hidden: bfloat16 [65536, 1024], P(('dp', 'ctx')), may hold values from -80 to 80
- doc_len: int32 [128], P('dp'), may hold values from 256 to 512, as said below
- doc_keep: int32 [65536], P(('dp', 'ctx')), may hold values 0 or 1
- w_query: bfloat16 [1024, 512], replicated, may hold values from -1 to 1
- w_key: bfloat16 [1024, 512], replicated, may hold values from -1 to 1
- w_value: bfloat16 [1024, 512], replicated, may hold values from -0.1875 to 0.1875
- w_out: bfloat16 [512, 1024], replicated, may hold values from -0.25 to 0.25
- ln_gain: float32 [1024], replicated, may hold values from 0.5 to 2
- w_proj: bfloat16 [1024, 128], replicated, may hold values from -0.1875 to 0.1875
- queries: bfloat16 [512, 32, 128], P(('dp', 'ctx')), may hold values from -8.5 to 8.5
- query_mask: bfloat16 [512, 32], P(('dp', 'ctx')), may hold values from 0.19921875 to 1
- positive: int32 [512], P(('dp', 'ctx')), may hold values from 0 to 127
Outputs:
- d_hidden: bfloat16 [65536, 1024], P(('dp', 'ctx'))
- loss: float32 [], replicated
The draws below stay inside these ranges and needn't reach their ends.
Inputs may be any that keep to these rules, and one draw needn't show every extreme that they name: `doc_len`: some document has exactly 512 valid tokens and some exactly 256.
All inputs are finite; a program needn't handle non-finite values. No bound on the sum of `doc_keep` on one device may be relied on, other than what follows from the above.
Results may differ from the reference program's by a relative error of at most 0.035.
The reference program's roundings to bfloat16 on the way count: a program that leaves them out, or rounds other values in their place, can miss the bound.
Values may be sent and summed in bfloat16 or wider, within the bound.
No kernel may reach another device: no remote copies, remote signals or barrier semaphores. Data moves between devices by JAX's collectives and lax.ppermute only.
A program may use at most 64 MiB of HBM per device.

```python
import math
import jax
import jax.numpy as jnp
from jax import lax

D = 1024
HEADS = 8
HD = 64
E = 128
QLEN = 32
L = 512
DOCS = 128
QUERIES = 512
TOKENS = 65536


def draw_w_query(key, part):
    key = jax.random.fold_in(key, 13)
    out = jnp.clip(jax.random.normal(key, (D, HEADS * HD), jnp.float32), -6.0, 6.0) * D ** (-0.5)
    return out.astype(jnp.bfloat16)


def draw_w_key(key, part):
    key = jax.random.fold_in(key, 17)
    first, second = jax.random.split(key)
    gains = jnp.exp(jax.random.uniform(first, (1, HEADS * HD), jnp.float32, math.log(0.8), math.log(1.25)))
    out = jnp.clip(jax.random.normal(second, (D, HEADS * HD), jnp.float32), -6.0, 6.0) * D ** (-0.5) * gains
    return out.astype(jnp.bfloat16)


def doc_offsets(key):
    key_e, key_f, key_g = jax.random.split(key, 3)
    centres = jnp.clip(jax.random.normal(key_e, (4, D), jnp.float32), -6.0, 6.0) * 0.7
    cluster_of = jax.random.randint(key_f, (DOCS,), 0, 4)
    own_part = jnp.clip(jax.random.normal(key_g, (DOCS, D), jnp.float32), -6.0, 6.0) * 0.5
    return centres[cluster_of] + own_part


def draw_hidden(key, part):
    key = jax.random.fold_in(key, 7)
    key_a = jax.random.fold_in(key, 0)
    key_h = jax.random.fold_in(key, 4)
    count = DOCS * L
    base = jnp.clip(jax.random.normal(key_a, (count, D), jnp.float32), -6.0, 6.0)
    offset = doc_offsets(key_h)
    doc_rows = jnp.arange(count) // L
    shifted = base + offset[doc_rows]
    return jnp.clip(shifted, -80.0, 80.0).astype(jnp.bfloat16)


def draw_queries(key, part):
    key = jax.random.fold_in(key, 23)
    key_a, key_b = jax.random.split(key)
    topics = jnp.clip(jax.random.normal(key_a, (QUERIES, 1, E), jnp.float32), -6.0, 6.0)
    jitter = jnp.clip(jax.random.normal(key_b, (QUERIES, QLEN, E), jnp.float32), -6.0, 6.0)
    return (0.85 * topics + 0.5 * jitter).astype(jnp.bfloat16)


def draw_doc_len(key, part):
    key = jax.random.fold_in(key, 5)
    first, second = jax.random.split(key)
    lengths = jax.random.randint(first, (DOCS,), L // 2, L + 1)
    order = jax.random.permutation(second, DOCS)
    lengths = lengths.at[order[0]].set(L).at[order[1]].set(L // 2)
    return lengths.astype(jnp.int32)


def with_ends(array, stream_key, least, largest):
    longest = array.shape.index(max(array.shape))
    spots = []
    for shift in (0, 1):
        where = [jax.random.randint(jax.random.fold_in(stream_key, axis), (), 0, length) for axis, length in enumerate(array.shape)]
        where[longest] = (where[longest] + shift) % array.shape[longest]
        spots.append(tuple(where))
    return array.at[spots[0]].set(least).at[spots[1]].set(largest)


def level_of(own_key, dims, shards, least, top_value):
    loudness = 1.0
    for position, parts in shards:
        heights = jax.random.uniform(jax.random.fold_in(jax.random.fold_in(own_key, 6), position), (parts,), jnp.float32, least / len(shards), top_value / len(shards))
        loudness = loudness * jnp.repeat(jnp.exp(heights), dims[position] // parts).reshape((-1,) + (1,) * (len(dims) - 1 - position))
    return loudness


def gaussian(rng, dims, spread, most, held_as=jnp.bfloat16):
    return jnp.clip(spread * jax.random.normal(rng, dims, jnp.float32), -most, most).astype(held_as)


def setup_inputs(seed: int = 0) -> dict:
    keys = jax.random.split(jax.random.key(seed), 13)
    return {
        "hidden": draw_hidden(jax.random.fold_in(keys[12], 71), 0),
        "doc_len": draw_doc_len(jax.random.fold_in(keys[12], 71), 0),
        "doc_keep": with_ends((jax.random.randint(keys[2], (TOKENS,), 0, 10) < 9).astype(jnp.int32), jax.random.fold_in(keys[2], 1), 0, 1),
        "w_query": draw_w_query(jax.random.fold_in(keys[12], 71), 0),
        "w_key": draw_w_key(jax.random.fold_in(keys[12], 71), 0),
        "w_value": gaussian(keys[5], (D, HEADS * HD), D ** -0.5, 0.1875),
        "w_out": gaussian(keys[6], (HEADS * HD, D), (HEADS * HD) ** -0.5, 0.25),
        "ln_gain": jnp.clip(jnp.exp(jax.random.uniform(keys[7], (D,), jnp.float32, math.log(0.5), math.log(2.0))), 0.5, 2.0),
        "w_proj": gaussian(keys[8], (D, E), D ** -0.5, 0.1875),
        "queries": draw_queries(jax.random.fold_in(keys[12], 71), 0),
        "query_mask": jnp.clip(0.19921875 + 0.80078125 * jax.random.uniform(keys[10], (QUERIES, QLEN), jnp.float32) ** level_of(keys[10], (QUERIES, QLEN), ((0, 512),), -0.2, 0.2), 0.19921875, 1.0).astype(jnp.bfloat16),
        "positive": with_ends(jax.random.randint(keys[11], (QUERIES,), 0, DOCS), jax.random.fold_in(keys[11], 1), 0, DOCS - 1).astype(jnp.int32),
    }


TAU = 0.05
GRAD_SCALE = 1024.0
NEG = -1e+30

def dot32(left, right):
    return jnp.dot(left, right, preferred_element_type=jnp.float32)

def split_heads(t):
    return t.reshape(t.shape[0], -1, HD).astype(jnp.float32)

def forward_doc(x, length, skip, w_query, w_key, w_value, w_out, ln_gain, w_proj):
    place = jnp.arange(L, dtype=jnp.int32)
    valid = place < length
    keep = jnp.where(valid & ((skip == 1) | (place == 0)), 1.0, 0.0).astype(jnp.float32)
    query = dot32(x, w_query).astype(jnp.bfloat16)
    keyed = dot32(x, w_key).astype(jnp.bfloat16)
    value = dot32(x, w_value).astype(jnp.bfloat16)
    scores = jnp.einsum('rhc,jhc->hrj', split_heads(query), split_heads(keyed)) * HD ** (-0.5)
    scores = jnp.where(valid[None, None, :], scores, NEG)
    top = lax.optimization_barrier(jnp.max(scores, -1, keepdims=True))
    expo = jnp.exp(scores - top)
    probs = expo / lax.optimization_barrier(jnp.sum(expo, -1, keepdims=True))
    probs_b = probs.astype(jnp.bfloat16)
    attended = jnp.einsum('hrj,jhc->rhc', probs_b.astype(jnp.float32), split_heads(value))
    attended = attended.reshape(L, -1).astype(jnp.bfloat16)
    mixed = x.astype(jnp.float32) + dot32(attended, w_out)
    centred = mixed - lax.optimization_barrier(jnp.mean(mixed, -1, keepdims=True))
    inv = lax.rsqrt(lax.optimization_barrier(jnp.mean(centred * centred, -1, keepdims=True)) + 1e-05)
    unit = centred * inv
    normed = (unit * ln_gain).astype(jnp.bfloat16)
    proj = dot32(normed, w_proj)
    scale = lax.rsqrt(lax.optimization_barrier(jnp.sum(proj * proj, -1, keepdims=True)) + 1e-06)
    embed_f = proj * scale
    return (keep, query, keyed, value, probs, probs_b, attended, unit, inv, scale, embed_f)

def reference(hidden, doc_len, doc_keep, w_query, w_key, w_value, w_out, ln_gain, w_proj, queries, query_mask, positive):
    qfull = queries.astype(jnp.float32)
    qn = (qfull * lax.rsqrt(lax.optimization_barrier(jnp.sum(qfull * qfull, -1, keepdims=True)) + 1e-06)).astype(jnp.bfloat16)
    qn_f = qn.astype(jnp.float32)
    qmask = query_mask.astype(jnp.float32)
    docs_x = hidden.reshape(DOCS, L, D)
    skips = doc_keep.reshape(DOCS, L)

    def first(args):
        x, length, skip = args
        out = forward_doc(x, length, skip, w_query, w_key, w_value, w_out, ln_gain, w_proj)
        keep, embed_f = (out[0], out[10])
        embed = embed_f.astype(jnp.bfloat16).astype(jnp.float32)
        close = jnp.einsum('qie,je->qij', qn_f, embed)
        return lax.optimization_barrier(jnp.sum(jnp.exp(close / TAU) * keep, -1))
    sums = lax.map(first, (docs_x, doc_len, skips))
    table = lax.optimization_barrier(jnp.sum(qmask[None] * TAU * jnp.log(sums), -1))
    lse = jnp.log(lax.optimization_barrier(jnp.sum(jnp.exp(table), 0)))
    hit = jnp.arange(DOCS, dtype=jnp.int32)[:, None] == positive[None, :]
    target = lax.optimization_barrier(jnp.sum(jnp.where(hit, table, 0.0), 0))
    loss = jnp.sum(lse - target)
    dscore = GRAD_SCALE * (jnp.exp(table - lse[None, :]) - hit.astype(jnp.float32))

    def second(args):
        x, length, skip, drow, dsums = args
        keep, query, keyed, value, probs, probs_b, attended, unit, inv, scale, embed_f = forward_doc(x, length, skip, w_query, w_key, w_value, w_out, ln_gain, w_proj)
        embed = embed_f.astype(jnp.bfloat16).astype(jnp.float32)
        close = jnp.einsum('qie,je->qij', qn_f, embed)
        coef = drow[:, None] * qmask / dsums
        coupling = (jnp.exp(close / TAU) * keep * coef[..., None]).astype(jnp.bfloat16)
        embed_grad = jnp.einsum('qij,qie->je', coupling.astype(jnp.float32), qn_f)
        proj_grad = ((embed_grad - embed_f * lax.optimization_barrier(jnp.sum(embed_f * embed_grad, -1, keepdims=True))) * scale).astype(jnp.bfloat16)
        normed_grad = dot32(proj_grad, w_proj.T)
        gained = normed_grad * ln_gain
        mixed_grad = inv * (gained - lax.optimization_barrier(jnp.mean(gained, -1, keepdims=True)) - unit * lax.optimization_barrier(jnp.mean(gained * unit, -1, keepdims=True)))
        mixed_b = mixed_grad.astype(jnp.bfloat16)
        attended_grad = dot32(mixed_b, w_out.T).astype(jnp.bfloat16)
        delta = jnp.transpose(lax.optimization_barrier(jnp.sum(split_heads(attended_grad) * split_heads(attended), -1)))
        inner = jnp.einsum('rhc,jhc->hrj', split_heads(attended_grad), split_heads(value))
        score_grad = (probs * (inner - delta[..., None]) * HD ** (-0.5)).astype(jnp.bfloat16)
        sgf = score_grad.astype(jnp.float32)
        q_grad = jnp.einsum('hrj,jhc->rhc', sgf, split_heads(keyed)).reshape(L, -1).astype(jnp.bfloat16)
        k_grad = jnp.einsum('hrj,rhc->jhc', sgf, split_heads(query)).reshape(L, -1).astype(jnp.bfloat16)
        v_grad = jnp.einsum('hrj,rhc->jhc', probs_b.astype(jnp.float32), split_heads(attended_grad)).reshape(L, -1).astype(jnp.bfloat16)
        total = mixed_grad + dot32(q_grad, w_query.T) + dot32(k_grad, w_key.T) + dot32(v_grad, w_value.T)
        return total.astype(jnp.bfloat16)
    grads = lax.map(second, (docs_x, doc_len, skips, dscore, sums))
    return (grads.reshape(TOKENS, D), loss)
```

```python
import jax
import jax.numpy as jnp
import numpy as np
from jax import lax
from jax.sharding import Mesh, PartitionSpec as P

HD = 64
TAU = 0.05
GRAD_SCALE = 1024.0
NEG = -1e30
AXES = ("z", "ylo", "x", "yhi", "core")
SIZES = (16, 2, 4, 2, 2)
DP = ("z", "ylo", "x")
SWAP = [(0, 1), (1, 0)]
bf16 = jnp.bfloat16
f32 = jnp.float32


def dot32(left, right):
    return jnp.dot(left, right, preferred_element_type=f32)


def split_heads(t):
    return t.reshape(t.shape[0], -1, HD)


def spread(x, axes, count):
    return lax.all_to_all(jnp.broadcast_to(x[None], (count,) + x.shape), axes, 0, 0)


def body(
    hidden,
    doc_len,
    doc_keep,
    w_query,
    w_key,
    w_value,
    w_out,
    ln_gain,
    w_proj,
    queries,
    query_mask,
    positive,
):
    rows = hidden.shape[0]
    length = doc_len[0]
    me = lax.axis_index("yhi") * 2 + lax.axis_index("core")
    mine = lax.axis_index(DP)

    keep_rows = jnp.zeros((16, hidden.shape[1]), bf16).at[0, :rows].set(doc_keep.astype(bf16))
    own = jnp.concatenate([hidden, keep_rows], 0)
    by_core = lax.ppermute(own, "core", SWAP)
    by_yhi = lax.ppermute(own, "yhi", SWAP)
    by_both = lax.ppermute(by_yhi, "core", SWAP)
    blocks = (own, by_core, by_yhi, by_both)
    x = jnp.concatenate([b[:rows] for b in blocks], 0)
    skip = jnp.stack([b[rows, :rows] for b in blocks])
    place = (me ^ jnp.arange(4, dtype=jnp.int32))[:, None] * rows + jnp.arange(
        rows, dtype=jnp.int32
    )
    valid = (place < length).reshape(-1)
    keep = ((place < length) & ((skip == 1) | (place == 0))).astype(f32).reshape(-1)

    qfull = queries[0].astype(f32)
    qn = (qfull * lax.rsqrt(jnp.sum(qfull * qfull, -1, keepdims=True) + 1e-06)).astype(bf16)
    qlen, width = qn.shape
    extra = jnp.concatenate(
        [
            jnp.tile(query_mask, (1, width // qlen)),
            jnp.broadcast_to(positive[:, None].astype(bf16), (1, width)),
            jnp.zeros((14, width), bf16),
        ],
        0,
    )
    line = spread(jnp.concatenate([qn, extra], 0), "z", 16)
    line = jnp.concatenate(
        [line[:, :qlen].reshape(-1, width), line[:, qlen], line[:, qlen + 1]], 0
    )
    plane = spread(line, ("ylo", "x"), 8)
    qset = plane[:, : 16 * qlen].reshape(-1, width)
    qmask = plane[:, 16 * qlen : 16 * qlen + 16, :qlen].reshape(-1, qlen).astype(f32)
    pos = plane[:, 16 * qlen + 16 :, 0].reshape(-1).astype(jnp.int32)
    count = pos.shape[0]

    query = dot32(x, w_query).astype(bf16)
    keyed = dot32(x, w_key).astype(bf16)
    value = dot32(x, w_value).astype(bf16)
    scores = jnp.einsum(
        "rhc,jhc->hrj", split_heads(query), split_heads(keyed), preferred_element_type=f32
    ) * HD ** (-0.5)
    scores = jnp.where(valid[None, None, :], scores, NEG)
    top = jnp.max(scores, -1, keepdims=True)
    expo = jnp.exp(scores - top)
    denom = jnp.sum(expo, -1, keepdims=True)
    probs = expo / denom
    probs_b = probs.astype(bf16)
    attended = jnp.einsum("hrj,jhc->rhc", probs_b, split_heads(value), preferred_element_type=f32)
    attended = attended.reshape(x.shape[0], -1).astype(bf16)
    mixed = x.astype(f32) + dot32(attended, w_out)
    centred = mixed - jnp.mean(mixed, -1, keepdims=True)
    inv = lax.rsqrt(jnp.mean(centred * centred, -1, keepdims=True) + 1e-05)
    unit = centred * inv
    normed = (unit * ln_gain).astype(bf16)
    proj = dot32(normed, w_proj)
    scale = lax.rsqrt(jnp.sum(proj * proj, -1, keepdims=True) + 1e-06)
    embed_f = proj * scale
    embed = embed_f.astype(bf16)

    close = lax.dot_general(embed, qset, (((1,), (1,)), ((), ())), preferred_element_type=f32)
    near = jnp.exp(close / TAU) * keep[:, None]
    sums = jnp.sum(near, 0).reshape(count, qlen)
    column = jnp.sum(qmask * TAU * jnp.log(sums), -1)
    table = spread(column, DP, 128)
    lse = jnp.log(jnp.sum(jnp.exp(table), 0))
    hit = jnp.arange(128, dtype=jnp.int32)[:, None] == pos[None, :]
    loss_part = jnp.sum(lse - jnp.sum(jnp.where(hit, table, 0.0), 0))
    dscore = GRAD_SCALE * (jnp.exp(column - lse) - (pos == mine).astype(f32))
    coef = (dscore[:, None] * qmask / sums).reshape(-1)
    coupling = (near * coef[None, :]).astype(bf16)
    partial = dot32(coupling, qset)

    sent = jnp.concatenate([partial, jnp.broadcast_to(loss_part, (8, width))], 0)

    def blocks_of(t, order):
        return jnp.concatenate([t[o * rows : (o + 1) * rows] for o in order] + [t[4 * rows :]], 0)

    sent = sent + blocks_of(lax.ppermute(sent, "core", SWAP), (1, 0, 3, 2))
    sent = sent + blocks_of(lax.ppermute(sent, "yhi", SWAP), (2, 3, 0, 1))
    embed_grad = sent[: 4 * rows]
    loss = sent[4 * rows, 0]

    proj_grad = (
        (embed_grad - embed_f * jnp.sum(embed_f * embed_grad, -1, keepdims=True)) * scale
    ).astype(bf16)
    normed_grad = dot32(proj_grad, w_proj.T)
    gained = normed_grad * ln_gain
    mixed_grad = inv * (
        gained
        - jnp.mean(gained, -1, keepdims=True)
        - unit * jnp.mean(gained * unit, -1, keepdims=True)
    )
    mixed_b = mixed_grad.astype(bf16)
    attended_grad = dot32(mixed_b, w_out.T).astype(bf16)
    delta = jnp.transpose(
        jnp.sum(
            split_heads(attended_grad).astype(f32) * split_heads(attended).astype(f32),
            -1,
        )
    )[..., None]

    def score_grads(left, right, prob, off):
        inner = jnp.einsum(
            "rhc,jhc->hrj", split_heads(left), split_heads(right), preferred_element_type=f32
        )
        return (prob * (inner - off) * HD ** (-0.5)).astype(bf16)

    by_row = score_grads(attended_grad[:rows], value, probs[:, :rows], delta[:, :rows])
    by_col = score_grads(attended_grad, value[:rows], probs[:, :, :rows], delta)
    q_grad = jnp.einsum("hrj,jhc->rhc", by_row, split_heads(keyed), preferred_element_type=f32)
    k_grad = jnp.einsum("hrj,rhc->jhc", by_col, split_heads(query), preferred_element_type=f32)
    v_grad = jnp.einsum(
        "hrj,rhc->jhc",
        probs_b[:, :, :rows],
        split_heads(attended_grad),
        preferred_element_type=f32,
    )
    q_grad, k_grad, v_grad = (t.reshape(rows, -1).astype(bf16) for t in (q_grad, k_grad, v_grad))
    total = (
        mixed_grad[:rows]
        + dot32(q_grad, w_query.T)
        + dot32(k_grad, w_key.T)
        + dot32(v_grad, w_value.T)
    )
    return (total.astype(bf16), loss)


def solution(mesh):
    fine = Mesh(np.asarray(mesh.devices).reshape(SIZES), AXES)
    placed = (
        P(AXES, None),
        P(DP),
        P(AXES),
        P(),
        P(),
        P(),
        P(),
        P(),
        P(),
        P(AXES, None, None),
        P(AXES, None),
        P(AXES),
    )
    return jax.shard_map(
        body, mesh=fine, in_specs=placed, out_specs=(P(AXES, None), P()), check_vma=False
    )
```

```python
import jax
import jax.numpy as jnp
import numpy as np
from jax import lax
from jax.experimental import pallas as pl
from jax.experimental.pallas import tpu as pltpu
from jax.sharding import Mesh, PartitionSpec as P

D = 1024
HEADS = 8
HD = 64
E = 128
QLEN = 32
L = 512
ROWS = 128
DOCS = 128
QSET = 128
AUX = 16
TAU = 0.05
GRAD_SCALE = 1024.0
NEG = -1e30
AXES = ("z", "ylo", "x", "yhi", "core")
SIZES = (16, 2, 4, 2, 2)
DP = ("z", "ylo", "x")
LINE = 16
PLANE = 8
CHUNK = LINE * QLEN
SWAP = [(0, 1), (1, 0)]
bf16 = jnp.bfloat16
f32 = jnp.float32
i32 = jnp.int32
VMEM = pl.BlockSpec(memory_space=pltpu.VMEM)
SMEM = pl.BlockSpec(memory_space=pltpu.SMEM)
NN = (((1,), (0,)), ((), ()))
NT = (((1,), (1,)), ((), ()))
TN = (((0,), (0,)), ((), ()))


def dot(left, right, dims=NN):
    return lax.dot_general(left, right, dims, preferred_element_type=f32)


def iota(shape, dim):
    return lax.broadcasted_iota(i32, shape, dim)


def select(x, choice):
    choice = choice.astype(bf16)
    high = x.astype(bf16)
    rest = x - high.astype(f32)
    middle = rest.astype(bf16)
    low = (rest - middle.astype(f32)).astype(bf16)
    return dot(high, choice) + (dot(middle, choice) + dot(low, choice))


def call(kernel, outs, ins, scratch=(), flops=0, limit=40):
    return pl.pallas_call(
        kernel,
        out_shape=outs,
        in_specs=ins,
        out_specs=jax.tree.map(lambda _: VMEM, outs),
        scratch_shapes=list(scratch),
        compiler_params=pltpu.CompilerParams(vmem_limit_bytes=limit * 2**20),
        cost_estimate=pl.CostEstimate(flops=flops, bytes_accessed=8 * 2**20, transcendentals=0),
    )


def shape(dims, kind):
    return jax.ShapeDtypeStruct(dims, kind)


def pack_kernel(pos_ref, queries_ref, mask_ref, hidden_ref, skip_ref, query_out, own_out):
    q = queries_ref[...].astype(f32)
    qn = (q * lax.rsqrt(jnp.sum(q * q, -1, keepdims=True) + 1e-06)).astype(bf16)
    repeat = (iota((QLEN, E), 1) % QLEN == iota((QLEN, E), 0)).astype(bf16)
    weights = dot(jnp.broadcast_to(mask_ref[...], (AUX, QLEN)), repeat)
    target = pos_ref[0].astype(f32)
    row = iota((AUX, E), 0)
    aux = jnp.where(row == 0, weights, jnp.where(row == 1, target, 0.0)).astype(bf16)
    for z in range(LINE):
        query_out[z, :QLEN, :] = qn
        query_out[z, QLEN:, :] = aux
    own_out[:ROWS, :] = hidden_ref[...]
    own_out[ROWS:, :] = jnp.zeros((AUX, D), bf16)
    own_out[ROWS:, :ROWS] = jnp.broadcast_to(skip_ref[...], (AUX, ROWS)).astype(f32).astype(bf16)


def pack(positive, queries, query_mask, hidden, doc_keep):
    return call(
        pack_kernel,
        (shape((LINE, QLEN + AUX, E), bf16), shape((ROWS + AUX, D), bf16)),
        [SMEM, VMEM, VMEM, VMEM, VMEM],
    )(positive, queries[0], query_mask, hidden, doc_keep[None])


def repack_kernel(line_ref, out_ref):
    aux = line_ref[:, QLEN:, :].astype(f32)
    weights = aux[:, 0, :].astype(bf16)
    target = aux[:, 1, :].astype(bf16)
    for p in range(PLANE):
        for z in range(LINE):
            out_ref[p, z * QLEN : (z + 1) * QLEN, :] = line_ref[z, :QLEN, :]
        out_ref[p, CHUNK : CHUNK + LINE, :] = weights
        out_ref[p, CHUNK + LINE :, :] = target


def repack(line):
    return call(repack_kernel, shape((PLANE, CHUNK + 2 * LINE, E), bf16), [VMEM])(line)


def forward_kernel(
    scalar_ref,
    x0_ref,
    x1_ref,
    x2_ref,
    x3_ref,
    wq_ref,
    wk_ref,
    wv_ref,
    wo_ref,
    gain_ref,
    wp_ref,
    q_ref,
    k_ref,
    v_ref,
    att_ref,
    prow_ref,
    pcol_ref,
    unit_ref,
    inv_ref,
    proj_ref,
    embed_ref,
    keep_ref,
    x_ref,
):
    length = scalar_ref[0]
    me = scalar_ref[1]
    sources = (x0_ref, x1_ref, x2_ref, x3_ref)
    bias = []
    for b, source in enumerate(sources):
        rows = slice(b * ROWS, (b + 1) * ROWS)
        x_ref[rows, :] = source[:ROWS, :]
        start = jnp.bitwise_xor(me, b) * ROWS
        skip = source[ROWS:, :ROWS].astype(f32)[0:1, :]
        place = start + iota((1, ROWS), 1)
        valid = place < length
        bias.append(jnp.where(valid, 0.0, NEG))
        kept = jnp.where(valid & ((skip == 1.0) | (place == 0)), 1.0, 0.0)
        diagonal = iota((ROWS, ROWS), 0) == iota((ROWS, ROWS), 1)
        column = jnp.sum(jnp.where(diagonal, kept, 0.0), -1, keepdims=True)
        keep_ref[rows, :] = jnp.broadcast_to(column, (ROWS, E))
    bias = jnp.concatenate(bias, 1)
    x = x_ref[...]
    k_ref[...] = dot(x, wk_ref[...]).astype(bf16)
    q_ref[...] = dot(x, wq_ref[...]).astype(bf16)
    v_ref[...] = dot(x, wv_ref[...]).astype(bf16)
    first = iota((ROWS, 2 * HD), 1) < HD
    for pair in range(HEADS // 2):
        lanes = slice(pair * 2 * HD, (pair + 1) * 2 * HD)
        kp = k_ref[:, lanes]
        vp = v_ref[:, lanes]
        for b in range(4):
            rows = slice(b * ROWS, (b + 1) * ROWS)
            qp = q_ref[rows, lanes] * jnp.array(HD**-0.5, bf16)
            mixes = []
            for half in range(2):
                head = 2 * pair + half
                own = first if half == 0 else ~first
                scores = dot(jnp.where(own, qp, jnp.zeros_like(qp)), kp, NT) + bias
                expo = jnp.exp(scores - jnp.max(scores, -1, keepdims=True))
                probs = expo * (1.0 / jnp.sum(expo, -1, keepdims=True))
                if b == 0:
                    prow_ref[head] = probs
                pcol_ref[head, rows, :] = probs[:, :ROWS]
                mixes.append(dot(probs.astype(bf16), vp))
            att_ref[rows, lanes] = jnp.where(first, mixes[0], mixes[1]).astype(bf16)
    unit_ref[...] = dot(att_ref[...], wo_ref[...])
    for c in range(8):
        rows = slice(c * 64, (c + 1) * 64)
        mixed = x_ref[rows, :].astype(f32) + unit_ref[rows, :]
        centred = mixed - jnp.mean(mixed, -1, keepdims=True)
        inv = lax.rsqrt(jnp.mean(centred * centred, -1, keepdims=True) + 1e-05)
        unit = centred * inv
        unit_ref[rows, :] = unit
        inv_ref[rows, :] = jnp.broadcast_to(inv, (64, E))
        x_ref[rows, :] = (unit * gain_ref[...]).astype(bf16)
    proj = dot(x_ref[...], wp_ref[...])
    proj_ref[...] = proj
    scale = lax.rsqrt(jnp.sum(proj * proj, -1, keepdims=True) + 1e-06)
    embed_ref[...] = (proj * scale).astype(bf16)


def forward(scalars, blocks, w_query, w_key, w_value, w_out, ln_gain, w_proj):
    square = shape((L, HEADS * HD), bf16)
    return call(
        forward_kernel,
        (
            square,
            square,
            square,
            square,
            shape((HEADS, ROWS, L), f32),
            shape((HEADS, L, ROWS), f32),
            shape((L, D), f32),
            shape((L, E), f32),
            shape((L, E), f32),
            shape((L, E), bf16),
            shape((L, E), f32),
        ),
        [SMEM] + [VMEM] * 10,
        [pltpu.VMEM((L, D), bf16)],
        flops=4 * 10**9,
    )(scalars, *blocks, w_query, w_key, w_value, w_out, ln_gain[None], w_proj)


def sums_kernel(plane_ref, embed_ref, keep_ref, send_ref, sums_ref, weight_ref):
    for c in range(PLANE):
        total = jnp.zeros((8, CHUNK), f32)
        for b in range(4):
            rows = slice(b * ROWS, (b + 1) * ROWS)
            close = dot(embed_ref[rows, :], plane_ref[c, :CHUNK, :], NT)
            near = jnp.exp(close * (1.0 / TAU)) * keep_ref[rows, 0:1]
            total += jnp.sum(near.reshape(ROWS // 8, 8, CHUNK), 0)
        total = jnp.sum(total, 0, keepdims=True)
        for j in range(4):
            sums_ref[4 * c + j : 4 * c + j + 1, :] = total[:, j * E : (j + 1) * E]
    weights = jnp.concatenate([plane_ref[c, CHUNK : CHUNK + LINE, :] for c in range(PLANE)], 0)
    row, col = iota((QLEN, QSET), 0), iota((QLEN, QSET), 1)
    weight = jnp.zeros((QLEN, E), f32)
    for g in range(4):
        picked = dot((col == 4 * row + g).astype(bf16), weights)
        weight = jnp.where(col // QLEN == g, picked, weight)
    weight_ref[...] = weight
    parts = weight * TAU * jnp.log(sums_ref[...])
    source, place = iota((E, QSET), 0), iota((E, QSET), 1)
    table = select(parts, source // QLEN == place % 4)
    table = jnp.sum(jnp.where(col // 4 == row, table, 0.0), 0, keepdims=True)
    send_ref[...] = jnp.broadcast_to(table, (DOCS, QSET))


def sums_call(plane, embed, keep):
    return call(
        sums_kernel,
        (shape((DOCS, QSET), f32), shape((QLEN, E), f32), shape((QLEN, E), f32)),
        [VMEM] * 3,
        flops=10**9,
    )(plane, embed, keep)


def grads_kernel(mine_ref, table_ref, plane_ref, embed_ref, keep_ref, sums_ref, weight_ref, out_ref):
    mine = mine_ref[0]
    table = table_ref[...]
    lse = jnp.log(jnp.sum(jnp.exp(table), 0, keepdims=True))
    targets = jnp.concatenate(
        [plane_ref[c, CHUNK + LINE :, :] for c in range(PLANE)], 0
    ).astype(f32)
    row, col = iota((QSET, QSET), 0), iota((QSET, QSET), 1)
    target = jnp.sum(jnp.where(row == col, targets, 0.0), 0, keepdims=True).astype(i32)
    hit = row == target
    gap = lse - jnp.sum(jnp.where(hit, table, 0.0), 0, keepdims=True)
    loss = jnp.sum(gap, -1, keepdims=True)
    own = jnp.sum(jnp.where(row == mine, table, 0.0), 0, keepdims=True)
    dscore = GRAD_SCALE * (jnp.exp(own - lse) - jnp.where(target == mine, 1.0, 0.0))
    group = iota((QLEN, QSET), 1) // 4 == iota((QLEN, QSET), 0)
    wide = select(jnp.where(group, dscore, 0.0), row % 4 == col // QLEN)
    coef = wide * weight_ref[...] / sums_ref[...]
    for b in range(4):
        rows = slice(b * ROWS, (b + 1) * ROWS)
        total = jnp.zeros((ROWS, E), f32)
        for c in range(PLANE):
            queries = plane_ref[c, :CHUNK, :]
            close = dot(embed_ref[rows, :], queries, NT)
            factor = jnp.concatenate([coef[4 * c + j : 4 * c + j + 1, :] for j in range(4)], 1)
            coupling = (jnp.exp(close * (1.0 / TAU)) * factor).astype(bf16)
            total += dot(coupling, queries)
        out_ref[rows, :] = total * keep_ref[rows, :]
    out_ref[L:, :] = jnp.broadcast_to(loss, (8, E))


def grads_call(mine, table, plane, embed, keep, sums, weight):
    return call(grads_kernel, shape((L + 8, E), f32), [SMEM] + [VMEM] * 6, flops=2 * 10**9)(
        mine, table, plane, embed, keep, sums, weight
    )


def add_kernel(own_ref, got_ref, sum_ref, send_ref):
    for b in range(4):
        rows = slice(b * ROWS, (b + 1) * ROWS)
        other = (b ^ 1) * ROWS
        total = own_ref[rows, :] + got_ref[other : other + ROWS, :]
        sum_ref[rows, :] = total
        send_ref[rows, :] = total.astype(bf16)
    loss = own_ref[L:, :] + got_ref[L:, :]
    sum_ref[L:, :] = loss
    high = loss.astype(bf16).astype(f32)
    middle = (loss - high).astype(bf16).astype(f32)
    low = loss - high - middle
    send_ref[L : L + 16, :] = jnp.concatenate([high, middle], 0).astype(bf16)
    send_ref[L + 16 :, :] = jnp.concatenate([low, low], 0).astype(bf16)


def add_call(own, got):
    return call(add_kernel, (shape((L + 8, E), f32), shape((L + 32, E), bf16)), [VMEM] * 2)(own, got)


def backward_kernel(
    sum_ref,
    got_ref,
    proj_ref,
    unit_ref,
    inv_ref,
    gain_ref,
    wp_ref,
    wo_ref,
    att_ref,
    q_ref,
    k_ref,
    v_ref,
    prow_ref,
    pcol_ref,
    wq_ref,
    wk_ref,
    wv_ref,
    out_ref,
    loss_ref,
    wide_ref,
    mixed_ref,
    ag_ref,
    qg_ref,
    kg_ref,
    vg_ref,
):
    tail = got_ref[L:, :].astype(f32)
    loss_ref[...] = sum_ref[L:, :] + (tail[0:8] + tail[8:16] + tail[16:24])
    got = got_ref[:L, :].astype(f32)
    grad = sum_ref[:L, :] + jnp.concatenate([got[2 * ROWS :], got[: 2 * ROWS]], 0)
    proj = proj_ref[...]
    scale = lax.rsqrt(jnp.sum(proj * proj, -1, keepdims=True) + 1e-06)
    embed = proj * scale
    proj_grad = ((grad - embed * jnp.sum(embed * grad, -1, keepdims=True)) * scale).astype(bf16)
    wide_ref[...] = dot(proj_grad, wp_ref[...], NT)
    for c in range(8):
        rows = slice(c * 64, (c + 1) * 64)
        gained = wide_ref[rows, :] * gain_ref[...]
        unit = unit_ref[rows, :]
        along = jnp.mean(gained * unit, -1, keepdims=True)
        mixed = inv_ref[rows, 0:1] * (gained - jnp.mean(gained, -1, keepdims=True) - unit * along)
        if c < 2:
            wide_ref[rows, :] = mixed
        mixed_ref[rows, :] = mixed.astype(bf16)
    ag_ref[...] = dot(mixed_ref[...], wo_ref[...], NT).astype(bf16)
    first = iota((ROWS, 2 * HD), 1) < HD
    for pair in range(HEADS // 2):
        lanes = slice(pair * 2 * HD, (pair + 1) * 2 * HD)
        kp = k_ref[:, lanes]
        vp = v_ref[:, lanes]
        grads = [[], [], []]
        for half in range(2):
            head = 2 * pair + half
            own = first if half == 0 else ~first
            kg = jnp.zeros((ROWS, 2 * HD), f32)
            vg = jnp.zeros((ROWS, 2 * HD), f32)
            for b in range(4):
                rows = slice(b * ROWS, (b + 1) * ROWS)
                agp = ag_ref[rows, lanes]
                part = jnp.where(own, agp, jnp.zeros_like(agp))
                delta = jnp.sum(
                    part.astype(f32) * att_ref[rows, lanes].astype(f32), -1, keepdims=True
                )
                if b == 0:
                    inner = dot(part, vp, NT)
                    score = (prow_ref[head] * ((inner - delta) * HD**-0.5)).astype(bf16)
                    grads[0].append(dot(score, kp))
                    inner = inner[:, :ROWS]
                    score = score[:, :ROWS]
                else:
                    inner = dot(part, vp[:ROWS], NT)
                    score = (pcol_ref[head, rows, :] * ((inner - delta) * HD**-0.5)).astype(bf16)
                kg += dot(score, q_ref[rows, lanes], TN)
                vg += dot(pcol_ref[head, rows, :].astype(bf16), agp, TN)
            grads[1].append(kg)
            grads[2].append(vg)
        for ref, (even, odd) in zip((qg_ref, kg_ref, vg_ref), grads):
            ref[:, lanes] = jnp.where(first, even, odd).astype(bf16)
    total = wide_ref[:ROWS, :]
    total += dot(qg_ref[...], wq_ref[...], NT)
    total += dot(kg_ref[...], wk_ref[...], NT)
    total += dot(vg_ref[...], wv_ref[...], NT)
    out_ref[...] = total.astype(bf16)


def backward(summed, got, kept, ln_gain, w_proj, w_out, w_query, w_key, w_value):
    q, k, v, att, prow, pcol, unit, inv, proj = kept
    width = HEADS * HD
    return call(
        backward_kernel,
        (shape((ROWS, D), bf16), shape((8, E), f32)),
        [VMEM] * 17,
        [
            pltpu.VMEM((L, D), f32),
            pltpu.VMEM((L, D), bf16),
            pltpu.VMEM((L, width), bf16),
            pltpu.VMEM((ROWS, width), bf16),
            pltpu.VMEM((ROWS, width), bf16),
            pltpu.VMEM((ROWS, width), bf16),
        ],
        flops=3 * 10**9,
    )(
        summed, got, proj, unit, inv, ln_gain[None], w_proj, w_out, att, q, k, v, prow, pcol,
        w_query, w_key, w_value,
    )


def spread(x, axes):
    return lax.all_to_all(x, axes, 0, 0)


def body(
    hidden,
    doc_len,
    doc_keep,
    w_query,
    w_key,
    w_value,
    w_out,
    ln_gain,
    w_proj,
    queries,
    query_mask,
    positive,
):
    me = lax.axis_index("yhi") * 2 + lax.axis_index("core")
    mine = lax.axis_index(DP)
    query_send, own = pack(positive, queries, query_mask, hidden, doc_keep)
    by_core = lax.ppermute(own, "core", SWAP)
    by_yhi = lax.ppermute(own, "yhi", SWAP)
    line = spread(query_send, "z")
    by_both = lax.ppermute(by_yhi, "core", SWAP)
    plane = spread(repack(line), ("ylo", "x"))
    scalars = jnp.stack([doc_len[0], me])
    *kept, embed, keep = forward(
        scalars, (own, by_core, by_yhi, by_both), w_query, w_key, w_value, w_out, ln_gain, w_proj
    )
    send, sums, weight = sums_call(plane, embed, keep)
    table = spread(send, DP)
    partial = grads_call(mine[None], table, plane, embed, keep, sums, weight)
    summed, half = add_call(partial, lax.ppermute(partial, "core", SWAP))
    got = lax.ppermute(half, "yhi", SWAP)
    out, loss = backward(summed, got, kept, ln_gain, w_proj, w_out, w_query, w_key, w_value)
    return (out, loss[0, 0])


def solution(mesh):
    fine = Mesh(np.asarray(mesh.devices).reshape(SIZES), AXES)
    placed = (
        P(AXES, None),
        P(DP),
        P(AXES),
        P(),
        P(),
        P(),
        P(),
        P(),
        P(),
        P(AXES, None, None),
        P(AXES, None),
        P(AXES),
    )
    return jax.shard_map(
        body, mesh=fine, in_specs=placed, out_specs=(P(AXES, None), P()), check_vma=False
    )
```

```python
import jax
import jax.numpy as jnp
import numpy as np
from jax import lax
from jax.experimental import pallas as pl
from jax.experimental.pallas import tpu as pltpu
from jax.sharding import Mesh, PartitionSpec as P

D = 1024
HEADS = 8
HD = 64
E = 128
QLEN = 32
L = 512
ROWS = 128
DOCS = 128
QSET = 128
AUX = 16
TAU = 0.05
GRAD_SCALE = 1024.0
NEG = -1e30
AXES = ("z", "ylo", "x", "yhi", "core")
SIZES = (16, 2, 4, 2, 2)
DP = ("z", "ylo", "x")
LINE = 16
PLANE = 8
CHUNK = LINE * QLEN
STRIP = 64
SWAP = [(0, 1), (1, 0)]
bf16 = jnp.bfloat16
f32 = jnp.float32
i32 = jnp.int32
BLOCK = pl.BlockSpec()
ANY = pl.BlockSpec(memory_space=pl.ANY)
SMEM = pl.BlockSpec(memory_space=pltpu.SMEM)
NN = (((1,), (0,)), ((), ()))
NT = (((1,), (1,)), ((), ()))
TN = (((0,), (0,)), ((), ()))


def dot(left, right, dims=NN):
    return lax.dot_general(left, right, dims, preferred_element_type=f32)


def iota(shape, dim):
    return lax.broadcasted_iota(i32, shape, dim)


def select(x, choice):
    choice = choice.astype(bf16)
    high = x.astype(bf16)
    rest = x - high.astype(f32)
    middle = rest.astype(bf16)
    low = (rest - middle.astype(f32)).astype(bf16)
    return dot(high, choice) + (dot(middle, choice) + dot(low, choice))


def position():
    return lax.axis_index("yhi") * 2 + lax.axis_index("core"), lax.axis_index(DP)


def call(kernel, outs, ins, out_specs=None, scratch=(), flops=0):
    return pl.pallas_call(
        kernel,
        out_shape=outs,
        in_specs=ins,
        out_specs=jax.tree.map(lambda _: BLOCK, outs) if out_specs is None else out_specs,
        scratch_shapes=list(scratch),
        compiler_params=pltpu.CompilerParams(vmem_limit_bytes=56 * 2**20),
        cost_estimate=pl.CostEstimate(flops=flops, bytes_accessed=4 * 2**20, transcendentals=0),
    )


class Moves:
    def __init__(self, sems):
        self.sems, self.used = sems, 0

    def start(self, source, target):
        copy = pltpu.make_async_copy(source, target, self.sems.at[self.used])
        self.used += 1
        copy.start()
        return copy


def shape(dims, kind):
    return jax.ShapeDtypeStruct(dims, kind)


def pack_kernel(pos_ref, queries_ref, mask_ref, hidden_ref, skip_ref, query_out, own_out):
    q = queries_ref[...].astype(f32)
    qn = (q * lax.rsqrt(jnp.sum(q * q, -1, keepdims=True) + 1e-06)).astype(bf16)
    repeat = (iota((QLEN, E), 1) % QLEN == iota((QLEN, E), 0)).astype(bf16)
    weights = dot(jnp.broadcast_to(mask_ref[...], (AUX, QLEN)), repeat)
    target = pos_ref[0].astype(f32)
    row = iota((AUX, E), 0)
    aux = jnp.where(row == 0, weights, jnp.where(row == 1, target, 0.0)).astype(bf16)
    for z in range(LINE):
        query_out[z, :QLEN, :] = qn
        query_out[z, QLEN:, :] = aux
    own_out[:ROWS, :] = hidden_ref[...]
    own_out[ROWS:, :] = jnp.zeros((AUX, D), bf16)
    own_out[ROWS:, :ROWS] = jnp.broadcast_to(skip_ref[...], (AUX, ROWS)).astype(f32).astype(bf16)


def pack(positive, queries, query_mask, hidden, doc_keep):
    return call(
        pack_kernel,
        (shape((LINE, QLEN + AUX, E), bf16), shape((ROWS + AUX, D), bf16)),
        [SMEM] + [BLOCK] * 4,
    )(positive, queries[0], query_mask, hidden, doc_keep[None])


def repack_kernel(line_ref, after_ref, out_ref):
    aux = line_ref[:, QLEN:, :].astype(f32)
    weights = aux[:, 0, :].astype(bf16)
    target = aux[:, 1, :].astype(bf16)
    for p in range(PLANE):
        for z in range(LINE):
            out_ref[p, z * QLEN : (z + 1) * QLEN, :] = line_ref[z, :QLEN, :]
        out_ref[p, CHUNK : CHUNK + LINE, :] = weights
        out_ref[p, CHUNK + LINE :, :] = target


def repack(line, after):
    out = shape((PLANE, CHUNK + 2 * LINE, E), bf16)
    return call(repack_kernel, out, [BLOCK, ANY])(line, after)


def forward_kernel(
    length_ref,
    x0_any,
    x1_any,
    x2_any,
    x3_any,
    wq_any,
    wk_any,
    wv_any,
    wo_any,
    gain_any,
    wp_any,
    q_any,
    k_any,
    v_any,
    att_any,
    prow_any,
    pcol_any,
    unit_any,
    inv_any,
    proj_any,
    embed_any,
    keep_any,
    x_ref,
    skip_ref,
    wq_ref,
    wk_ref,
    wv_ref,
    wo_ref,
    gain_ref,
    wp_ref,
    q_ref,
    k_ref,
    v_ref,
    att_ref,
    prow_ref,
    pcol_ref,
    unit_ref,
    inv_ref,
    proj_ref,
    embed_ref,
    keep_ref,
    score_ref,
    prob_ref,
    sems,
):
    moves = Moves(sems)
    blocks = [
        moves.start(source.at[pl.ds(0, ROWS)], x_ref.at[pl.ds(b * ROWS, ROWS)])
        for b, source in enumerate((x0_any, x1_any, x2_any, x3_any))
    ]
    at_k = moves.start(wk_any, wk_ref)
    skips = [
        moves.start(source.at[pl.ds(ROWS, AUX), pl.ds(0, ROWS)], skip_ref.at[b])
        for b, source in enumerate((x0_any, x1_any, x2_any, x3_any))
    ]
    at_q = moves.start(wq_any, wq_ref)
    at_v = moves.start(wv_any, wv_ref)
    at_o = moves.start(wo_any, wo_ref)
    at_gain = moves.start(gain_any, gain_ref)
    at_p = moves.start(wp_any, wp_ref)
    ends = []
    length = length_ref[0]
    me, _ = position()
    for copy in blocks:
        copy.wait()
    at_k.wait()
    k_ref[...] = dot(x_ref[...], wk_ref[...]).astype(bf16)
    ends.append(moves.start(k_ref, k_any))
    at_q.wait()
    q_ref[...] = dot(x_ref[...], wq_ref[...]).astype(bf16)
    ends.append(moves.start(q_ref, q_any))
    at_v.wait()
    v_ref[...] = dot(x_ref[...], wv_ref[...]).astype(bf16)
    ends.append(moves.start(v_ref, v_any))
    bias = []
    for b in range(4):
        skips[b].wait()
        start = jnp.bitwise_xor(me, b) * ROWS
        skip = skip_ref[b].astype(f32)[0:1, :]
        place = start + iota((1, ROWS), 1)
        valid = place < length
        bias.append(jnp.where(valid, 0.0, NEG))
        kept = jnp.where(valid & ((skip == 1.0) | (place == 0)), 1.0, 0.0)
        diagonal = iota((ROWS, ROWS), 0) == iota((ROWS, ROWS), 1)
        column = jnp.sum(jnp.where(diagonal, kept, 0.0), -1, keepdims=True)
        keep_ref[b * ROWS : (b + 1) * ROWS, :] = jnp.broadcast_to(column, (ROWS, E))
    ends.append(moves.start(keep_ref, keep_any))
    bias = jnp.concatenate(bias, 1)
    first = iota((L, 2 * HD), 1) < HD
    for pair in range(HEADS // 2):
        lanes = slice(pair * 2 * HD, (pair + 1) * 2 * HD)
        qp = q_ref[:, lanes] * jnp.array(HD**-0.5, bf16)
        mixes = []
        for half in range(2):
            head = 2 * pair + half
            own = first if half == 0 else ~first
            score_ref[half] = dot(jnp.where(own, qp, jnp.zeros_like(qp)), k_ref[:, lanes], NT)
            for c in range(L // STRIP):
                rows = slice(c * STRIP, (c + 1) * STRIP)
                scores = score_ref[half, rows, :] + bias
                expo = jnp.exp(scores - jnp.max(scores, -1, keepdims=True))
                probs = expo * (1.0 / jnp.sum(expo, -1, keepdims=True))
                if (c + 1) * STRIP <= ROWS:
                    prow_ref[head, rows, :] = probs
                pcol_ref[head, rows, :] = probs[:, :ROWS]
                prob_ref[half, rows, :] = probs.astype(bf16)
            mixes.append(dot(prob_ref[half], v_ref[:, lanes]))
        att_ref[:, lanes] = jnp.where(first, mixes[0], mixes[1]).astype(bf16)
        two = pl.ds(2 * pair, 2)
        ends.append(moves.start(prow_ref.at[two], prow_any.at[two]))
        ends.append(moves.start(pcol_ref.at[two], pcol_any.at[two]))
    ends.append(moves.start(att_ref, att_any))
    at_o.wait()
    unit_ref[...] = dot(att_ref[...], wo_ref[...])
    at_gain.wait()
    for c in range(L // STRIP):
        rows = slice(c * STRIP, (c + 1) * STRIP)
        mixed = x_ref[rows, :].astype(f32) + unit_ref[rows, :]
        centred = mixed - jnp.mean(mixed, -1, keepdims=True)
        inv = lax.rsqrt(jnp.mean(centred * centred, -1, keepdims=True) + 1e-05)
        unit = centred * inv
        unit_ref[rows, :] = unit
        inv_ref[rows, :] = jnp.broadcast_to(inv, (STRIP, E))
        x_ref[rows, :] = (unit * gain_ref[...]).astype(bf16)
    ends.append(moves.start(unit_ref, unit_any))
    ends.append(moves.start(inv_ref, inv_any))
    at_p.wait()
    proj = dot(x_ref[...], wp_ref[...])
    proj_ref[...] = proj
    ends.append(moves.start(proj_ref, proj_any))
    scale = lax.rsqrt(jnp.sum(proj * proj, -1, keepdims=True) + 1e-06)
    embed_ref[...] = (proj * scale).astype(bf16)
    ends.append(moves.start(embed_ref, embed_any))
    for copy in ends:
        copy.wait()


def forward(doc_len, blocks, w_query, w_key, w_value, w_out, ln_gain, w_proj):
    width = HEADS * HD
    square = shape((L, width), bf16)
    outs = (
        square,
        square,
        square,
        square,
        shape((HEADS, ROWS, L), f32),
        shape((HEADS, L, ROWS), f32),
        shape((L, D), f32),
        shape((L, E), f32),
        shape((L, E), f32),
        shape((L, E), bf16),
        shape((L, E), f32),
    )
    ins = [
        pltpu.VMEM((L, D), bf16),
        pltpu.VMEM((4, AUX, ROWS), bf16),
        pltpu.VMEM((D, width), bf16),
        pltpu.VMEM((D, width), bf16),
        pltpu.VMEM((D, width), bf16),
        pltpu.VMEM((width, D), bf16),
        pltpu.VMEM((1, D), f32),
        pltpu.VMEM((D, E), bf16),
    ]
    work = [
        pltpu.VMEM((2, L, L), f32),
        pltpu.VMEM((2, L, L), bf16),
        pltpu.SemaphoreType.DMA((32,)),
    ]
    return call(
        forward_kernel,
        outs,
        [SMEM] + [ANY] * 10,
        tuple(ANY for _ in outs),
        ins + [pltpu.VMEM(o.shape, o.dtype) for o in outs] + work,
        flops=4 * 10**9,
    )(doc_len, *blocks, w_query, w_key, w_value, w_out, ln_gain[None], w_proj)


def sums_kernel(plane_ref, embed_ref, keep_ref, send_ref, sums_ref, weight_ref):
    for c in range(PLANE):
        total = jnp.zeros((8, CHUNK), f32)
        for b in range(4):
            rows = slice(b * ROWS, (b + 1) * ROWS)
            close = dot(embed_ref[rows, :], plane_ref[c, :CHUNK, :], NT)
            near = jnp.exp(close * (1.0 / TAU)) * keep_ref[rows, 0:1]
            total += jnp.sum(near.reshape(ROWS // 8, 8, CHUNK), 0)
        total = jnp.sum(total, 0, keepdims=True)
        for j in range(4):
            sums_ref[4 * c + j : 4 * c + j + 1, :] = total[:, j * E : (j + 1) * E]
    weights = jnp.concatenate([plane_ref[c, CHUNK : CHUNK + LINE, :] for c in range(PLANE)], 0)
    row, col = iota((QLEN, QSET), 0), iota((QLEN, QSET), 1)
    weight = jnp.zeros((QLEN, E), f32)
    for g in range(4):
        picked = dot((col == 4 * row + g).astype(bf16), weights)
        weight = jnp.where(col // QLEN == g, picked, weight)
    weight_ref[...] = weight
    parts = weight * TAU * jnp.log(sums_ref[...])
    source, place = iota((E, QSET), 0), iota((E, QSET), 1)
    table = select(parts, source // QLEN == place % 4)
    table = jnp.sum(jnp.where(col // 4 == row, table, 0.0), 0, keepdims=True)
    send_ref[...] = jnp.broadcast_to(table, (DOCS, QSET))


def sums_call(plane, embed, keep):
    return call(
        sums_kernel,
        (shape((DOCS, QSET), f32), shape((QLEN, E), f32), shape((QLEN, E), f32)),
        [BLOCK] * 3,
        flops=10**9,
    )(plane, embed, keep)


def grads_kernel(table_ref, plane_ref, embed_ref, keep_ref, sums_ref, weight_ref, out_ref):
    _, mine = position()
    table = table_ref[...]
    lse = jnp.log(jnp.sum(jnp.exp(table), 0, keepdims=True))
    targets = jnp.concatenate(
        [plane_ref[c, CHUNK + LINE :, :] for c in range(PLANE)], 0
    ).astype(f32)
    row, col = iota((QSET, QSET), 0), iota((QSET, QSET), 1)
    target = jnp.sum(jnp.where(row == col, targets, 0.0), 0, keepdims=True).astype(i32)
    hit = row == target
    gap = lse - jnp.sum(jnp.where(hit, table, 0.0), 0, keepdims=True)
    loss = jnp.sum(gap, -1, keepdims=True)
    own = jnp.sum(jnp.where(row == mine, table, 0.0), 0, keepdims=True)
    dscore = GRAD_SCALE * (jnp.exp(own - lse) - jnp.where(target == mine, 1.0, 0.0))
    group = iota((QLEN, QSET), 1) // 4 == iota((QLEN, QSET), 0)
    wide = select(jnp.where(group, dscore, 0.0), row % 4 == col // QLEN)
    coef = wide * weight_ref[...] / sums_ref[...]
    for b in range(4):
        rows = slice(b * ROWS, (b + 1) * ROWS)
        total = jnp.zeros((ROWS, E), f32)
        for c in range(PLANE):
            queries = plane_ref[c, :CHUNK, :]
            close = dot(embed_ref[rows, :], queries, NT)
            factor = jnp.concatenate([coef[4 * c + j : 4 * c + j + 1, :] for j in range(4)], 1)
            coupling = (jnp.exp(close * (1.0 / TAU)) * factor).astype(bf16)
            total += dot(coupling, queries)
        out_ref[rows, :] = total * keep_ref[rows, :]
    out_ref[L:, :] = jnp.broadcast_to(loss, (8, E))


def grads_call(table, plane, embed, keep, sums, weight):
    return call(grads_kernel, shape((L + 8, E), f32), [BLOCK] * 6, flops=2 * 10**9)(
        table, plane, embed, keep, sums, weight
    )


def add_kernel(own_ref, got_ref, sum_ref, send_ref):
    for b in range(4):
        rows = slice(b * ROWS, (b + 1) * ROWS)
        other = (b ^ 1) * ROWS
        total = own_ref[rows, :] + got_ref[other : other + ROWS, :]
        sum_ref[rows, :] = total
        send_ref[rows, :] = total.astype(bf16)
    loss = own_ref[L:, :] + got_ref[L:, :]
    sum_ref[L:, :] = loss
    high = loss.astype(bf16).astype(f32)
    middle = (loss - high).astype(bf16).astype(f32)
    low = loss - high - middle
    send_ref[L : L + 16, :] = jnp.concatenate([high, middle], 0).astype(bf16)
    send_ref[L + 16 :, :] = jnp.concatenate([low, low], 0).astype(bf16)


def add_call(own, got):
    return call(add_kernel, (shape((L + 8, E), f32), shape((L + 32, E), bf16)), [BLOCK] * 2)(own, got)


def backward_kernel(
    sum_ref,
    got_ref,
    proj_ref,
    wp_ref,
    inv_ref,
    gain_ref,
    unit_any,
    wo_any,
    att_any,
    v_any,
    k_any,
    q_any,
    prow_any,
    pcol_any,
    wq_any,
    wk_any,
    wv_any,
    out_ref,
    loss_ref,
    unit_ref,
    wo_ref,
    att_ref,
    v_ref,
    k_ref,
    q_ref,
    prow_ref,
    pcol_ref,
    wq_ref,
    wk_ref,
    wv_ref,
    wide_ref,
    mixed_ref,
    ag_ref,
    qg_ref,
    kg_ref,
    vg_ref,
    sems,
):
    moves = Moves(sems)
    at_unit = moves.start(unit_any, unit_ref)
    at_out = moves.start(wo_any, wo_ref)
    at_att = [
        moves.start(source, target)
        for source, target in (
            (att_any, att_ref),
            (v_any, v_ref),
            (k_any, k_ref),
            (q_any, q_ref),
            (prow_any, prow_ref),
            (pcol_any, pcol_ref),
        )
    ]
    at_weights = [
        moves.start(source, target)
        for source, target in ((wq_any, wq_ref), (wk_any, wk_ref), (wv_any, wv_ref))
    ]
    tail = got_ref[L:, :].astype(f32)
    loss_ref[...] = sum_ref[L:, :] + (tail[0:8] + tail[8:16] + tail[16:24])
    got = got_ref[:L, :].astype(f32)
    grad = sum_ref[:L, :] + jnp.concatenate([got[2 * ROWS :], got[: 2 * ROWS]], 0)
    proj = proj_ref[...]
    scale = lax.rsqrt(jnp.sum(proj * proj, -1, keepdims=True) + 1e-06)
    embed = proj * scale
    proj_grad = ((grad - embed * jnp.sum(embed * grad, -1, keepdims=True)) * scale).astype(bf16)
    wide_ref[...] = dot(proj_grad, wp_ref[...], NT)
    at_unit.wait()
    for c in range(8):
        rows = slice(c * 64, (c + 1) * 64)
        gained = wide_ref[rows, :] * gain_ref[...]
        unit = unit_ref[rows, :]
        along = jnp.mean(gained * unit, -1, keepdims=True)
        mixed = inv_ref[rows, 0:1] * (gained - jnp.mean(gained, -1, keepdims=True) - unit * along)
        if c < 2:
            wide_ref[rows, :] = mixed
        mixed_ref[rows, :] = mixed.astype(bf16)
    at_out.wait()
    ag_ref[...] = dot(mixed_ref[...], wo_ref[...], NT).astype(bf16)
    for copy in at_att:
        copy.wait()
    first = iota((ROWS, 2 * HD), 1) < HD
    for pair in range(HEADS // 2):
        lanes = slice(pair * 2 * HD, (pair + 1) * 2 * HD)
        kp = k_ref[:, lanes]
        vp = v_ref[:, lanes]
        grads = [[], [], []]
        for half in range(2):
            head = 2 * pair + half
            own = first if half == 0 else ~first
            kg = jnp.zeros((ROWS, 2 * HD), f32)
            vg = jnp.zeros((ROWS, 2 * HD), f32)
            for b in range(4):
                rows = slice(b * ROWS, (b + 1) * ROWS)
                agp = ag_ref[rows, lanes]
                part = jnp.where(own, agp, jnp.zeros_like(agp))
                delta = jnp.sum(
                    part.astype(f32) * att_ref[rows, lanes].astype(f32), -1, keepdims=True
                )
                if b == 0:
                    inner = dot(part, vp, NT)
                    score = (prow_ref[head] * ((inner - delta) * HD**-0.5)).astype(bf16)
                    grads[0].append(dot(score, kp))
                    inner = inner[:, :ROWS]
                    score = score[:, :ROWS]
                else:
                    inner = dot(part, vp[:ROWS], NT)
                    score = (pcol_ref[head, rows, :] * ((inner - delta) * HD**-0.5)).astype(bf16)
                kg += dot(score, q_ref[rows, lanes], TN)
                vg += dot(pcol_ref[head, rows, :].astype(bf16), agp, TN)
            grads[1].append(kg)
            grads[2].append(vg)
        for ref, (even, odd) in zip((qg_ref, kg_ref, vg_ref), grads):
            ref[:, lanes] = jnp.where(first, even, odd).astype(bf16)
    for copy in at_weights:
        copy.wait()
    total = wide_ref[:ROWS, :]
    total += dot(qg_ref[...], wq_ref[...], NT)
    total += dot(kg_ref[...], wk_ref[...], NT)
    total += dot(vg_ref[...], wv_ref[...], NT)
    out_ref[...] = total.astype(bf16)


def backward(summed, got, kept, ln_gain, w_proj, w_out, w_query, w_key, w_value):
    q, k, v, att, prow, pcol, unit, inv, proj = kept
    width = HEADS * HD
    moved = (unit, w_out, att, v, k, q, prow, pcol, w_query, w_key, w_value)
    return call(
        backward_kernel,
        (shape((ROWS, D), bf16), shape((8, E), f32)),
        [BLOCK] * 6 + [ANY] * len(moved),
        scratch=[pltpu.VMEM(m.shape, m.dtype) for m in moved]
        + [
            pltpu.VMEM((L, D), f32),
            pltpu.VMEM((L, D), bf16),
            pltpu.VMEM((L, width), bf16),
            pltpu.VMEM((ROWS, width), bf16),
            pltpu.VMEM((ROWS, width), bf16),
            pltpu.VMEM((ROWS, width), bf16),
            pltpu.SemaphoreType.DMA((len(moved),)),
        ],
        flops=3 * 10**9,
    )(summed, got, proj, w_proj, inv, ln_gain[None], *moved)


def spread(x, axes):
    return lax.all_to_all(x, axes, 0, 0)


def body(
    hidden,
    doc_len,
    doc_keep,
    w_query,
    w_key,
    w_value,
    w_out,
    ln_gain,
    w_proj,
    queries,
    query_mask,
    positive,
):
    query_send, own = pack(positive, queries, query_mask, hidden, doc_keep)
    by_core = lax.ppermute(own, "core", SWAP)
    by_yhi = lax.ppermute(own, "yhi", SWAP)
    line = spread(query_send, "z")
    by_both = lax.ppermute(by_yhi, "core", SWAP)
    plane = spread(repack(line, by_both), ("ylo", "x"))
    *kept, embed, keep = forward(
        doc_len, (own, by_core, by_yhi, by_both), w_query, w_key, w_value, w_out, ln_gain, w_proj
    )
    send, sums, weight = sums_call(plane, embed, keep)
    table = spread(send, DP)
    partial = grads_call(table, plane, embed, keep, sums, weight)
    summed, half = add_call(partial, lax.ppermute(partial, "core", SWAP))
    got = lax.ppermute(half, "yhi", SWAP)
    out, loss = backward(summed, got, kept, ln_gain, w_proj, w_out, w_query, w_key, w_value)
    return (out, loss[0, 0])


def solution(mesh):
    fine = Mesh(np.asarray(mesh.devices).reshape(SIZES), AXES)
    placed = (
        P(AXES, None),
        P(DP),
        P(AXES),
        P(),
        P(),
        P(),
        P(),
        P(),
        P(),
        P(AXES, None, None),
        P(AXES, None),
        P(AXES),
    )
    return jax.shard_map(
        body, mesh=fine, in_specs=placed, out_specs=(P(AXES, None), P()), check_vma=False
    )
```

```python
import jax
import jax.numpy as jnp
import numpy as np
from jax import lax
from jax.experimental import pallas as pl
from jax.experimental.pallas import tpu as pltpu
from jax.sharding import Mesh, PartitionSpec as P

D = 1024
HEADS = 8
HD = 64
E = 128
QLEN = 32
L = 512
ROWS = 128
DOCS = 128
QSET = 128
AUX = 16
TAU = 0.05
GRAD_SCALE = 1024.0
NEG = -1e30
AXES = ("z", "ylo", "x", "yhi", "core")
SIZES = (16, 2, 4, 2, 2)
DP = ("z", "ylo", "x")
LINE = 16
PLANE = 8
CHUNK = LINE * QLEN
STRIP = 64
THIN = 32
MARKS_FLOPS = 3 * 10**9
LOG2E = 1.4426950408889634
SWAP = [(0, 1), (1, 0)]
bf16 = jnp.bfloat16
f32 = jnp.float32
i32 = jnp.int32
BLOCK = pl.BlockSpec()
VMEM = pl.BlockSpec(memory_space=pltpu.VMEM)
ANY = pl.BlockSpec(memory_space=pl.ANY)
HBM = pl.BlockSpec(memory_space=pltpu.MemorySpace.HBM)
SMEM = pl.BlockSpec(memory_space=pltpu.SMEM)
NN = (((1,), (0,)), ((), ()))
NT = (((1,), (1,)), ((), ()))
TN = (((0,), (0,)), ((), ()))


def dot(left, right, dims=NN):
    return lax.dot_general(left, right, dims, preferred_element_type=f32)


def iota(shape, dim):
    return lax.broadcasted_iota(i32, shape, dim)


def select(x, choice):
    choice = choice.astype(bf16)
    high = x.astype(bf16)
    rest = x - high.astype(f32)
    middle = rest.astype(bf16)
    low = (rest - middle.astype(f32)).astype(bf16)
    return dot(high, choice) + (dot(middle, choice) + dot(low, choice))


def position():
    return lax.axis_index("yhi") * 2 + lax.axis_index("core"), lax.axis_index(DP)


def call(kernel, outs, ins, out_specs=None, scratch=(), flops=0, limit=12):
    return pl.pallas_call(
        kernel,
        out_shape=outs,
        in_specs=ins,
        out_specs=jax.tree.map(lambda _: BLOCK, outs) if out_specs is None else out_specs,
        scratch_shapes=list(scratch),
        compiler_params=pltpu.CompilerParams(vmem_limit_bytes=limit * 2**20),
        cost_estimate=pl.CostEstimate(flops=flops, bytes_accessed=4 * 2**20, transcendentals=0),
    )


class Moves:
    def __init__(self, sems):
        self.sems, self.used = sems, 0

    def start(self, source, target):
        copy = pltpu.make_async_copy(source, target, self.sems.at[self.used])
        self.used += 1
        copy.start()
        return copy


def shape(dims, kind):
    return jax.ShapeDtypeStruct(dims, kind)


def pack_hidden_kernel(hidden_ref, skip_ref, own_out):
    own_out[:ROWS, :] = hidden_ref[...]
    own_out[ROWS:, :] = jnp.zeros((AUX, D), bf16)
    own_out[ROWS:, :ROWS] = jnp.broadcast_to(skip_ref[...], (AUX, ROWS)).astype(f32).astype(bf16)


def pack_hidden(hidden, doc_keep):
    return call(pack_hidden_kernel, shape((ROWS + AUX, D), bf16), [BLOCK] * 2, limit=56)(
        hidden, doc_keep[None]
    )


def pack_query_kernel(pos_ref, queries_ref, mask_ref, after_ref, query_out):
    q = queries_ref[...].astype(f32)
    qn = (q * lax.rsqrt(jnp.sum(q * q, -1, keepdims=True) + 1e-06)).astype(bf16)
    repeat = (iota((QLEN, E), 1) % QLEN == iota((QLEN, E), 0)).astype(bf16)
    weights = dot(jnp.broadcast_to(mask_ref[...], (AUX, QLEN)), repeat)
    target = pos_ref[0].astype(f32)
    row = iota((AUX, E), 0)
    aux = jnp.where(row == 0, weights, jnp.where(row == 1, target, 0.0)).astype(bf16)
    for z in range(LINE):
        query_out[z, :QLEN, :] = qn
        query_out[z, QLEN:, :] = aux


def pack_query(positive, queries, query_mask, after):
    return call(
        pack_query_kernel,
        shape((LINE, QLEN + AUX, E), bf16),
        [SMEM, BLOCK, BLOCK, ANY],
        limit=56,
    )(positive, queries[0], query_mask, after)


def repack_kernel(line_ref, after_ref, out_ref):
    aux = line_ref[:, QLEN:, :].astype(f32)
    weights = aux[:, 0, :].astype(bf16)
    target = aux[:, 1, :].astype(bf16)
    for p in range(PLANE):
        for z in range(LINE):
            out_ref[p, z * QLEN : (z + 1) * QLEN, :] = line_ref[z, :QLEN, :]
        out_ref[p, CHUNK : CHUNK + LINE, :] = weights
        out_ref[p, CHUNK + LINE :, :] = target


def repack(line, after):
    out = shape((PLANE, CHUNK + 2 * LINE, E), bf16)
    return call(repack_kernel, out, [BLOCK, ANY])(line, after)


def marks_kernel(length_ref, x0_any, x1_any, x2_any, x3_any, keep_ref, bias_ref, skip_ref, sems):
    moves = Moves(sems)
    skips = [
        moves.start(source.at[pl.ds(ROWS, AUX), pl.ds(0, ROWS)], skip_ref.at[b])
        for b, source in enumerate((x0_any, x1_any, x2_any, x3_any))
    ]
    length = length_ref[0]
    me, _ = position()
    for b in range(4):
        skips[b].wait()
        start = jnp.bitwise_xor(me, b) * ROWS
        skip = skip_ref[b].astype(f32)[0:1, :]
        place = start + iota((1, ROWS), 1)
        valid = place < length
        bias = jnp.where(valid, 0.0, NEG)
        bias_ref[:, b * ROWS : (b + 1) * ROWS] = jnp.broadcast_to(bias, (8, ROWS))
        kept = jnp.where(valid & ((skip == 1.0) | (place == 0)), 1.0, 0.0)
        diagonal = iota((ROWS, ROWS), 0) == iota((ROWS, ROWS), 1)
        column = jnp.sum(jnp.where(diagonal, kept, 0.0), -1, keepdims=True)
        keep_ref[b * ROWS : (b + 1) * ROWS, :] = jnp.broadcast_to(column, (ROWS, E)).astype(bf16)


def marks_call(doc_len, blocks):
    return call(
        marks_kernel,
        (shape((L, E), bf16), shape((8, L), f32)),
        [SMEM] + [ANY] * 4,
        scratch=[pltpu.VMEM((4, AUX, ROWS), bf16), pltpu.SemaphoreType.DMA((4,))],
        flops=MARKS_FLOPS,
        limit=4,
    )(doc_len, *blocks)


def forward_kernel(
    keep_any,
    bias_any,
    x0_any,
    x1_any,
    x2_any,
    x3_any,
    wq_any,
    wk_any,
    wv_any,
    wo_any,
    gain_any,
    wp_any,
    q_any,
    k_any,
    v_any,
    att_any,
    prow_any,
    pcol_any,
    unit_any,
    inv_any,
    proj_any,
    embed_any,
    x_ref,
    bias_ref,
    wq_ref,
    wk_ref,
    wv_ref,
    wo_ref,
    gain_ref,
    wp_ref,
    q_ref,
    k_ref,
    v_ref,
    att_ref,
    prow_ref,
    pcol_ref,
    unit_ref,
    inv_ref,
    proj_ref,
    embed_ref,
    score_ref,
    prob_ref,
    sems,
):
    moves = Moves(sems)
    blocks = [
        moves.start(source.at[pl.ds(0, ROWS)], x_ref.at[pl.ds(b * ROWS, ROWS)])
        for b, source in enumerate((x0_any, x1_any, x2_any, x3_any))
    ]
    at_k = moves.start(wk_any, wk_ref)
    at_keep = moves.start(keep_any, embed_ref.at[pl.ds(L, L)])
    at_bias = moves.start(bias_any, bias_ref)
    at_q = moves.start(wq_any, wq_ref)
    at_v = moves.start(wv_any, wv_ref)
    at_o = moves.start(wo_any, wo_ref)
    at_gain = moves.start(gain_any, gain_ref)
    at_p = moves.start(wp_any, wp_ref)
    ends = []
    for copy in blocks:
        copy.wait()
    at_k.wait()
    k_ref[...] = dot(x_ref[...], wk_ref[...]).astype(bf16)
    ends.append(moves.start(k_ref, k_any))
    at_q.wait()
    q_ref[...] = dot(x_ref[...], wq_ref[...]).astype(bf16)
    ends.append(moves.start(q_ref, q_any))
    at_v.wait()
    v_ref[...] = dot(x_ref[...], wv_ref[...]).astype(bf16)
    ends.append(moves.start(v_ref, v_any))
    at_keep.wait()
    at_bias.wait()
    bias = bias_ref[0:1, :]
    first = iota((L, 2 * HD), 1) < HD
    for pair in range(HEADS // 2):
        lanes = slice(pair * 2 * HD, (pair + 1) * 2 * HD)
        qp = q_ref[:, lanes] * jnp.array(HD**-0.5, bf16)
        mixes = []
        for half in range(2):
            head = 2 * pair + half
            own = first if half == 0 else ~first
            score_ref[half] = dot(jnp.where(own, qp, jnp.zeros_like(qp)), k_ref[:, lanes], NT)
            for c in range(L // STRIP):
                rows = slice(c * STRIP, (c + 1) * STRIP)
                scores = score_ref[half, rows, :] + bias
                expo = jnp.exp(scores - jnp.max(scores, -1, keepdims=True))
                probs = expo * (1.0 / jnp.sum(expo, -1, keepdims=True))
                prob_ref[half, rows, :] = probs.astype(bf16)
            prow_ref[head] = prob_ref[half, :ROWS, :]
            pcol_ref[head] = jnp.transpose(prob_ref[half, :, :ROWS])
            mixes.append(dot(prob_ref[half], v_ref[:, lanes]))
        att_ref[:, lanes] = jnp.where(first, mixes[0], mixes[1]).astype(bf16)
        two = pl.ds(2 * pair, 2)
        ends.append(moves.start(prow_ref.at[two], prow_any.at[two]))
        ends.append(moves.start(pcol_ref.at[two], pcol_any.at[two]))
    ends.append(moves.start(att_ref, att_any))
    at_o.wait()
    unit_ref[...] = dot(att_ref[...], wo_ref[...])
    at_gain.wait()
    for c in range(L // THIN):
        rows = slice(c * THIN, (c + 1) * THIN)
        mixed = x_ref[rows, :].astype(f32) + unit_ref[rows, :]
        centred = mixed - jnp.mean(mixed, -1, keepdims=True)
        inv = lax.rsqrt(jnp.mean(centred * centred, -1, keepdims=True) + 1e-05)
        unit = centred * inv
        unit_ref[rows, :] = unit
        inv_ref[rows, :] = jnp.broadcast_to(inv, (THIN, E))
        x_ref[rows, :] = (unit * gain_ref[...]).astype(bf16)
    ends.append(moves.start(unit_ref, unit_any))
    ends.append(moves.start(inv_ref, inv_any))
    at_p.wait()
    proj = dot(x_ref[...], wp_ref[...])
    proj_ref[...] = proj
    ends.append(moves.start(proj_ref, proj_any))
    scale = lax.rsqrt(jnp.sum(proj * proj, -1, keepdims=True) + 1e-06)
    embed_ref[:L, :] = (proj * scale).astype(bf16)
    ends.append(moves.start(embed_ref, embed_any))
    for copy in ends:
        copy.wait()


def forward(keep, bias, blocks, w_query, w_key, w_value, w_out, ln_gain, w_proj):
    width = HEADS * HD
    square = shape((L, width), bf16)
    outs = (
        square,
        square,
        square,
        square,
        shape((HEADS, ROWS, L), bf16),
        shape((HEADS, ROWS, L), bf16),
        shape((L, D), f32),
        shape((L, E), f32),
        shape((L, E), f32),
        shape((2 * L, E), bf16),
    )
    ins = [
        pltpu.VMEM((L, D), bf16),
        pltpu.VMEM((8, L), f32),
        pltpu.VMEM((D, width), bf16),
        pltpu.VMEM((D, width), bf16),
        pltpu.VMEM((D, width), bf16),
        pltpu.VMEM((width, D), bf16),
        pltpu.VMEM((1, D), f32),
        pltpu.VMEM((D, E), bf16),
    ]
    work = [
        pltpu.VMEM((2, L, L), f32),
        pltpu.VMEM((2, L, L), bf16),
        pltpu.SemaphoreType.DMA((32,)),
    ]
    return call(
        forward_kernel,
        outs,
        [ANY] * 6 + [HBM] * 6,
        tuple(HBM for _ in outs),
        ins + [pltpu.VMEM(o.shape, o.dtype) for o in outs] + work,
        flops=4 * 10**9,
        limit=56,
    )(keep, bias, *blocks, w_query, w_key, w_value, w_out, ln_gain[None], w_proj)


def sums_kernel(plane_ref, embed_ref, send_ref, sums_ref, weight_ref, keep_ref):
    keep_ref[...] = embed_ref[L:, :].astype(f32)
    for c in range(PLANE):
        total = jnp.zeros((8, CHUNK), f32)
        for b in range(4):
            rows = slice(b * ROWS, (b + 1) * ROWS)
            close = dot(embed_ref[rows, :], plane_ref[c, :CHUNK, :], NT)
            near = jnp.exp2(close * (LOG2E / TAU)) * keep_ref[rows, 0:1]
            total += jnp.sum(near.reshape(ROWS // 8, 8, CHUNK), 0)
        total = jnp.sum(total, 0, keepdims=True)
        for j in range(4):
            sums_ref[4 * c + j : 4 * c + j + 1, :] = total[:, j * E : (j + 1) * E]
    weights = jnp.concatenate([plane_ref[c, CHUNK : CHUNK + LINE, :] for c in range(PLANE)], 0)
    row, col = iota((QLEN, QSET), 0), iota((QLEN, QSET), 1)
    weight = jnp.zeros((QLEN, E), f32)
    for g in range(4):
        picked = dot((col == 4 * row + g).astype(bf16), weights)
        weight = jnp.where(col // QLEN == g, picked, weight)
    weight_ref[...] = weight
    parts = weight * TAU * jnp.log(sums_ref[...])
    source, place = iota((E, QSET), 0), iota((E, QSET), 1)
    table = select(parts, source // QLEN == place % 4)
    table = jnp.sum(jnp.where(col // 4 == row, table, 0.0), 0, keepdims=True)
    send_ref[...] = jnp.broadcast_to(table, (DOCS, QSET))


def sums_call(plane, embed):
    return call(
        sums_kernel,
        (shape((DOCS, QSET), f32), shape((QLEN, E), f32), shape((QLEN, E), f32)),
        [VMEM] * 2,
        (VMEM, VMEM, VMEM),
        [pltpu.VMEM((L, E), f32)],
        flops=10**9,
    )(plane, embed)


def grads_kernel(
    table_ref, sums_ref, weight_ref, plane_ref, embed_ref, out_ref, score_ref, couple_ref
):
    _, mine = position()
    table = table_ref[...]
    lse = jnp.log(jnp.sum(jnp.exp(table), 0, keepdims=True))
    targets = jnp.concatenate(
        [plane_ref[c, CHUNK + LINE :, :] for c in range(PLANE)], 0
    ).astype(f32)
    row, col = iota((QSET, QSET), 0), iota((QSET, QSET), 1)
    target = jnp.sum(jnp.where(row == col, targets, 0.0), 0, keepdims=True).astype(i32)
    hit = row == target
    gap = lse - jnp.sum(jnp.where(hit, table, 0.0), 0, keepdims=True)
    loss = jnp.sum(gap, -1, keepdims=True)
    own = jnp.sum(jnp.where(row == mine, table, 0.0), 0, keepdims=True)
    dscore = GRAD_SCALE * (jnp.exp(own - lse) - jnp.where(target == mine, 1.0, 0.0))
    group = iota((QLEN, QSET), 1) // 4 == iota((QLEN, QSET), 0)
    wide = select(jnp.where(group, dscore, 0.0), row % 4 == col // QLEN)
    coef = wide * weight_ref[...] / sums_ref[...]
    for c in range(PLANE):
        queries = plane_ref[c, :CHUNK, :]
        score_ref[c % 2] = dot(embed_ref[:L, :], queries, NT)
        factor = jnp.concatenate([coef[4 * c + j : 4 * c + j + 1, :] for j in range(4)], 1)
        for b in range(L // STRIP):
            rows = slice(b * STRIP, (b + 1) * STRIP)
            near = jnp.exp2(score_ref[c % 2, rows, :] * (LOG2E / TAU))
            couple_ref[c % 2, rows, :] = (near * factor).astype(bf16)
        part = dot(couple_ref[c % 2], queries)
        if c == 0:
            out_ref[:L, :] = part
        else:
            out_ref[:L, :] += part
    out_ref[:L, :] = out_ref[:L, :] * embed_ref[L:, :].astype(f32)
    out_ref[L:, :] = jnp.broadcast_to(loss, (8, E))


def grads_call(table, plane, embed, sums, weight):
    return call(
        grads_kernel,
        shape((L + 8, E), f32),
        [VMEM] * 5,
        VMEM,
        [pltpu.VMEM((2, L, CHUNK), f32), pltpu.VMEM((2, L, CHUNK), bf16)],
        flops=2 * 10**9,
    )(table, sums, weight, plane, embed)


def add_kernel(own_ref, got_ref, sum_ref, send_ref):
    for b in range(4):
        rows = slice(b * ROWS, (b + 1) * ROWS)
        other = (b ^ 1) * ROWS
        total = own_ref[rows, :] + got_ref[other : other + ROWS, :]
        sum_ref[rows, :] = total
        send_ref[rows, :] = total.astype(bf16)
    loss = own_ref[L:, :] + got_ref[L:, :]
    sum_ref[L:, :] = loss
    high = loss.astype(bf16).astype(f32)
    middle = (loss - high).astype(bf16).astype(f32)
    low = loss - high - middle
    send_ref[L : L + 16, :] = jnp.concatenate([high, middle], 0).astype(bf16)
    send_ref[L + 16 :, :] = jnp.concatenate([low, low], 0).astype(bf16)


def add_call(own, got):
    return call(add_kernel, (shape((L + 8, E), f32), shape((L + 32, E), bf16)), [VMEM] * 2, (VMEM, VMEM), limit=4)(own, got)


def backward_kernel(
    sum_ref,
    got_ref,
    proj_ref,
    wp_ref,
    inv_ref,
    gain_ref,
    unit_ref,
    wo_ref,
    att_ref,
    v_ref,
    k_ref,
    q_ref,
    prow_ref,
    pcol_ref,
    wq_ref,
    wk_ref,
    wv_ref,
    out_ref,
    loss_ref,
    wide_ref,
    mixed_ref,
    ag_ref,
    qg_ref,
    kg_ref,
    vg_ref,
    delta_ref,
    inner_ref,
    score_ref,
):
    tail = got_ref[L:, :].astype(f32)
    loss = sum_ref[L:, :] + (tail[0:8] + tail[8:16] + tail[16:24])
    loss_ref[0] = loss[0, 0]
    got = got_ref[:L, :].astype(f32)
    grad = sum_ref[:L, :] + jnp.concatenate([got[2 * ROWS :], got[: 2 * ROWS]], 0)
    proj = proj_ref[...]
    scale = lax.rsqrt(jnp.sum(proj * proj, -1, keepdims=True) + 1e-06)
    embed = proj * scale
    proj_grad = ((grad - embed * jnp.sum(embed * grad, -1, keepdims=True)) * scale).astype(bf16)
    wide_ref[...] = dot(proj_grad, wp_ref[...], NT)
    for c in range(L // THIN):
        rows = slice(c * THIN, (c + 1) * THIN)
        gained = wide_ref[rows, :] * gain_ref[...]
        unit = unit_ref[rows, :]
        along = jnp.mean(gained * unit, -1, keepdims=True)
        mixed = inv_ref[rows, 0:1] * (gained - jnp.mean(gained, -1, keepdims=True) - unit * along)
        if (c + 1) * THIN <= ROWS:
            wide_ref[rows, :] = mixed
        mixed_ref[rows, :] = mixed.astype(bf16)
    ag_ref[...] = dot(mixed_ref[...], wo_ref[...], NT).astype(bf16)
    product = ag_ref[...].astype(f32) * att_ref[...].astype(f32)
    high = product.astype(bf16)
    low = (product - high.astype(f32)).astype(bf16)
    heads = (iota((HEADS * HD, E), 0) // HD == iota((HEADS * HD, E), 1)).astype(bf16)
    delta = dot(high, heads) + dot(low, heads)
    delta_ref[...] = jnp.transpose(delta)
    first = iota((ROWS, 2 * HD), 1) < HD

    def halves(t):
        none = jnp.zeros_like(t)
        return jnp.concatenate([jnp.where(first, t, none), jnp.where(first, none, t)], 0)

    def joined(t):
        return jnp.where(first, t[:ROWS], t[ROWS:]).astype(bf16)

    for pair in range(HEADS // 2):
        lanes = slice(pair * 2 * HD, (pair + 1) * 2 * HD)
        kp, qp, vp, agp = k_ref[:, lanes], q_ref[:, lanes], v_ref[:, lanes], ag_ref[:, lanes]
        inner_ref[0] = dot(halves(vp[:ROWS]), agp, NT)
        inner_ref[1] = dot(halves(agp[:ROWS]), vp, NT)
        for half in range(2):
            head = 2 * pair + half
            for c in range(ROWS // STRIP):
                rows = slice(c * STRIP, (c + 1) * STRIP)
                place = slice(half * ROWS + c * STRIP, half * ROWS + (c + 1) * STRIP)
                off = inner_ref[0, place, :] - delta_ref[head : head + 1, :]
                prob = pcol_ref[head, rows, :].astype(f32)
                score_ref[0, place, :] = (prob * (off * HD**-0.5)).astype(bf16)
                off = inner_ref[1, place, :] - delta[rows, head : head + 1]
                prob = prow_ref[head, rows, :].astype(f32)
                score_ref[1, place, :] = (prob * (off * HD**-0.5)).astype(bf16)
        two = slice(2 * pair, 2 * pair + 2)
        kg_ref[:, lanes] = joined(dot(score_ref[0], qp))
        qg_ref[:, lanes] = joined(dot(score_ref[1], kp))
        vg_ref[:, lanes] = joined(dot(pcol_ref[two].reshape(2 * ROWS, L), agp))
    total = wide_ref[:ROWS, :]
    total += dot(qg_ref[...], wq_ref[...], NT)
    total += dot(kg_ref[...], wk_ref[...], NT)
    total += dot(vg_ref[...], wv_ref[...], NT)
    out_ref[...] = total.astype(bf16)


def backward(summed, got, kept, ln_gain, w_proj, w_out, w_query, w_key, w_value):
    q, k, v, att, prow, pcol, unit, inv, proj = kept
    width = HEADS * HD
    moved = (unit, w_out, att, v, k, q, prow, pcol, w_query, w_key, w_value)
    return call(
        backward_kernel,
        (shape((ROWS, D), bf16), shape((1,), f32)),
        [VMEM] * (6 + len(moved)),
        (VMEM, SMEM),
        [
            pltpu.VMEM((L, D), f32),
            pltpu.VMEM((L, D), bf16),
            pltpu.VMEM((L, width), bf16),
            pltpu.VMEM((ROWS, width), bf16),
            pltpu.VMEM((ROWS, width), bf16),
            pltpu.VMEM((ROWS, width), bf16),
            pltpu.VMEM((E, L), f32),
            pltpu.VMEM((2, 2 * ROWS, L), f32),
            pltpu.VMEM((2, 2 * ROWS, L), bf16),
        ],
        flops=3 * 10**9,
        limit=12,
    )(summed, got, proj, w_proj, inv, ln_gain[None], *moved)


def spread(x, axes):
    return lax.all_to_all(x, axes, 0, 0)


def body(
    hidden,
    doc_len,
    doc_keep,
    w_query,
    w_key,
    w_value,
    w_out,
    ln_gain,
    w_proj,
    queries,
    query_mask,
    positive,
):
    own = pack_hidden(hidden, doc_keep)
    by_core = lax.ppermute(own, "core", SWAP)
    by_yhi = lax.ppermute(own, "yhi", SWAP)
    line = spread(pack_query(positive, queries, query_mask, by_core), "z")
    by_both = lax.ppermute(by_yhi, "core", SWAP)
    blocks = (own, by_core, by_yhi, by_both)
    keep, bias = marks_call(doc_len, blocks)
    plane = spread(repack(line, keep), ("ylo", "x"))
    *kept, embed = forward(
        keep, bias, blocks, w_query, w_key, w_value, w_out, ln_gain, w_proj
    )
    send, sums, weight = sums_call(plane, embed)
    table = spread(send, DP)
    partial = grads_call(table, plane, embed, sums, weight)
    summed, half = add_call(partial, lax.ppermute(partial, "core", SWAP))
    got = lax.ppermute(half, "yhi", SWAP)
    out, loss = backward(summed, got, kept, ln_gain, w_proj, w_out, w_query, w_key, w_value)
    return (out, loss[0])


def solution(mesh):
    fine = Mesh(np.asarray(mesh.devices).reshape(SIZES), AXES)
    placed = (
        P(AXES, None),
        P(DP),
        P(AXES),
        P(),
        P(),
        P(),
        P(),
        P(),
        P(),
        P(AXES, None, None),
        P(AXES, None),
        P(AXES),
    )
    return jax.shard_map(
        body, mesh=fine, in_specs=placed, out_specs=(P(AXES, None), P()), check_vma=False
    )
```

```python
import jax
import jax.numpy as jnp
import numpy as np
from jax import lax
from jax.experimental import pallas as pl
from jax.experimental.pallas import tpu as pltpu
from jax.sharding import Mesh, PartitionSpec as P

D = 1024
HEADS = 8
HD = 64
E = 128
QLEN = 32
L = 512
ROWS = 128
DOCS = 128
QSET = 128
AUX = 16
TAU = 0.05
GRAD_SCALE = 1024.0
NEG = -1e30
AXES = ("z", "ylo", "x", "yhi", "core")
SIZES = (16, 2, 4, 2, 2)
DP = ("z", "ylo", "x")
LINE = 16
PLANE = 8
CHUNK = LINE * QLEN
STRIP = 64
THIN = 32
MARKS_FLOPS = 10**8
LOG2E = 1.4426950408889634
SWAP = [(0, 1), (1, 0)]
bf16 = jnp.bfloat16
f32 = jnp.float32
i32 = jnp.int32
BLOCK = pl.BlockSpec()
VMEM = pl.BlockSpec(memory_space=pltpu.VMEM)
ANY = pl.BlockSpec(memory_space=pl.ANY)
HBM = pl.BlockSpec(memory_space=pltpu.MemorySpace.HBM)
SMEM = pl.BlockSpec(memory_space=pltpu.SMEM)
NN = (((1,), (0,)), ((), ()))
NT = (((1,), (1,)), ((), ()))
TN = (((0,), (0,)), ((), ()))


def dot(left, right, dims=NN):
    return lax.dot_general(left, right, dims, preferred_element_type=f32)


def iota(shape, dim):
    return lax.broadcasted_iota(i32, shape, dim)


def select(x, choice):
    choice = choice.astype(bf16)
    high = x.astype(bf16)
    rest = x - high.astype(f32)
    middle = rest.astype(bf16)
    low = (rest - middle.astype(f32)).astype(bf16)
    return dot(high, choice) + (dot(middle, choice) + dot(low, choice))


def position():
    return lax.axis_index("yhi") * 2 + lax.axis_index("core"), lax.axis_index(DP)


def call(kernel, outs, ins, out_specs=None, scratch=(), flops=0, limit=12):
    return pl.pallas_call(
        kernel,
        out_shape=outs,
        in_specs=ins,
        out_specs=jax.tree.map(lambda _: BLOCK, outs) if out_specs is None else out_specs,
        scratch_shapes=list(scratch),
        compiler_params=pltpu.CompilerParams(vmem_limit_bytes=limit * 2**20),
        cost_estimate=pl.CostEstimate(flops=flops, bytes_accessed=4 * 2**20, transcendentals=0),
    )


class Moves:
    def __init__(self, sems):
        self.sems, self.used = sems, 0

    def start(self, source, target):
        copy = pltpu.make_async_copy(source, target, self.sems.at[self.used])
        self.used += 1
        copy.start()
        return copy


def shape(dims, kind):
    return jax.ShapeDtypeStruct(dims, kind)


def pack_hidden_kernel(hidden_ref, skip_ref, own_out):
    own_out[:ROWS, :] = hidden_ref[...]
    own_out[ROWS:, :] = jnp.zeros((AUX, D), bf16)
    own_out[ROWS:, :ROWS] = jnp.broadcast_to(skip_ref[...], (AUX, ROWS)).astype(f32).astype(bf16)


def pack_hidden(hidden, doc_keep):
    return call(pack_hidden_kernel, shape((ROWS + AUX, D), bf16), [BLOCK] * 2, limit=56)(
        hidden, doc_keep[None]
    )


def pack_query_kernel(pos_ref, queries_ref, mask_ref, query_out):
    q = queries_ref[...].astype(f32)
    qn = (q * lax.rsqrt(jnp.sum(q * q, -1, keepdims=True) + 1e-06)).astype(bf16)
    repeat = (iota((QLEN, E), 1) % QLEN == iota((QLEN, E), 0)).astype(bf16)
    weights = dot(jnp.broadcast_to(mask_ref[...], (AUX, QLEN)), repeat)
    target = pos_ref[0].astype(f32)
    row = iota((AUX, E), 0)
    aux = jnp.where(row == 0, weights, jnp.where(row == 1, target, 0.0)).astype(bf16)
    for z in range(LINE):
        query_out[z, :QLEN, :] = qn
        query_out[z, QLEN:, :] = aux


def pack_query(positive, queries, query_mask):
    return call(
        pack_query_kernel,
        shape((LINE, QLEN + AUX, E), bf16),
        [SMEM, BLOCK, BLOCK],
        limit=56,
    )(positive, queries[0], query_mask)


def repack_kernel(line_ref, after_ref, out_ref):
    aux = line_ref[:, QLEN:, :].astype(f32)
    weights = aux[:, 0, :].astype(bf16)
    target = aux[:, 1, :].astype(bf16)
    for p in range(PLANE):
        for z in range(LINE):
            out_ref[p, z * QLEN : (z + 1) * QLEN, :] = line_ref[z, :QLEN, :]
        out_ref[p, CHUNK : CHUNK + LINE, :] = weights
        out_ref[p, CHUNK + LINE :, :] = target


def repack(line, after):
    out = shape((PLANE, CHUNK + 2 * LINE, E), bf16)
    return call(repack_kernel, out, [BLOCK, ANY])(line, after)


def marks_kernel(length_ref, x0_any, x1_any, x2_any, x3_any, keep_ref, bias_ref, skip_ref, sems):
    moves = Moves(sems)
    skips = [
        moves.start(source.at[pl.ds(ROWS, AUX), pl.ds(0, ROWS)], skip_ref.at[b])
        for b, source in enumerate((x0_any, x1_any, x2_any, x3_any))
    ]
    length = length_ref[0]
    me, _ = position()
    for b in range(4):
        skips[b].wait()
        start = jnp.bitwise_xor(me, b) * ROWS
        skip = skip_ref[b].astype(f32)[0:1, :]
        place = start + iota((1, ROWS), 1)
        valid = place < length
        bias = jnp.where(valid, 0.0, NEG)
        bias_ref[:, b * ROWS : (b + 1) * ROWS] = jnp.broadcast_to(bias, (8, ROWS))
        kept = jnp.where(valid & ((skip == 1.0) | (place == 0)), 1.0, 0.0)
        diagonal = iota((ROWS, ROWS), 0) == iota((ROWS, ROWS), 1)
        column = jnp.sum(jnp.where(diagonal, kept, 0.0), -1, keepdims=True)
        keep_ref[b * ROWS : (b + 1) * ROWS, :] = jnp.broadcast_to(column, (ROWS, E)).astype(bf16)


def marks_call(doc_len, blocks):
    return call(
        marks_kernel,
        (shape((L, E), bf16), shape((8, L), f32)),
        [SMEM] + [ANY] * 4,
        scratch=[pltpu.VMEM((4, AUX, ROWS), bf16), pltpu.SemaphoreType.DMA((4,))],
        flops=MARKS_FLOPS,
        limit=4,
    )(doc_len, *blocks)


def forward_kernel(
    keep_any,
    bias_any,
    x0_any,
    x1_any,
    x2_any,
    x3_any,
    wq_any,
    wk_any,
    wv_any,
    wo_any,
    gain_any,
    wp_any,
    q_any,
    k_any,
    v_any,
    att_any,
    prow_any,
    pcol_any,
    unit_any,
    inv_any,
    proj_any,
    embed_any,
    x_ref,
    bias_ref,
    wq_ref,
    wk_ref,
    wv_ref,
    wo_ref,
    gain_ref,
    wp_ref,
    q_ref,
    k_ref,
    v_ref,
    att_ref,
    prow_ref,
    pcol_ref,
    unit_ref,
    inv_ref,
    proj_ref,
    embed_ref,
    score_ref,
    prob_ref,
    sems,
):
    moves = Moves(sems)
    blocks = [
        moves.start(source.at[pl.ds(0, ROWS)], x_ref.at[pl.ds(b * ROWS, ROWS)])
        for b, source in enumerate((x0_any, x1_any, x2_any, x3_any))
    ]
    at_k = moves.start(wk_any, wk_ref)
    at_keep = moves.start(keep_any, embed_ref.at[pl.ds(L, L)])
    at_bias = moves.start(bias_any, bias_ref)
    at_q = moves.start(wq_any, wq_ref)
    at_v = moves.start(wv_any, wv_ref)
    at_o = moves.start(wo_any, wo_ref)
    at_gain = moves.start(gain_any, gain_ref)
    at_p = moves.start(wp_any, wp_ref)
    ends = []
    for copy in blocks:
        copy.wait()
    at_k.wait()
    k_ref[...] = dot(x_ref[...], wk_ref[...]).astype(bf16)
    ends.append(moves.start(k_ref, k_any))
    at_q.wait()
    q_ref[...] = dot(x_ref[...], wq_ref[...]).astype(bf16)
    ends.append(moves.start(q_ref, q_any))
    at_v.wait()
    v_ref[...] = dot(x_ref[...], wv_ref[...]).astype(bf16)
    ends.append(moves.start(v_ref, v_any))
    at_keep.wait()
    at_bias.wait()
    bias = bias_ref[0:1, :]
    first = iota((L, 2 * HD), 1) < HD
    for pair in range(HEADS // 2):
        lanes = slice(pair * 2 * HD, (pair + 1) * 2 * HD)
        qp = q_ref[:, lanes] * jnp.array(HD**-0.5, bf16)
        mixes = []
        for half in range(2):
            head = 2 * pair + half
            own = first if half == 0 else ~first
            score_ref[half] = dot(jnp.where(own, qp, jnp.zeros_like(qp)), k_ref[:, lanes], NT)
            for c in range(L // STRIP):
                rows = slice(c * STRIP, (c + 1) * STRIP)
                scores = score_ref[half, rows, :] + bias
                expo = jnp.exp(scores - jnp.max(scores, -1, keepdims=True))
                probs = expo * (1.0 / jnp.sum(expo, -1, keepdims=True))
                prob_ref[half, rows, :] = probs.astype(bf16)
            prow_ref[head] = prob_ref[half, :ROWS, :]
            pcol_ref[head] = jnp.transpose(prob_ref[half, :, :ROWS])
            mixes.append(dot(prob_ref[half], v_ref[:, lanes]))
        att_ref[:, lanes] = jnp.where(first, mixes[0], mixes[1]).astype(bf16)
        two = pl.ds(2 * pair, 2)
        ends.append(moves.start(prow_ref.at[two], prow_any.at[two]))
        ends.append(moves.start(pcol_ref.at[two], pcol_any.at[two]))
    ends.append(moves.start(att_ref, att_any))
    at_o.wait()
    unit_ref[...] = dot(att_ref[...], wo_ref[...])
    at_gain.wait()
    for c in range(L // THIN):
        rows = slice(c * THIN, (c + 1) * THIN)
        mixed = x_ref[rows, :].astype(f32) + unit_ref[rows, :]
        centred = mixed - jnp.mean(mixed, -1, keepdims=True)
        inv = lax.rsqrt(jnp.mean(centred * centred, -1, keepdims=True) + 1e-05)
        unit = centred * inv
        unit_ref[rows, :] = unit
        inv_ref[rows, :] = jnp.broadcast_to(inv, (THIN, E))
        x_ref[rows, :] = (unit * gain_ref[...]).astype(bf16)
    ends.append(moves.start(unit_ref, unit_any))
    ends.append(moves.start(inv_ref, inv_any))
    at_p.wait()
    proj = dot(x_ref[...], wp_ref[...])
    proj_ref[...] = proj
    ends.append(moves.start(proj_ref, proj_any))
    scale = lax.rsqrt(jnp.sum(proj * proj, -1, keepdims=True) + 1e-06)
    embed_ref[:L, :] = (proj * scale).astype(bf16)
    ends.append(moves.start(embed_ref, embed_any))
    for copy in ends:
        copy.wait()


def forward(keep, bias, blocks, w_query, w_key, w_value, w_out, ln_gain, w_proj):
    width = HEADS * HD
    square = shape((L, width), bf16)
    outs = (
        square,
        square,
        square,
        square,
        shape((HEADS, ROWS, L), bf16),
        shape((HEADS, ROWS, L), bf16),
        shape((L, D), f32),
        shape((L, E), f32),
        shape((L, E), f32),
        shape((2 * L, E), bf16),
    )
    ins = [
        pltpu.VMEM((L, D), bf16),
        pltpu.VMEM((8, L), f32),
        pltpu.VMEM((D, width), bf16),
        pltpu.VMEM((D, width), bf16),
        pltpu.VMEM((D, width), bf16),
        pltpu.VMEM((width, D), bf16),
        pltpu.VMEM((1, D), f32),
        pltpu.VMEM((D, E), bf16),
    ]
    work = [
        pltpu.VMEM((2, L, L), f32),
        pltpu.VMEM((2, L, L), bf16),
        pltpu.SemaphoreType.DMA((32,)),
    ]
    return call(
        forward_kernel,
        outs,
        [ANY] * 6 + [HBM] * 6,
        tuple(HBM for _ in outs),
        ins + [pltpu.VMEM(o.shape, o.dtype) for o in outs] + work,
        flops=6 * 10**9,
        limit=52,
    )(keep, bias, *blocks, w_query, w_key, w_value, w_out, ln_gain[None], w_proj)


def sums_kernel(plane_ref, embed_ref, send_ref, sums_ref, weight_ref, keep_ref):
    keep_ref[...] = embed_ref[L:, :].astype(f32)
    for c in range(PLANE):
        total = jnp.zeros((8, CHUNK), f32)
        for b in range(4):
            rows = slice(b * ROWS, (b + 1) * ROWS)
            close = dot(embed_ref[rows, :], plane_ref[c, :CHUNK, :], NT)
            near = jnp.exp2(close * (LOG2E / TAU)) * keep_ref[rows, 0:1]
            total += jnp.sum(near.reshape(ROWS // 8, 8, CHUNK), 0)
        total = jnp.sum(total, 0, keepdims=True)
        for j in range(4):
            sums_ref[4 * c + j : 4 * c + j + 1, :] = total[:, j * E : (j + 1) * E]
    weights = jnp.concatenate([plane_ref[c, CHUNK : CHUNK + LINE, :] for c in range(PLANE)], 0)
    row, col = iota((QLEN, QSET), 0), iota((QLEN, QSET), 1)
    weight = jnp.zeros((QLEN, E), f32)
    for g in range(4):
        picked = dot((col == 4 * row + g).astype(bf16), weights)
        weight = jnp.where(col // QLEN == g, picked, weight)
    weight_ref[...] = weight
    parts = weight * TAU * jnp.log(sums_ref[...])
    source, place = iota((E, QSET), 0), iota((E, QSET), 1)
    table = select(parts, source // QLEN == place % 4)
    table = jnp.sum(jnp.where(col // 4 == row, table, 0.0), 0, keepdims=True)
    send_ref[...] = jnp.broadcast_to(table, (DOCS, QSET))


def sums_call(plane, embed):
    return call(
        sums_kernel,
        (shape((DOCS, QSET), f32), shape((QLEN, E), f32), shape((QLEN, E), f32)),
        [VMEM] * 2,
        (VMEM, VMEM, VMEM),
        [pltpu.VMEM((L, E), f32)],
        flops=10**9,
    )(plane, embed)


def grads_kernel(
    table_ref, sums_ref, weight_ref, plane_ref, embed_ref, out_ref, score_ref, couple_ref
):
    _, mine = position()
    table = table_ref[...]
    lse = jnp.log(jnp.sum(jnp.exp(table), 0, keepdims=True))
    targets = jnp.concatenate(
        [plane_ref[c, CHUNK + LINE :, :] for c in range(PLANE)], 0
    ).astype(f32)
    row, col = iota((QSET, QSET), 0), iota((QSET, QSET), 1)
    target = jnp.sum(jnp.where(row == col, targets, 0.0), 0, keepdims=True).astype(i32)
    hit = row == target
    gap = lse - jnp.sum(jnp.where(hit, table, 0.0), 0, keepdims=True)
    loss = jnp.sum(gap, -1, keepdims=True)
    own = jnp.sum(jnp.where(row == mine, table, 0.0), 0, keepdims=True)
    dscore = GRAD_SCALE * (jnp.exp(own - lse) - jnp.where(target == mine, 1.0, 0.0))
    group = iota((QLEN, QSET), 1) // 4 == iota((QLEN, QSET), 0)
    wide = select(jnp.where(group, dscore, 0.0), row % 4 == col // QLEN)
    coef = wide * weight_ref[...] / sums_ref[...]
    for c in range(PLANE):
        queries = plane_ref[c, :CHUNK, :]
        score_ref[c % 2] = dot(embed_ref[:L, :], queries, NT)
        factor = jnp.concatenate([coef[4 * c + j : 4 * c + j + 1, :] for j in range(4)], 1)
        for b in range(L // STRIP):
            rows = slice(b * STRIP, (b + 1) * STRIP)
            near = jnp.exp2(score_ref[c % 2, rows, :] * (LOG2E / TAU))
            couple_ref[c % 2, rows, :] = (near * factor).astype(bf16)
        part = dot(couple_ref[c % 2], queries)
        if c == 0:
            out_ref[:L, :] = part
        else:
            out_ref[:L, :] += part
    out_ref[:L, :] = out_ref[:L, :] * embed_ref[L:, :].astype(f32)
    out_ref[L:, :] = jnp.broadcast_to(loss, (8, E))


def grads_call(table, plane, embed, sums, weight):
    return call(
        grads_kernel,
        shape((L + 8, E), f32),
        [VMEM] * 5,
        VMEM,
        [pltpu.VMEM((2, L, CHUNK), f32), pltpu.VMEM((2, L, CHUNK), bf16)],
        flops=2 * 10**9,
    )(table, sums, weight, plane, embed)


def add_kernel(own_ref, got_ref, sum_ref, send_ref):
    for b in range(4):
        rows = slice(b * ROWS, (b + 1) * ROWS)
        other = (b ^ 1) * ROWS
        total = own_ref[rows, :] + got_ref[other : other + ROWS, :]
        sum_ref[rows, :] = total
        send_ref[rows, :] = total.astype(bf16)
    loss = own_ref[L:, :] + got_ref[L:, :]
    sum_ref[L:, :] = loss
    high = loss.astype(bf16).astype(f32)
    middle = (loss - high).astype(bf16).astype(f32)
    low = loss - high - middle
    send_ref[L : L + 16, :] = jnp.concatenate([high, middle], 0).astype(bf16)
    send_ref[L + 16 :, :] = jnp.concatenate([low, low], 0).astype(bf16)


def add_call(own, got):
    return call(add_kernel, (shape((L + 8, E), f32), shape((L + 32, E), bf16)), [VMEM] * 2, (VMEM, VMEM), limit=4)(own, got)


def backward_kernel(
    sum_ref,
    got_ref,
    proj_ref,
    wp_ref,
    inv_ref,
    gain_ref,
    unit_ref,
    wo_ref,
    att_ref,
    v_ref,
    k_ref,
    q_ref,
    prow_ref,
    pcol_ref,
    wq_ref,
    wk_ref,
    wv_ref,
    out_ref,
    loss_ref,
    wide_ref,
    mixed_ref,
    ag_ref,
    qg_ref,
    kg_ref,
    vg_ref,
    delta_ref,
    inner_ref,
    score_ref,
):
    tail = got_ref[L:, :].astype(f32)
    loss = sum_ref[L:, :] + (tail[0:8] + tail[8:16] + tail[16:24])
    loss_ref[0] = loss[0, 0]
    got = got_ref[:L, :].astype(f32)
    grad = sum_ref[:L, :] + jnp.concatenate([got[2 * ROWS :], got[: 2 * ROWS]], 0)
    proj = proj_ref[...]
    scale = lax.rsqrt(jnp.sum(proj * proj, -1, keepdims=True) + 1e-06)
    embed = proj * scale
    proj_grad = ((grad - embed * jnp.sum(embed * grad, -1, keepdims=True)) * scale).astype(bf16)
    wide_ref[...] = dot(proj_grad, wp_ref[...], NT)
    for c in range(L // THIN):
        rows = slice(c * THIN, (c + 1) * THIN)
        gained = wide_ref[rows, :] * gain_ref[...]
        unit = unit_ref[rows, :]
        along = jnp.mean(gained * unit, -1, keepdims=True)
        mixed = inv_ref[rows, 0:1] * (gained - jnp.mean(gained, -1, keepdims=True) - unit * along)
        if (c + 1) * THIN <= ROWS:
            wide_ref[rows, :] = mixed
        mixed_ref[rows, :] = mixed.astype(bf16)
    ag_ref[...] = dot(mixed_ref[...], wo_ref[...], NT).astype(bf16)
    product = ag_ref[...].astype(f32) * att_ref[...].astype(f32)
    high = product.astype(bf16)
    low = (product - high.astype(f32)).astype(bf16)
    heads = (iota((HEADS * HD, E), 0) // HD == iota((HEADS * HD, E), 1)).astype(bf16)
    delta = dot(high, heads) + dot(low, heads)
    delta_ref[...] = jnp.transpose(delta)
    first = iota((ROWS, 2 * HD), 1) < HD

    def halves(t):
        none = jnp.zeros_like(t)
        return jnp.concatenate([jnp.where(first, t, none), jnp.where(first, none, t)], 0)

    def joined(t):
        return jnp.where(first, t[:ROWS], t[ROWS:]).astype(bf16)

    for pair in range(HEADS // 2):
        lanes = slice(pair * 2 * HD, (pair + 1) * 2 * HD)
        kp, qp, vp, agp = k_ref[:, lanes], q_ref[:, lanes], v_ref[:, lanes], ag_ref[:, lanes]
        inner_ref[0] = dot(halves(vp[:ROWS]), agp, NT)
        inner_ref[1] = dot(halves(agp[:ROWS]), vp, NT)
        for half in range(2):
            head = 2 * pair + half
            for c in range(ROWS // STRIP):
                rows = slice(c * STRIP, (c + 1) * STRIP)
                place = slice(half * ROWS + c * STRIP, half * ROWS + (c + 1) * STRIP)
                off = inner_ref[0, place, :] - delta_ref[head : head + 1, :]
                prob = pcol_ref[head, rows, :].astype(f32)
                score_ref[0, place, :] = (prob * (off * HD**-0.5)).astype(bf16)
                off = inner_ref[1, place, :] - delta[rows, head : head + 1]
                prob = prow_ref[head, rows, :].astype(f32)
                score_ref[1, place, :] = (prob * (off * HD**-0.5)).astype(bf16)
        two = slice(2 * pair, 2 * pair + 2)
        kg_ref[:, lanes] = joined(dot(score_ref[0], qp))
        qg_ref[:, lanes] = joined(dot(score_ref[1], kp))
        vg_ref[:, lanes] = joined(dot(pcol_ref[two].reshape(2 * ROWS, L), agp))
    total = wide_ref[:ROWS, :]
    total += dot(qg_ref[...], wq_ref[...], NT)
    total += dot(kg_ref[...], wk_ref[...], NT)
    total += dot(vg_ref[...], wv_ref[...], NT)
    out_ref[...] = total.astype(bf16)


def backward(summed, got, kept, ln_gain, w_proj, w_out, w_query, w_key, w_value):
    q, k, v, att, prow, pcol, unit, inv, proj = kept
    width = HEADS * HD
    moved = (unit, w_out, att, v, k, q, prow, pcol, w_query, w_key, w_value)
    return call(
        backward_kernel,
        (shape((ROWS, D), bf16), shape((1,), f32)),
        [VMEM] * (6 + len(moved)),
        (VMEM, SMEM),
        [
            pltpu.VMEM((L, D), f32),
            pltpu.VMEM((L, D), bf16),
            pltpu.VMEM((L, width), bf16),
            pltpu.VMEM((ROWS, width), bf16),
            pltpu.VMEM((ROWS, width), bf16),
            pltpu.VMEM((ROWS, width), bf16),
            pltpu.VMEM((E, L), f32),
            pltpu.VMEM((2, 2 * ROWS, L), f32),
            pltpu.VMEM((2, 2 * ROWS, L), bf16),
        ],
        flops=3 * 10**9,
        limit=12,
    )(summed, got, proj, w_proj, inv, ln_gain[None], *moved)


def spread(x, axes):
    return lax.all_to_all(x, axes, 0, 0)


def body(
    hidden,
    doc_len,
    doc_keep,
    w_query,
    w_key,
    w_value,
    w_out,
    ln_gain,
    w_proj,
    queries,
    query_mask,
    positive,
):
    own = pack_hidden(hidden, doc_keep)
    by_core = lax.ppermute(own, "core", SWAP)
    by_yhi = lax.ppermute(own, "yhi", SWAP)
    line = spread(pack_query(positive, queries, query_mask), "z")
    packed = repack(line, by_core)
    plane = spread(packed, ("ylo", "x"))
    by_yhi, _ = lax.optimization_barrier((by_yhi, packed))
    by_both = lax.ppermute(by_yhi, "core", SWAP)
    blocks = (own, by_core, by_yhi, by_both)
    keep, bias = marks_call(doc_len, blocks)
    *kept, embed = forward(
        keep, bias, blocks, w_query, w_key, w_value, w_out, ln_gain, w_proj
    )
    send, sums, weight = sums_call(plane, embed)
    table = spread(send, DP)
    partial = grads_call(table, plane, embed, sums, weight)
    summed, half = add_call(partial, lax.ppermute(partial, "core", SWAP))
    got = lax.ppermute(half, "yhi", SWAP)
    out, loss = backward(summed, got, kept, ln_gain, w_proj, w_out, w_query, w_key, w_value)
    return (out, loss[0])


def solution(mesh):
    fine = Mesh(np.asarray(mesh.devices).reshape(SIZES), AXES)
    placed = (
        P(AXES, None),
        P(DP),
        P(AXES),
        P(),
        P(),
        P(),
        P(),
        P(),
        P(),
        P(AXES, None, None),
        P(AXES, None),
        P(AXES),
    )
    return jax.shard_map(
        body, mesh=fine, in_specs=placed, out_specs=(P(AXES, None), P()), check_vma=False
    )
```

```python
import jax
import jax.numpy as jnp
import numpy as np
from jax import lax
from jax.experimental import pallas as pl
from jax.experimental.pallas import tpu as pltpu
from jax.sharding import Mesh, PartitionSpec as P

D = 1024
HEADS = 8
HD = 64
E = 128
QLEN = 32
L = 512
ROWS = 128
DOCS = 128
QSET = 128
AUX = 16
TAIL = 8
TAU = 0.05
GRAD_SCALE = 1024.0
NEG = -1e30
AXES = ("z", "ylo", "x", "yhi", "core")
SIZES = (16, 2, 4, 2, 2)
DP = ("z", "ylo", "x")
LINE = 16
PLANE = 8
CHUNK = LINE * QLEN
STRIP = 64
THIN = 32
MARKS_FLOPS = 10**8
LOG2E = 1.4426950408889634
SWAP = [(0, 1), (1, 0)]
bf16 = jnp.bfloat16
f32 = jnp.float32
i32 = jnp.int32
BLOCK = pl.BlockSpec()
VMEM = pl.BlockSpec(memory_space=pltpu.VMEM)
ANY = pl.BlockSpec(memory_space=pl.ANY)
HBM = pl.BlockSpec(memory_space=pltpu.MemorySpace.HBM)
SMEM = pl.BlockSpec(memory_space=pltpu.SMEM)
NN = (((1,), (0,)), ((), ()))
NT = (((1,), (1,)), ((), ()))
TN = (((0,), (0,)), ((), ()))


def dot(left, right, dims=NN):
    return lax.dot_general(left, right, dims, preferred_element_type=f32)


def iota(shape, dim):
    return lax.broadcasted_iota(i32, shape, dim)


def select(x, choice):
    choice = choice.astype(bf16)
    high = x.astype(bf16)
    rest = x - high.astype(f32)
    middle = rest.astype(bf16)
    low = (rest - middle.astype(f32)).astype(bf16)
    return dot(high, choice) + (dot(middle, choice) + dot(low, choice))


def position():
    return lax.axis_index("yhi") * 2 + lax.axis_index("core"), lax.axis_index(DP)


def call(kernel, outs, ins, out_specs=None, scratch=(), flops=0, limit=12):
    return pl.pallas_call(
        kernel,
        out_shape=outs,
        in_specs=ins,
        out_specs=jax.tree.map(lambda _: BLOCK, outs) if out_specs is None else out_specs,
        scratch_shapes=list(scratch),
        compiler_params=pltpu.CompilerParams(vmem_limit_bytes=limit * 2**20),
        cost_estimate=pl.CostEstimate(flops=flops, bytes_accessed=4 * 2**20, transcendentals=0),
    )


class Moves:
    def __init__(self, sems):
        self.sems, self.used = sems, 0

    def start(self, source, target):
        copy = pltpu.make_async_copy(source, target, self.sems.at[self.used])
        self.used += 1
        copy.start()
        return copy


def shape(dims, kind):
    return jax.ShapeDtypeStruct(dims, kind)


def pack_hidden_kernel(hidden_ref, skip_ref, own_out):
    own_out[:ROWS, :] = hidden_ref[...]
    own_out[ROWS:, :] = jnp.zeros((AUX, D), bf16)
    own_out[ROWS:, :ROWS] = jnp.broadcast_to(skip_ref[...], (AUX, ROWS)).astype(f32).astype(bf16)


def pack_hidden(hidden, doc_keep):
    return call(pack_hidden_kernel, shape((ROWS + AUX, D), bf16), [BLOCK] * 2, limit=56)(
        hidden, doc_keep[None]
    )


def pack_query_kernel(pos_ref, queries_ref, mask_ref, query_out):
    q = queries_ref[...].astype(f32)
    qn = q * lax.rsqrt(jnp.sum(q * q, -1, keepdims=True) + 1e-06)
    repeat = (iota((QLEN, E), 1) % QLEN == iota((QLEN, E), 0)).astype(bf16)
    weights = dot(jnp.broadcast_to(mask_ref[...], (16, QLEN)), repeat)[:TAIL]
    target = jnp.broadcast_to(pos_ref[...], (TAIL, E)).astype(f32)
    row = iota((TAIL, E), 0)
    tail = jnp.where(row == 0, weights, jnp.where(row == 1, target, 0.0))
    packet = jnp.concatenate([qn, tail], 0).astype(bf16)
    query_out[...] = jnp.broadcast_to(packet[None], (LINE, QLEN + TAIL, E))


def pack_query(positive, queries, query_mask):
    return call(
        pack_query_kernel,
        shape((LINE, QLEN + TAIL, E), bf16),
        [BLOCK] * 3,
        VMEM,
        limit=56,
    )(positive[None], queries[0], query_mask)


def repack_kernel(line_ref, after_ref, out_ref):
    line = line_ref[...].astype(f32)
    queries = line[:, :QLEN, :].reshape(CHUNK, E)
    packed = jnp.concatenate([queries, line[:, QLEN, :], line[:, QLEN + 1, :]], 0).astype(bf16)
    for p in range(PLANE):
        out_ref[p] = packed


def repack(line, after):
    out = shape((PLANE, CHUNK + 2 * LINE, E), bf16)
    return call(repack_kernel, out, [VMEM, ANY], VMEM, limit=8)(line, after)


def marks_kernel(length_ref, x0_any, x1_any, x2_any, x3_any, keep_ref, bias_ref, skip_ref, sems):
    moves = Moves(sems)
    skips = [
        moves.start(source.at[pl.ds(ROWS, AUX), pl.ds(0, ROWS)], skip_ref.at[b])
        for b, source in enumerate((x0_any, x1_any, x2_any, x3_any))
    ]
    length = length_ref[0]
    me, _ = position()
    for b in range(4):
        skips[b].wait()
        start = jnp.bitwise_xor(me, b) * ROWS
        skip = skip_ref[b].astype(f32)[0:1, :]
        place = start + iota((1, ROWS), 1)
        valid = place < length
        bias = jnp.where(valid, 0.0, NEG)
        bias_ref[:, b * ROWS : (b + 1) * ROWS] = jnp.broadcast_to(bias, (8, ROWS))
        kept = jnp.where(valid & ((skip == 1.0) | (place == 0)), 1.0, 0.0)
        diagonal = iota((ROWS, ROWS), 0) == iota((ROWS, ROWS), 1)
        column = jnp.sum(jnp.where(diagonal, kept, 0.0), -1, keepdims=True)
        keep_ref[b * ROWS : (b + 1) * ROWS, :] = jnp.broadcast_to(column, (ROWS, E)).astype(bf16)


def marks_call(doc_len, blocks):
    return call(
        marks_kernel,
        (shape((L, E), bf16), shape((8, L), f32)),
        [SMEM] + [ANY] * 4,
        scratch=[pltpu.VMEM((4, AUX, ROWS), bf16), pltpu.SemaphoreType.DMA((4,))],
        flops=MARKS_FLOPS,
        limit=4,
    )(doc_len, *blocks)


def forward_kernel(
    keep_any,
    bias_any,
    x0_any,
    x1_any,
    x2_any,
    x3_any,
    wq_any,
    wk_any,
    wv_any,
    wo_any,
    gain_any,
    wp_any,
    q_any,
    k_any,
    v_any,
    att_any,
    prow_any,
    pcol_any,
    unit_any,
    inv_any,
    proj_any,
    embed_ref,
    x_ref,
    bias_ref,
    wq_ref,
    wk_ref,
    wv_ref,
    wo_ref,
    gain_ref,
    wp_ref,
    q_ref,
    k_ref,
    v_ref,
    att_ref,
    prow_ref,
    pcol_ref,
    unit_ref,
    inv_ref,
    proj_ref,
    score_ref,
    prob_ref,
    sems,
):
    moves = Moves(sems)
    blocks = [
        moves.start(source.at[pl.ds(0, ROWS)], x_ref.at[pl.ds(b * ROWS, ROWS)])
        for b, source in enumerate((x0_any, x1_any, x2_any, x3_any))
    ]
    at_k = moves.start(wk_any, wk_ref)
    at_keep = moves.start(keep_any, embed_ref.at[pl.ds(L, L)])
    at_bias = moves.start(bias_any, bias_ref)
    at_q = moves.start(wq_any, wq_ref)
    at_v = moves.start(wv_any, wv_ref)
    at_o = moves.start(wo_any, wo_ref)
    at_gain = moves.start(gain_any, gain_ref)
    at_p = moves.start(wp_any, wp_ref)
    ends = []
    for copy in blocks:
        copy.wait()
    at_k.wait()
    k_ref[...] = dot(x_ref[...], wk_ref[...]).astype(bf16)
    ends.append(moves.start(k_ref, k_any))
    at_q.wait()
    q_ref[...] = dot(x_ref[...], wq_ref[...]).astype(bf16)
    ends.append(moves.start(q_ref, q_any))
    at_v.wait()
    v_ref[...] = dot(x_ref[...], wv_ref[...]).astype(bf16)
    ends.append(moves.start(v_ref, v_any))
    at_keep.wait()
    at_bias.wait()
    bias = bias_ref[0:1, :]
    first = iota((L, 2 * HD), 1) < HD
    for pair in range(HEADS // 2):
        lanes = slice(pair * 2 * HD, (pair + 1) * 2 * HD)
        qp = q_ref[:, lanes] * jnp.array(HD**-0.5, bf16)
        mixes = []
        for half in range(2):
            head = 2 * pair + half
            own = first if half == 0 else ~first
            score_ref[half] = dot(jnp.where(own, qp, jnp.zeros_like(qp)), k_ref[:, lanes], NT)
            for c in range(L // STRIP):
                rows = slice(c * STRIP, (c + 1) * STRIP)
                scores = score_ref[half, rows, :] + bias
                expo = jnp.exp(scores - jnp.max(scores, -1, keepdims=True))
                probs = expo * (1.0 / jnp.sum(expo, -1, keepdims=True))
                prob_ref[half, rows, :] = probs.astype(bf16)
            prow_ref[head] = prob_ref[half, :ROWS, :]
            pcol_ref[head] = jnp.transpose(prob_ref[half, :, :ROWS])
            mixes.append(dot(prob_ref[half], v_ref[:, lanes]))
        att_ref[:, lanes] = jnp.where(first, mixes[0], mixes[1]).astype(bf16)
        two = pl.ds(2 * pair, 2)
        ends.append(moves.start(prow_ref.at[two], prow_any.at[two]))
        ends.append(moves.start(pcol_ref.at[two], pcol_any.at[two]))
    ends.append(moves.start(att_ref, att_any))
    at_o.wait()
    unit_ref[...] = dot(att_ref[...], wo_ref[...])
    at_gain.wait()
    for c in range(L // THIN):
        rows = slice(c * THIN, (c + 1) * THIN)
        mixed = x_ref[rows, :].astype(f32) + unit_ref[rows, :]
        centred = mixed - jnp.mean(mixed, -1, keepdims=True)
        inv = lax.rsqrt(jnp.mean(centred * centred, -1, keepdims=True) + 1e-05)
        unit = centred * inv
        unit_ref[rows, :] = unit
        inv_ref[rows, :] = jnp.broadcast_to(inv, (THIN, E))
        x_ref[rows, :] = (unit * gain_ref[...]).astype(bf16)
        if (c + 1) * THIN % ROWS == 0:
            done = pl.ds((c + 1) * THIN - ROWS, ROWS)
            ends.append(moves.start(unit_ref.at[done], unit_any.at[done]))
    ends.append(moves.start(inv_ref, inv_any))
    at_p.wait()
    proj = dot(x_ref[...], wp_ref[...])
    proj_ref[...] = proj
    ends.append(moves.start(proj_ref, proj_any))
    scale = lax.rsqrt(jnp.sum(proj * proj, -1, keepdims=True) + 1e-06)
    embed_ref[:L, :] = (proj * scale).astype(bf16)
    for copy in ends:
        copy.wait()


def forward(keep, bias, blocks, w_query, w_key, w_value, w_out, ln_gain, w_proj):
    width = HEADS * HD
    square = shape((L, width), bf16)
    outs = (
        square,
        square,
        square,
        square,
        shape((HEADS, ROWS, L), bf16),
        shape((HEADS, ROWS, L), bf16),
        shape((L, D), f32),
        shape((L, E), f32),
        shape((L, E), f32),
        shape((2 * L, E), bf16),
    )
    ins = [
        pltpu.VMEM((L, D), bf16),
        pltpu.VMEM((8, L), f32),
        pltpu.VMEM((D, width), bf16),
        pltpu.VMEM((D, width), bf16),
        pltpu.VMEM((D, width), bf16),
        pltpu.VMEM((width, D), bf16),
        pltpu.VMEM((1, D), f32),
        pltpu.VMEM((D, E), bf16),
    ]
    work = [
        pltpu.VMEM((2, L, L), f32),
        pltpu.VMEM((2, L, L), bf16),
        pltpu.SemaphoreType.DMA((32,)),
    ]
    return call(
        forward_kernel,
        outs,
        [ANY] * 6 + [HBM] * 6,
        tuple(HBM for _ in outs[:-1]) + (VMEM,),
        ins + [pltpu.VMEM(o.shape, o.dtype) for o in outs[:-1]] + work,
        flops=6 * 10**9,
        limit=52,
    )(keep, bias, *blocks, w_query, w_key, w_value, w_out, ln_gain[None], w_proj)


def sums_kernel(plane_ref, embed_ref, send_ref, sums_ref, weight_ref, keep_ref):
    keep_ref[...] = embed_ref[L:, :].astype(f32)
    for c in range(PLANE):
        total = jnp.zeros((8, CHUNK), f32)
        for b in range(4):
            rows = slice(b * ROWS, (b + 1) * ROWS)
            close = dot(embed_ref[rows, :], plane_ref[c, :CHUNK, :], NT)
            near = jnp.exp2(close * (LOG2E / TAU)) * keep_ref[rows, 0:1]
            total += jnp.sum(near.reshape(ROWS // 8, 8, CHUNK), 0)
        total = jnp.sum(total, 0, keepdims=True)
        for j in range(4):
            sums_ref[4 * c + j : 4 * c + j + 1, :] = total[:, j * E : (j + 1) * E]
    weights = jnp.concatenate([plane_ref[c, CHUNK : CHUNK + LINE, :] for c in range(PLANE)], 0)
    row, col = iota((QLEN, QSET), 0), iota((QLEN, QSET), 1)
    weight = jnp.zeros((QLEN, E), f32)
    for g in range(4):
        picked = dot((col == 4 * row + g).astype(bf16), weights)
        weight = jnp.where(col // QLEN == g, picked, weight)
    weight_ref[...] = weight
    parts = weight * TAU * jnp.log(sums_ref[...])
    source, place = iota((E, QSET), 0), iota((E, QSET), 1)
    table = select(parts, source // QLEN == place % 4)
    table = jnp.sum(jnp.where(col // 4 == row, table, 0.0), 0, keepdims=True)
    send_ref[...] = jnp.broadcast_to(table, (DOCS, QSET))


def sums_call(plane, embed):
    return call(
        sums_kernel,
        (shape((DOCS, QSET), f32), shape((QLEN, E), f32), shape((QLEN, E), f32)),
        [VMEM] * 2,
        (VMEM, VMEM, VMEM),
        [pltpu.VMEM((L, E), f32)],
        flops=10**9,
    )(plane, embed)


def grads_kernel(
    table_ref, sums_ref, weight_ref, plane_ref, embed_ref, out_ref, score_ref, couple_ref
):
    _, mine = position()
    table = table_ref[...]
    lse = jnp.log(jnp.sum(jnp.exp(table), 0, keepdims=True))
    targets = jnp.concatenate(
        [plane_ref[c, CHUNK + LINE :, :] for c in range(PLANE)], 0
    ).astype(f32)
    row, col = iota((QSET, QSET), 0), iota((QSET, QSET), 1)
    target = jnp.sum(jnp.where(row == col, targets, 0.0), 0, keepdims=True).astype(i32)
    hit = row == target
    gap = lse - jnp.sum(jnp.where(hit, table, 0.0), 0, keepdims=True)
    loss = jnp.sum(gap, -1, keepdims=True)
    own = jnp.sum(jnp.where(row == mine, table, 0.0), 0, keepdims=True)
    dscore = GRAD_SCALE * (jnp.exp(own - lse) - jnp.where(target == mine, 1.0, 0.0))
    group = iota((QLEN, QSET), 1) // 4 == iota((QLEN, QSET), 0)
    wide = select(jnp.where(group, dscore, 0.0), row % 4 == col // QLEN)
    coef = wide * weight_ref[...] / sums_ref[...]
    for c in range(PLANE):
        queries = plane_ref[c, :CHUNK, :]
        score_ref[c % 2] = dot(embed_ref[:L, :], queries, NT)
        factor = jnp.concatenate([coef[4 * c + j : 4 * c + j + 1, :] for j in range(4)], 1)
        for b in range(L // STRIP):
            rows = slice(b * STRIP, (b + 1) * STRIP)
            near = jnp.exp2(score_ref[c % 2, rows, :] * (LOG2E / TAU))
            couple_ref[c % 2, rows, :] = (near * factor).astype(bf16)
        part = dot(couple_ref[c % 2], queries)
        if c == 0:
            out_ref[:L, :] = part
        else:
            out_ref[:L, :] += part
    out_ref[:L, :] = out_ref[:L, :] * embed_ref[L:, :].astype(f32)
    out_ref[L:, :] = jnp.broadcast_to(loss, (8, E))


def grads_call(table, plane, embed, sums, weight):
    return call(
        grads_kernel,
        shape((L + 8, E), f32),
        [VMEM] * 5,
        VMEM,
        [pltpu.VMEM((2, L, CHUNK), f32), pltpu.VMEM((2, L, CHUNK), bf16)],
        flops=2 * 10**9,
    )(table, sums, weight, plane, embed)


def add_kernel(own_ref, got_ref, sum_ref, send_ref):
    for b in range(4):
        rows = slice(b * ROWS, (b + 1) * ROWS)
        other = (b ^ 1) * ROWS
        total = own_ref[rows, :] + got_ref[other : other + ROWS, :]
        sum_ref[rows, :] = total
        send_ref[rows, :] = total.astype(bf16)
    loss = own_ref[L:, :] + got_ref[L:, :]
    sum_ref[L:, :] = loss
    high = loss.astype(bf16).astype(f32)
    middle = (loss - high).astype(bf16).astype(f32)
    low = loss - high - middle
    send_ref[L : L + 16, :] = jnp.concatenate([high, middle], 0).astype(bf16)
    send_ref[L + 16 :, :] = jnp.concatenate([low, low], 0).astype(bf16)


def add_call(own, got):
    return call(add_kernel, (shape((L + 8, E), f32), shape((L + 32, E), bf16)), [VMEM] * 2, (VMEM, VMEM), limit=4)(own, got)


def backward_kernel(
    sum_ref,
    got_ref,
    proj_ref,
    wp_ref,
    inv_ref,
    gain_ref,
    unit_ref,
    wo_ref,
    att_ref,
    v_ref,
    k_ref,
    q_ref,
    prow_ref,
    pcol_ref,
    wq_ref,
    wk_ref,
    wv_ref,
    out_ref,
    loss_ref,
    wide_ref,
    mixed_ref,
    ag_ref,
    qg_ref,
    kg_ref,
    vg_ref,
    delta_ref,
    inner_ref,
    score_ref,
):
    tail = got_ref[L:, :].astype(f32)
    loss = sum_ref[L:, :] + (tail[0:8] + tail[8:16] + tail[16:24])
    loss_ref[0] = loss[0, 0]
    got = got_ref[:L, :].astype(f32)
    grad = sum_ref[:L, :] + jnp.concatenate([got[2 * ROWS :], got[: 2 * ROWS]], 0)
    proj = proj_ref[...]
    scale = lax.rsqrt(jnp.sum(proj * proj, -1, keepdims=True) + 1e-06)
    embed = proj * scale
    proj_grad = ((grad - embed * jnp.sum(embed * grad, -1, keepdims=True)) * scale).astype(bf16)
    wide_ref[...] = dot(proj_grad, wp_ref[...], NT)
    for c in range(L // THIN):
        rows = slice(c * THIN, (c + 1) * THIN)
        gained = wide_ref[rows, :] * gain_ref[...]
        unit = unit_ref[rows, :]
        along = jnp.mean(gained * unit, -1, keepdims=True)
        mixed = inv_ref[rows, 0:1] * (gained - jnp.mean(gained, -1, keepdims=True) - unit * along)
        if (c + 1) * THIN <= ROWS:
            wide_ref[rows, :] = mixed
        mixed_ref[rows, :] = mixed.astype(bf16)
    ag_ref[...] = dot(mixed_ref[...], wo_ref[...], NT).astype(bf16)
    product = ag_ref[...].astype(f32) * att_ref[...].astype(f32)
    high = product.astype(bf16)
    low = (product - high.astype(f32)).astype(bf16)
    heads = (iota((HEADS * HD, E), 0) // HD == iota((HEADS * HD, E), 1)).astype(bf16)
    delta = dot(high, heads) + dot(low, heads)
    delta_ref[...] = jnp.transpose(delta)
    first = iota((ROWS, 2 * HD), 1) < HD

    def halves(t):
        none = jnp.zeros_like(t)
        return jnp.concatenate([jnp.where(first, t, none), jnp.where(first, none, t)], 0)

    def joined(t):
        return jnp.where(first, t[:ROWS], t[ROWS:]).astype(bf16)

    for pair in range(HEADS // 2):
        lanes = slice(pair * 2 * HD, (pair + 1) * 2 * HD)
        kp, qp, vp, agp = k_ref[:, lanes], q_ref[:, lanes], v_ref[:, lanes], ag_ref[:, lanes]
        inner_ref[0] = dot(halves(vp[:ROWS]), agp, NT)
        inner_ref[1] = dot(halves(agp[:ROWS]), vp, NT)
        for half in range(2):
            head = 2 * pair + half
            for c in range(ROWS // STRIP):
                rows = slice(c * STRIP, (c + 1) * STRIP)
                place = slice(half * ROWS + c * STRIP, half * ROWS + (c + 1) * STRIP)
                off = inner_ref[0, place, :] - delta_ref[head : head + 1, :]
                prob = pcol_ref[head, rows, :].astype(f32)
                score_ref[0, place, :] = (prob * (off * HD**-0.5)).astype(bf16)
                off = inner_ref[1, place, :] - delta[rows, head : head + 1]
                prob = prow_ref[head, rows, :].astype(f32)
                score_ref[1, place, :] = (prob * (off * HD**-0.5)).astype(bf16)
        two = slice(2 * pair, 2 * pair + 2)
        kg_ref[:, lanes] = joined(dot(score_ref[0], qp))
        qg_ref[:, lanes] = joined(dot(score_ref[1], kp))
        vg_ref[:, lanes] = joined(dot(pcol_ref[two].reshape(2 * ROWS, L), agp))
    total = wide_ref[:ROWS, :]
    total += dot(qg_ref[...], wq_ref[...], NT)
    total += dot(kg_ref[...], wk_ref[...], NT)
    total += dot(vg_ref[...], wv_ref[...], NT)
    out_ref[...] = total.astype(bf16)


def backward(summed, got, kept, ln_gain, w_proj, w_out, w_query, w_key, w_value):
    q, k, v, att, prow, pcol, unit, inv, proj = kept
    width = HEADS * HD
    moved = (unit, w_out, att, v, k, q, prow, pcol, w_query, w_key, w_value)
    return call(
        backward_kernel,
        (shape((ROWS, D), bf16), shape((1,), f32)),
        [VMEM] * (6 + len(moved)),
        (VMEM, SMEM),
        [
            pltpu.VMEM((L, D), f32),
            pltpu.VMEM((L, D), bf16),
            pltpu.VMEM((L, width), bf16),
            pltpu.VMEM((ROWS, width), bf16),
            pltpu.VMEM((ROWS, width), bf16),
            pltpu.VMEM((ROWS, width), bf16),
            pltpu.VMEM((E, L), f32),
            pltpu.VMEM((2, 2 * ROWS, L), f32),
            pltpu.VMEM((2, 2 * ROWS, L), bf16),
        ],
        flops=3 * 10**9,
        limit=12,
    )(summed, got, proj, w_proj, inv, ln_gain[None], *moved)


def spread(x, axes):
    return lax.all_to_all(x, axes, 0, 0)


def body(
    hidden,
    doc_len,
    doc_keep,
    w_query,
    w_key,
    w_value,
    w_out,
    ln_gain,
    w_proj,
    queries,
    query_mask,
    positive,
):
    own = pack_hidden(hidden, doc_keep)
    by_core = lax.ppermute(own, "core", SWAP)
    by_yhi = lax.ppermute(own, "yhi", SWAP)
    line = spread(pack_query(positive, queries, query_mask), "z")
    packed = repack(line, by_core)
    plane = spread(packed, ("ylo", "x"))
    by_yhi, _ = lax.optimization_barrier((by_yhi, packed))
    by_both = lax.ppermute(by_yhi, "core", SWAP)
    blocks = (own, by_core, by_yhi, by_both)
    keep, bias = marks_call(doc_len, blocks)
    *kept, embed = forward(
        keep, bias, blocks, w_query, w_key, w_value, w_out, ln_gain, w_proj
    )
    send, sums, weight = sums_call(plane, embed)
    table = spread(send, DP)
    partial = grads_call(table, plane, embed, sums, weight)
    summed, half = add_call(partial, lax.ppermute(partial, "core", SWAP))
    got = lax.ppermute(half, "yhi", SWAP)
    out, loss = backward(summed, got, kept, ln_gain, w_proj, w_out, w_query, w_key, w_value)
    return (out, loss[0])


def solution(mesh):
    fine = Mesh(np.asarray(mesh.devices).reshape(SIZES), AXES)
    placed = (
        P(AXES, None),
        P(DP),
        P(AXES),
        P(),
        P(),
        P(),
        P(),
        P(),
        P(),
        P(AXES, None, None),
        P(AXES, None),
        P(AXES),
    )
    return jax.shard_map(
        body, mesh=fine, in_specs=placed, out_specs=(P(AXES, None), P()), check_vma=False
    )
```

```python
import jax
import jax.numpy as jnp
import numpy as np
from jax import lax
from jax.experimental import pallas as pl
from jax.experimental.pallas import tpu as pltpu
from jax.sharding import Mesh, PartitionSpec as P

D = 1024
HEADS = 8
HD = 64
E = 128
QLEN = 32
L = 512
ROWS = 128
DOCS = 128
QSET = 128
AUX = 16
TAIL = 8
TAU = 0.05
GRAD_SCALE = 1024.0
NEG = -1e30
AXES = ("z", "ylo", "x", "yhi", "core")
SIZES = (16, 2, 4, 2, 2)
DP = ("z", "ylo", "x")
LINE = 16
PLANE = 8
CHUNK = LINE * QLEN
STRIP = 64
THIN = 32
MARKS_FLOPS = 10**8
LOG2E = 1.4426950408889634
SWAP = [(0, 1), (1, 0)]
bf16 = jnp.bfloat16
f32 = jnp.float32
i32 = jnp.int32
BLOCK = pl.BlockSpec()
VMEM = pl.BlockSpec(memory_space=pltpu.VMEM)
ANY = pl.BlockSpec(memory_space=pl.ANY)
HBM = pl.BlockSpec(memory_space=pltpu.MemorySpace.HBM)
SMEM = pl.BlockSpec(memory_space=pltpu.SMEM)
NN = (((1,), (0,)), ((), ()))
NT = (((1,), (1,)), ((), ()))
TN = (((0,), (0,)), ((), ()))


def dot(left, right, dims=NN):
    return lax.dot_general(left, right, dims, preferred_element_type=f32)


def iota(shape, dim):
    return lax.broadcasted_iota(i32, shape, dim)


def select(x, choice):
    choice = choice.astype(bf16)
    high = x.astype(bf16)
    rest = x - high.astype(f32)
    middle = rest.astype(bf16)
    low = (rest - middle.astype(f32)).astype(bf16)
    return dot(high, choice) + (dot(middle, choice) + dot(low, choice))


def position():
    return lax.axis_index("yhi") * 2 + lax.axis_index("core"), lax.axis_index(DP)


def call(kernel, outs, ins, out_specs=None, scratch=(), flops=0, limit=12):
    return pl.pallas_call(
        kernel,
        out_shape=outs,
        in_specs=ins,
        out_specs=jax.tree.map(lambda _: BLOCK, outs) if out_specs is None else out_specs,
        scratch_shapes=list(scratch),
        compiler_params=pltpu.CompilerParams(vmem_limit_bytes=limit * 2**20),
        cost_estimate=pl.CostEstimate(flops=flops, bytes_accessed=4 * 2**20, transcendentals=0),
    )


class Moves:
    def __init__(self, sems):
        self.sems, self.used = sems, 0

    def start(self, source, target):
        copy = pltpu.make_async_copy(source, target, self.sems.at[self.used])
        self.used += 1
        copy.start()
        return copy


def shape(dims, kind):
    return jax.ShapeDtypeStruct(dims, kind)


def pack_kernel(pos_ref, queries_ref, mask_ref, skip_ref, hidden_any, query_out, own_out, sems):
    moves = Moves(sems)
    copy = moves.start(hidden_any, own_out.at[pl.ds(0, ROWS)])
    own_out[ROWS:, :] = jnp.zeros((AUX, D), bf16)
    own_out[ROWS:, :ROWS] = jnp.broadcast_to(skip_ref[...], (AUX, ROWS)).astype(f32).astype(bf16)
    q = queries_ref[...].astype(f32)
    qn = q * lax.rsqrt(jnp.sum(q * q, -1, keepdims=True) + 1e-06)
    repeat = (iota((QLEN, E), 1) % QLEN == iota((QLEN, E), 0)).astype(bf16)
    weights = dot(jnp.broadcast_to(mask_ref[...], (16, QLEN)), repeat)[:TAIL]
    target = jnp.broadcast_to(pos_ref[...], (TAIL, E)).astype(f32)
    row = iota((TAIL, E), 0)
    tail = jnp.where(row == 0, weights, jnp.where(row == 1, target, 0.0))
    packet = jnp.concatenate([qn, tail], 0).astype(bf16)
    query_out[...] = jnp.broadcast_to(packet[None], (LINE, QLEN + TAIL, E))
    copy.wait()


def pack(positive, queries, query_mask, hidden, doc_keep):
    return call(
        pack_kernel,
        (shape((LINE, QLEN + TAIL, E), bf16), shape((ROWS + AUX, D), bf16)),
        [BLOCK] * 4 + [ANY],
        (VMEM, VMEM),
        [pltpu.SemaphoreType.DMA((1,))],
        limit=56,
    )(positive[None], queries[0], query_mask, doc_keep[None], hidden)


def repack_kernel(line_ref, after_ref, out_ref):
    line = line_ref[...].astype(f32)
    queries = line[:, :QLEN, :].reshape(CHUNK, E)
    packed = jnp.concatenate([queries, line[:, QLEN, :], line[:, QLEN + 1, :]], 0).astype(bf16)
    for p in range(PLANE):
        out_ref[p] = packed


def repack(line, after):
    out = shape((PLANE, CHUNK + 2 * LINE, E), bf16)
    return call(repack_kernel, out, [VMEM, ANY], VMEM, limit=8)(line, after)


def marks_kernel(length_ref, x0_any, x1_any, x2_any, x3_any, keep_ref, bias_ref, skip_ref, sems):
    moves = Moves(sems)
    skips = [
        moves.start(source.at[pl.ds(ROWS, AUX), pl.ds(0, ROWS)], skip_ref.at[b])
        for b, source in enumerate((x0_any, x1_any, x2_any, x3_any))
    ]
    length = length_ref[0]
    me, _ = position()
    for b in range(4):
        skips[b].wait()
        start = jnp.bitwise_xor(me, b) * ROWS
        skip = skip_ref[b].astype(f32)[0:1, :]
        place = start + iota((1, ROWS), 1)
        valid = place < length
        bias = jnp.where(valid, 0.0, NEG)
        bias_ref[:, b * ROWS : (b + 1) * ROWS] = jnp.broadcast_to(bias, (8, ROWS))
        kept = jnp.where(valid & ((skip == 1.0) | (place == 0)), 1.0, 0.0)
        diagonal = iota((ROWS, ROWS), 0) == iota((ROWS, ROWS), 1)
        column = jnp.sum(jnp.where(diagonal, kept, 0.0), -1, keepdims=True)
        keep_ref[b * ROWS : (b + 1) * ROWS, :] = jnp.broadcast_to(column, (ROWS, E)).astype(bf16)


def marks_call(doc_len, blocks):
    return call(
        marks_kernel,
        (shape((L, E), bf16), shape((8, L), f32)),
        [SMEM] + [ANY] * 4,
        scratch=[pltpu.VMEM((4, AUX, ROWS), bf16), pltpu.SemaphoreType.DMA((4,))],
        flops=MARKS_FLOPS,
        limit=4,
    )(doc_len, *blocks)


def forward_kernel(
    keep_any,
    bias_any,
    x0_any,
    x1_any,
    x2_any,
    x3_any,
    wq_any,
    wk_any,
    wv_any,
    wo_any,
    gain_any,
    wp_any,
    q_any,
    k_any,
    v_any,
    att_any,
    prow_any,
    pcol_any,
    unit_any,
    inv_any,
    proj_any,
    embed_ref,
    x_ref,
    bias_ref,
    wq_ref,
    wk_ref,
    wv_ref,
    wo_ref,
    gain_ref,
    wp_ref,
    q_ref,
    k_ref,
    v_ref,
    att_ref,
    prow_ref,
    pcol_ref,
    unit_ref,
    inv_ref,
    proj_ref,
    score_ref,
    prob_ref,
    sems,
):
    moves = Moves(sems)
    blocks = [
        moves.start(source.at[pl.ds(0, ROWS)], x_ref.at[pl.ds(b * ROWS, ROWS)])
        for b, source in enumerate((x0_any, x1_any, x2_any, x3_any))
    ]
    at_k = moves.start(wk_any, wk_ref)
    at_keep = moves.start(keep_any, embed_ref.at[pl.ds(L, L)])
    at_bias = moves.start(bias_any, bias_ref)
    at_q = moves.start(wq_any, wq_ref)
    at_v = moves.start(wv_any, wv_ref)
    at_o = moves.start(wo_any, wo_ref)
    at_gain = moves.start(gain_any, gain_ref)
    at_p = moves.start(wp_any, wp_ref)
    ends = []
    for copy in blocks:
        copy.wait()
    at_k.wait()
    k_ref[...] = dot(x_ref[...], wk_ref[...]).astype(bf16)
    ends.append(moves.start(k_ref, k_any))
    at_q.wait()
    q_ref[...] = dot(x_ref[...], wq_ref[...]).astype(bf16)
    ends.append(moves.start(q_ref, q_any))
    at_v.wait()
    v_ref[...] = dot(x_ref[...], wv_ref[...]).astype(bf16)
    ends.append(moves.start(v_ref, v_any))
    at_keep.wait()
    at_bias.wait()
    bias = bias_ref[0:1, :]
    first = iota((L, 2 * HD), 1) < HD
    for pair in range(HEADS // 2):
        lanes = slice(pair * 2 * HD, (pair + 1) * 2 * HD)
        qp = q_ref[:, lanes] * jnp.array(HD**-0.5, bf16)
        mixes = []
        for half in range(2):
            head = 2 * pair + half
            own = first if half == 0 else ~first
            score_ref[half] = dot(jnp.where(own, qp, jnp.zeros_like(qp)), k_ref[:, lanes], NT)
            for c in range(L // STRIP):
                rows = slice(c * STRIP, (c + 1) * STRIP)
                scores = score_ref[half, rows, :] + bias
                expo = jnp.exp(scores - jnp.max(scores, -1, keepdims=True))
                probs = expo * (1.0 / jnp.sum(expo, -1, keepdims=True))
                prob_ref[half, rows, :] = probs.astype(bf16)
            prow_ref[head] = prob_ref[half, :ROWS, :]
            pcol_ref[head] = jnp.transpose(prob_ref[half, :, :ROWS])
            mixes.append(dot(prob_ref[half], v_ref[:, lanes]))
        att_ref[:, lanes] = jnp.where(first, mixes[0], mixes[1]).astype(bf16)
        two = pl.ds(2 * pair, 2)
        ends.append(moves.start(prow_ref.at[two], prow_any.at[two]))
        ends.append(moves.start(pcol_ref.at[two], pcol_any.at[two]))
    ends.append(moves.start(att_ref, att_any))
    at_o.wait()
    unit_ref[...] = dot(att_ref[...], wo_ref[...])
    at_gain.wait()
    for c in range(L // THIN):
        rows = slice(c * THIN, (c + 1) * THIN)
        mixed = x_ref[rows, :].astype(f32) + unit_ref[rows, :]
        centred = mixed - jnp.mean(mixed, -1, keepdims=True)
        inv = lax.rsqrt(jnp.mean(centred * centred, -1, keepdims=True) + 1e-05)
        unit = centred * inv
        unit_ref[rows, :] = unit
        inv_ref[rows, :] = jnp.broadcast_to(inv, (THIN, E))
        x_ref[rows, :] = (unit * gain_ref[...]).astype(bf16)
        if (c + 1) * THIN % ROWS == 0:
            done = pl.ds((c + 1) * THIN - ROWS, ROWS)
            ends.append(moves.start(unit_ref.at[done], unit_any.at[done]))
    ends.append(moves.start(inv_ref, inv_any))
    at_p.wait()
    proj = dot(x_ref[...], wp_ref[...])
    proj_ref[...] = proj
    ends.append(moves.start(proj_ref, proj_any))
    scale = lax.rsqrt(jnp.sum(proj * proj, -1, keepdims=True) + 1e-06)
    embed_ref[:L, :] = (proj * scale).astype(bf16)
    for copy in ends:
        copy.wait()


def forward(keep, bias, blocks, w_query, w_key, w_value, w_out, ln_gain, w_proj):
    width = HEADS * HD
    square = shape((L, width), bf16)
    outs = (
        square,
        square,
        square,
        square,
        shape((HEADS, ROWS, L), bf16),
        shape((HEADS, ROWS, L), bf16),
        shape((L, D), f32),
        shape((L, E), f32),
        shape((L, E), f32),
        shape((2 * L, E), bf16),
    )
    ins = [
        pltpu.VMEM((L, D), bf16),
        pltpu.VMEM((8, L), f32),
        pltpu.VMEM((D, width), bf16),
        pltpu.VMEM((D, width), bf16),
        pltpu.VMEM((D, width), bf16),
        pltpu.VMEM((width, D), bf16),
        pltpu.VMEM((1, D), f32),
        pltpu.VMEM((D, E), bf16),
    ]
    work = [
        pltpu.VMEM((2, L, L), f32),
        pltpu.VMEM((2, L, L), bf16),
        pltpu.SemaphoreType.DMA((32,)),
    ]
    return call(
        forward_kernel,
        outs,
        [ANY] * 6 + [HBM] * 6,
        tuple(HBM for _ in outs[:-1]) + (VMEM,),
        ins + [pltpu.VMEM(o.shape, o.dtype) for o in outs[:-1]] + work,
        flops=6 * 10**9,
        limit=52,
    )(keep, bias, *blocks, w_query, w_key, w_value, w_out, ln_gain[None], w_proj)


def sums_kernel(plane_ref, embed_ref, send_ref, sums_ref, weight_ref, keep_ref):
    keep_ref[...] = embed_ref[L:, :].astype(f32)
    for c in range(PLANE):
        total = jnp.zeros((8, CHUNK), f32)
        for b in range(4):
            rows = slice(b * ROWS, (b + 1) * ROWS)
            close = dot(embed_ref[rows, :], plane_ref[c, :CHUNK, :], NT)
            near = jnp.exp2(close * (LOG2E / TAU)) * keep_ref[rows, 0:1]
            total += jnp.sum(near.reshape(ROWS // 8, 8, CHUNK), 0)
        total = jnp.sum(total, 0, keepdims=True)
        for j in range(4):
            sums_ref[4 * c + j : 4 * c + j + 1, :] = total[:, j * E : (j + 1) * E]
    weights = jnp.concatenate([plane_ref[c, CHUNK : CHUNK + LINE, :] for c in range(PLANE)], 0)
    row, col = iota((QLEN, QSET), 0), iota((QLEN, QSET), 1)
    weight = jnp.zeros((QLEN, E), f32)
    for g in range(4):
        picked = dot((col == 4 * row + g).astype(bf16), weights)
        weight = jnp.where(col // QLEN == g, picked, weight)
    weight_ref[...] = weight
    parts = weight * TAU * jnp.log(sums_ref[...])
    source, place = iota((E, QSET), 0), iota((E, QSET), 1)
    table = select(parts, source // QLEN == place % 4)
    table = jnp.sum(jnp.where(col // 4 == row, table, 0.0), 0, keepdims=True)
    send_ref[...] = jnp.broadcast_to(table, (DOCS, QSET))


def sums_call(plane, embed):
    return call(
        sums_kernel,
        (shape((DOCS, QSET), f32), shape((QLEN, E), f32), shape((QLEN, E), f32)),
        [VMEM] * 2,
        (VMEM, VMEM, VMEM),
        [pltpu.VMEM((L, E), f32)],
        flops=10**9,
    )(plane, embed)


def grads_kernel(
    table_ref, sums_ref, weight_ref, plane_ref, embed_ref, out_ref, score_ref, couple_ref
):
    _, mine = position()
    table = table_ref[...]
    lse = jnp.log(jnp.sum(jnp.exp(table), 0, keepdims=True))
    targets = jnp.concatenate(
        [plane_ref[c, CHUNK + LINE :, :] for c in range(PLANE)], 0
    ).astype(f32)
    row, col = iota((QSET, QSET), 0), iota((QSET, QSET), 1)
    target = jnp.sum(jnp.where(row == col, targets, 0.0), 0, keepdims=True).astype(i32)
    hit = row == target
    gap = lse - jnp.sum(jnp.where(hit, table, 0.0), 0, keepdims=True)
    loss = jnp.sum(gap, -1, keepdims=True)
    own = jnp.sum(jnp.where(row == mine, table, 0.0), 0, keepdims=True)
    dscore = GRAD_SCALE * (jnp.exp(own - lse) - jnp.where(target == mine, 1.0, 0.0))
    group = iota((QLEN, QSET), 1) // 4 == iota((QLEN, QSET), 0)
    wide = select(jnp.where(group, dscore, 0.0), row % 4 == col // QLEN)
    coef = wide * weight_ref[...] / sums_ref[...]
    for c in range(PLANE):
        queries = plane_ref[c, :CHUNK, :]
        score_ref[c % 2] = dot(embed_ref[:L, :], queries, NT)
        factor = jnp.concatenate([coef[4 * c + j : 4 * c + j + 1, :] for j in range(4)], 1)
        for b in range(L // STRIP):
            rows = slice(b * STRIP, (b + 1) * STRIP)
            near = jnp.exp2(score_ref[c % 2, rows, :] * (LOG2E / TAU))
            couple_ref[c % 2, rows, :] = (near * factor).astype(bf16)
        part = dot(couple_ref[c % 2], queries)
        if c == 0:
            out_ref[:L, :] = part
        else:
            out_ref[:L, :] += part
    out_ref[:L, :] = out_ref[:L, :] * embed_ref[L:, :].astype(f32)
    out_ref[L:, :] = jnp.broadcast_to(loss, (8, E))


def grads_call(table, plane, embed, sums, weight):
    return call(
        grads_kernel,
        shape((L + 8, E), f32),
        [VMEM] * 5,
        VMEM,
        [pltpu.VMEM((2, L, CHUNK), f32), pltpu.VMEM((2, L, CHUNK), bf16)],
        flops=2 * 10**9,
    )(table, sums, weight, plane, embed)


def add_kernel(own_ref, got_ref, sum_ref, send_ref):
    for b in range(4):
        rows = slice(b * ROWS, (b + 1) * ROWS)
        other = (b ^ 1) * ROWS
        total = own_ref[rows, :] + got_ref[other : other + ROWS, :]
        sum_ref[rows, :] = total
        send_ref[rows, :] = total.astype(bf16)
    loss = own_ref[L:, :] + got_ref[L:, :]
    sum_ref[L:, :] = loss
    high = loss.astype(bf16).astype(f32)
    middle = (loss - high).astype(bf16).astype(f32)
    low = loss - high - middle
    send_ref[L : L + 16, :] = jnp.concatenate([high, middle], 0).astype(bf16)
    send_ref[L + 16 :, :] = jnp.concatenate([low, low], 0).astype(bf16)


def add_call(own, got):
    return call(add_kernel, (shape((L + 8, E), f32), shape((L + 32, E), bf16)), [VMEM] * 2, (VMEM, VMEM), limit=4)(own, got)


def backward_kernel(
    sum_ref,
    got_ref,
    proj_ref,
    wp_ref,
    inv_ref,
    gain_ref,
    unit_ref,
    wo_ref,
    att_ref,
    v_ref,
    k_ref,
    q_ref,
    prow_ref,
    pcol_ref,
    wq_ref,
    wk_ref,
    wv_ref,
    out_ref,
    loss_ref,
    wide_ref,
    mixed_ref,
    ag_ref,
    qg_ref,
    kg_ref,
    vg_ref,
    delta_ref,
    inner_ref,
    score_ref,
):
    tail = got_ref[L:, :].astype(f32)
    loss = sum_ref[L:, :] + (tail[0:8] + tail[8:16] + tail[16:24])
    loss_ref[0] = loss[0, 0]
    got = got_ref[:L, :].astype(f32)
    grad = sum_ref[:L, :] + jnp.concatenate([got[2 * ROWS :], got[: 2 * ROWS]], 0)
    proj = proj_ref[...]
    scale = lax.rsqrt(jnp.sum(proj * proj, -1, keepdims=True) + 1e-06)
    embed = proj * scale
    proj_grad = ((grad - embed * jnp.sum(embed * grad, -1, keepdims=True)) * scale).astype(bf16)
    wide_ref[...] = dot(proj_grad, wp_ref[...], NT)
    for c in range(L // THIN):
        rows = slice(c * THIN, (c + 1) * THIN)
        gained = wide_ref[rows, :] * gain_ref[...]
        unit = unit_ref[rows, :]
        along = jnp.mean(gained * unit, -1, keepdims=True)
        mixed = inv_ref[rows, 0:1] * (gained - jnp.mean(gained, -1, keepdims=True) - unit * along)
        if (c + 1) * THIN <= ROWS:
            wide_ref[rows, :] = mixed
        mixed_ref[rows, :] = mixed.astype(bf16)
    ag_ref[...] = dot(mixed_ref[...], wo_ref[...], NT).astype(bf16)
    product = ag_ref[...].astype(f32) * att_ref[...].astype(f32)
    high = product.astype(bf16)
    low = (product - high.astype(f32)).astype(bf16)
    heads = (iota((HEADS * HD, E), 0) // HD == iota((HEADS * HD, E), 1)).astype(bf16)
    delta = dot(high, heads) + dot(low, heads)
    delta_ref[...] = jnp.transpose(delta)
    first = iota((ROWS, 2 * HD), 1) < HD

    def halves(t):
        none = jnp.zeros_like(t)
        return jnp.concatenate([jnp.where(first, t, none), jnp.where(first, none, t)], 0)

    def joined(t):
        return jnp.where(first, t[:ROWS], t[ROWS:]).astype(bf16)

    for pair in range(HEADS // 2):
        lanes = slice(pair * 2 * HD, (pair + 1) * 2 * HD)
        kp, qp, vp, agp = k_ref[:, lanes], q_ref[:, lanes], v_ref[:, lanes], ag_ref[:, lanes]
        inner_ref[0] = dot(halves(vp[:ROWS]), agp, NT)
        inner_ref[1] = dot(halves(agp[:ROWS]), vp, NT)
        for half in range(2):
            head = 2 * pair + half
            for c in range(ROWS // STRIP):
                rows = slice(c * STRIP, (c + 1) * STRIP)
                place = slice(half * ROWS + c * STRIP, half * ROWS + (c + 1) * STRIP)
                off = inner_ref[0, place, :] - delta_ref[head : head + 1, :]
                prob = pcol_ref[head, rows, :].astype(f32)
                score_ref[0, place, :] = (prob * (off * HD**-0.5)).astype(bf16)
                off = inner_ref[1, place, :] - delta[rows, head : head + 1]
                prob = prow_ref[head, rows, :].astype(f32)
                score_ref[1, place, :] = (prob * (off * HD**-0.5)).astype(bf16)
        two = slice(2 * pair, 2 * pair + 2)
        kg_ref[:, lanes] = joined(dot(score_ref[0], qp))
        qg_ref[:, lanes] = joined(dot(score_ref[1], kp))
        vg_ref[:, lanes] = joined(dot(pcol_ref[two].reshape(2 * ROWS, L), agp))
    total = wide_ref[:ROWS, :]
    total += dot(qg_ref[...], wq_ref[...], NT)
    total += dot(kg_ref[...], wk_ref[...], NT)
    total += dot(vg_ref[...], wv_ref[...], NT)
    out_ref[...] = total.astype(bf16)


def backward(summed, got, kept, ln_gain, w_proj, w_out, w_query, w_key, w_value):
    q, k, v, att, prow, pcol, unit, inv, proj = kept
    width = HEADS * HD
    moved = (unit, w_out, att, v, k, q, prow, pcol, w_query, w_key, w_value)
    return call(
        backward_kernel,
        (shape((ROWS, D), bf16), shape((1,), f32)),
        [VMEM] * (6 + len(moved)),
        (VMEM, SMEM),
        [
            pltpu.VMEM((L, D), f32),
            pltpu.VMEM((L, D), bf16),
            pltpu.VMEM((L, width), bf16),
            pltpu.VMEM((ROWS, width), bf16),
            pltpu.VMEM((ROWS, width), bf16),
            pltpu.VMEM((ROWS, width), bf16),
            pltpu.VMEM((E, L), f32),
            pltpu.VMEM((2, 2 * ROWS, L), f32),
            pltpu.VMEM((2, 2 * ROWS, L), bf16),
        ],
        flops=3 * 10**9,
        limit=12,
    )(summed, got, proj, w_proj, inv, ln_gain[None], *moved)


def spread(x, axes):
    return lax.all_to_all(x, axes, 0, 0)


def body(
    hidden,
    doc_len,
    doc_keep,
    w_query,
    w_key,
    w_value,
    w_out,
    ln_gain,
    w_proj,
    queries,
    query_mask,
    positive,
):
    query_send, own = pack(positive, queries, query_mask, hidden, doc_keep)
    by_core = lax.ppermute(own, "core", SWAP)
    by_yhi = lax.ppermute(own, "yhi", SWAP)
    line = spread(query_send, "z")
    packed = repack(line, by_core)
    plane = spread(packed, ("ylo", "x"))
    by_yhi, _ = lax.optimization_barrier((by_yhi, packed))
    by_both = lax.ppermute(by_yhi, "core", SWAP)
    blocks = (own, by_core, by_yhi, by_both)
    keep, bias = marks_call(doc_len, blocks)
    *kept, embed = forward(
        keep, bias, blocks, w_query, w_key, w_value, w_out, ln_gain, w_proj
    )
    send, sums, weight = sums_call(plane, embed)
    table = spread(send, DP)
    partial = grads_call(table, plane, embed, sums, weight)
    summed, half = add_call(partial, lax.ppermute(partial, "core", SWAP))
    got = lax.ppermute(half, "yhi", SWAP)
    out, loss = backward(summed, got, kept, ln_gain, w_proj, w_out, w_query, w_key, w_value)
    return (out, loss[0])


def solution(mesh):
    fine = Mesh(np.asarray(mesh.devices).reshape(SIZES), AXES)
    placed = (
        P(AXES, None),
        P(DP),
        P(AXES),
        P(),
        P(),
        P(),
        P(),
        P(),
        P(),
        P(AXES, None, None),
        P(AXES, None),
        P(AXES),
    )
    return jax.shard_map(
        body, mesh=fine, in_specs=placed, out_specs=(P(AXES, None), P()), check_vma=False
    )
```

```python
import jax
import jax.numpy as jnp
import numpy as np
from jax import lax
from jax.experimental import pallas as pl
from jax.experimental.pallas import tpu as pltpu
from jax.sharding import Mesh, PartitionSpec as P

D = 1024
HEADS = 8
HD = 64
E = 128
QLEN = 32
L = 512
ROWS = 128
DOCS = 128
QSET = 128
AUX = 16
TAIL = 8
TAU = 0.05
GRAD_SCALE = 1024.0
NEG = -1e30
AXES = ("z", "ylo", "x", "yhi", "core")
SIZES = (16, 2, 4, 2, 2)
DP = ("z", "ylo", "x")
LINE = 16
PLANE = 8
CHUNK = LINE * QLEN
STRIP = 64
THIN = 32
MARKS_FLOPS = 10**8
LOG2E = 1.4426950408889634
SWAP = [(0, 1), (1, 0)]
bf16 = jnp.bfloat16
f32 = jnp.float32
i32 = jnp.int32
BLOCK = pl.BlockSpec()
VMEM = pl.BlockSpec(memory_space=pltpu.VMEM)
ANY = pl.BlockSpec(memory_space=pl.ANY)
HBM = pl.BlockSpec(memory_space=pltpu.MemorySpace.HBM)
SMEM = pl.BlockSpec(memory_space=pltpu.SMEM)
NN = (((1,), (0,)), ((), ()))
NT = (((1,), (1,)), ((), ()))
TN = (((0,), (0,)), ((), ()))


def dot(left, right, dims=NN):
    return lax.dot_general(left, right, dims, preferred_element_type=f32)


def iota(shape, dim):
    return lax.broadcasted_iota(i32, shape, dim)


def select(x, choice):
    choice = choice.astype(bf16)
    high = x.astype(bf16)
    rest = x - high.astype(f32)
    middle = rest.astype(bf16)
    low = (rest - middle.astype(f32)).astype(bf16)
    return dot(high, choice) + (dot(middle, choice) + dot(low, choice))


def position():
    return lax.axis_index("yhi") * 2 + lax.axis_index("core"), lax.axis_index(DP)


def call(kernel, outs, ins, out_specs=None, scratch=(), flops=0, limit=12):
    return pl.pallas_call(
        kernel,
        out_shape=outs,
        in_specs=ins,
        out_specs=jax.tree.map(lambda _: BLOCK, outs) if out_specs is None else out_specs,
        scratch_shapes=list(scratch),
        compiler_params=pltpu.CompilerParams(vmem_limit_bytes=limit * 2**20),
        cost_estimate=pl.CostEstimate(flops=flops, bytes_accessed=4 * 2**20, transcendentals=0),
    )


class Moves:
    def __init__(self, sems):
        self.sems, self.used = sems, 0

    def start(self, source, target):
        copy = pltpu.make_async_copy(source, target, self.sems.at[self.used])
        self.used += 1
        copy.start()
        return copy


def shape(dims, kind):
    return jax.ShapeDtypeStruct(dims, kind)


def pack_kernel(pos_ref, queries_ref, mask_ref, skip_ref, hidden_ref, query_out, own_out):
    own_out[:ROWS, :] = hidden_ref[...]
    own_out[ROWS:, :] = jnp.zeros((AUX, D), bf16)
    own_out[ROWS:, :ROWS] = jnp.broadcast_to(skip_ref[...], (AUX, ROWS)).astype(f32).astype(bf16)
    q = queries_ref[...].astype(f32)
    qn = q * lax.rsqrt(jnp.sum(q * q, -1, keepdims=True) + 1e-06)
    repeat = (iota((QLEN, E), 1) % QLEN == iota((QLEN, E), 0)).astype(bf16)
    weights = dot(jnp.broadcast_to(mask_ref[...], (16, QLEN)), repeat)[:TAIL]
    target = jnp.broadcast_to(pos_ref[...], (TAIL, E)).astype(f32)
    row = iota((TAIL, E), 0)
    tail = jnp.where(row == 0, weights, jnp.where(row == 1, target, 0.0))
    packet = jnp.concatenate([qn, tail], 0).astype(bf16)
    query_out[...] = jnp.broadcast_to(packet[None], (LINE, QLEN + TAIL, E))


def pack(positive, queries, query_mask, hidden, doc_keep):
    return call(
        pack_kernel,
        (shape((LINE, QLEN + TAIL, E), bf16), shape((ROWS + AUX, D), bf16)),
        [BLOCK] * 5,
        (VMEM, VMEM),
        limit=56,
    )(positive[None], queries[0], query_mask, doc_keep[None], hidden)


def repack_kernel(line_ref, after_ref, out_ref):
    line = line_ref[...].astype(f32)
    queries = line[:, :QLEN, :].reshape(CHUNK, E)
    packed = jnp.concatenate([queries, line[:, QLEN, :], line[:, QLEN + 1, :]], 0).astype(bf16)
    for p in range(PLANE):
        out_ref[p] = packed


def repack(line, after):
    out = shape((PLANE, CHUNK + 2 * LINE, E), bf16)
    return call(repack_kernel, out, [VMEM, ANY], VMEM, limit=8)(line, after)


def marks_kernel(length_ref, x0_any, x1_any, x2_any, x3_any, keep_ref, bias_ref, skip_ref, sems):
    moves = Moves(sems)
    skips = [
        moves.start(source.at[pl.ds(ROWS, AUX), pl.ds(0, ROWS)], skip_ref.at[b])
        for b, source in enumerate((x0_any, x1_any, x2_any, x3_any))
    ]
    length = length_ref[0]
    me, _ = position()
    for b in range(4):
        skips[b].wait()
        start = jnp.bitwise_xor(me, b) * ROWS
        skip = skip_ref[b].astype(f32)[0:1, :]
        place = start + iota((1, ROWS), 1)
        valid = place < length
        bias = jnp.where(valid, 0.0, NEG)
        bias_ref[:, b * ROWS : (b + 1) * ROWS] = jnp.broadcast_to(bias, (8, ROWS))
        kept = jnp.where(valid & ((skip == 1.0) | (place == 0)), 1.0, 0.0)
        diagonal = iota((ROWS, ROWS), 0) == iota((ROWS, ROWS), 1)
        column = jnp.sum(jnp.where(diagonal, kept, 0.0), -1, keepdims=True)
        keep_ref[b * ROWS : (b + 1) * ROWS, :] = jnp.broadcast_to(column, (ROWS, E)).astype(bf16)


def marks_call(doc_len, blocks):
    return call(
        marks_kernel,
        (shape((L, E), bf16), shape((8, L), f32)),
        [SMEM] + [ANY] * 4,
        scratch=[pltpu.VMEM((4, AUX, ROWS), bf16), pltpu.SemaphoreType.DMA((4,))],
        flops=MARKS_FLOPS,
        limit=4,
    )(doc_len, *blocks)


def forward_kernel(
    keep_any,
    bias_any,
    x0_any,
    x1_any,
    x2_any,
    x3_any,
    wq_any,
    wk_any,
    wv_any,
    wo_any,
    gain_any,
    wp_any,
    q_any,
    k_any,
    v_any,
    att_any,
    prow_any,
    pcol_any,
    unit_any,
    inv_any,
    proj_any,
    embed_ref,
    x_ref,
    bias_ref,
    wq_ref,
    wk_ref,
    wv_ref,
    wo_ref,
    gain_ref,
    wp_ref,
    q_ref,
    k_ref,
    v_ref,
    att_ref,
    prow_ref,
    pcol_ref,
    unit_ref,
    inv_ref,
    proj_ref,
    score_ref,
    prob_ref,
    sems,
):
    moves = Moves(sems)
    blocks = [
        moves.start(source.at[pl.ds(0, ROWS)], x_ref.at[pl.ds(b * ROWS, ROWS)])
        for b, source in enumerate((x0_any, x1_any, x2_any, x3_any))
    ]
    at_k = moves.start(wk_any, wk_ref)
    at_keep = moves.start(keep_any, embed_ref.at[pl.ds(L, L)])
    at_bias = moves.start(bias_any, bias_ref)
    at_q = moves.start(wq_any, wq_ref)
    at_v = moves.start(wv_any, wv_ref)
    at_o = moves.start(wo_any, wo_ref)
    at_gain = moves.start(gain_any, gain_ref)
    at_p = moves.start(wp_any, wp_ref)
    ends = []
    for copy in blocks:
        copy.wait()
    at_k.wait()
    k_ref[...] = dot(x_ref[...], wk_ref[...]).astype(bf16)
    ends.append(moves.start(k_ref, k_any))
    at_q.wait()
    q_ref[...] = dot(x_ref[...], wq_ref[...]).astype(bf16)
    ends.append(moves.start(q_ref, q_any))
    at_v.wait()
    v_ref[...] = dot(x_ref[...], wv_ref[...]).astype(bf16)
    ends.append(moves.start(v_ref, v_any))
    at_keep.wait()
    at_bias.wait()
    bias = bias_ref[0:1, :]
    first = iota((L, 2 * HD), 1) < HD
    for pair in range(HEADS // 2):
        lanes = slice(pair * 2 * HD, (pair + 1) * 2 * HD)
        qp = q_ref[:, lanes] * jnp.array(HD**-0.5, bf16)
        mixes = []
        for half in range(2):
            head = 2 * pair + half
            own = first if half == 0 else ~first
            score_ref[half] = dot(jnp.where(own, qp, jnp.zeros_like(qp)), k_ref[:, lanes], NT)
            for c in range(L // STRIP):
                rows = slice(c * STRIP, (c + 1) * STRIP)
                scores = score_ref[half, rows, :] + bias
                expo = jnp.exp(scores - jnp.max(scores, -1, keepdims=True))
                probs = expo * (1.0 / jnp.sum(expo, -1, keepdims=True))
                prob_ref[half, rows, :] = probs.astype(bf16)
            prow_ref[head] = prob_ref[half, :ROWS, :]
            pcol_ref[head] = jnp.transpose(prob_ref[half, :, :ROWS])
            mixes.append(dot(prob_ref[half], v_ref[:, lanes]))
        att_ref[:, lanes] = jnp.where(first, mixes[0], mixes[1]).astype(bf16)
        two = pl.ds(2 * pair, 2)
        ends.append(moves.start(prow_ref.at[two], prow_any.at[two]))
        ends.append(moves.start(pcol_ref.at[two], pcol_any.at[two]))
    ends.append(moves.start(att_ref, att_any))
    at_o.wait()
    unit_ref[...] = dot(att_ref[...], wo_ref[...])
    at_gain.wait()
    for c in range(L // THIN):
        rows = slice(c * THIN, (c + 1) * THIN)
        mixed = x_ref[rows, :].astype(f32) + unit_ref[rows, :]
        centred = mixed - jnp.mean(mixed, -1, keepdims=True)
        inv = lax.rsqrt(jnp.mean(centred * centred, -1, keepdims=True) + 1e-05)
        unit = centred * inv
        unit_ref[rows, :] = unit
        inv_ref[rows, :] = jnp.broadcast_to(inv, (THIN, E))
        x_ref[rows, :] = (unit * gain_ref[...]).astype(bf16)
        if (c + 1) * THIN % ROWS == 0:
            done = pl.ds((c + 1) * THIN - ROWS, ROWS)
            ends.append(moves.start(unit_ref.at[done], unit_any.at[done]))
    ends.append(moves.start(inv_ref, inv_any))
    at_p.wait()
    proj = dot(x_ref[...], wp_ref[...])
    proj_ref[...] = proj
    ends.append(moves.start(proj_ref, proj_any))
    scale = lax.rsqrt(jnp.sum(proj * proj, -1, keepdims=True) + 1e-06)
    embed_ref[:L, :] = (proj * scale).astype(bf16)
    for copy in ends:
        copy.wait()


def forward(keep, bias, blocks, w_query, w_key, w_value, w_out, ln_gain, w_proj):
    width = HEADS * HD
    square = shape((L, width), bf16)
    outs = (
        square,
        square,
        square,
        square,
        shape((HEADS, ROWS, L), bf16),
        shape((HEADS, ROWS, L), bf16),
        shape((L, D), f32),
        shape((L, E), f32),
        shape((L, E), f32),
        shape((2 * L, E), bf16),
    )
    ins = [
        pltpu.VMEM((L, D), bf16),
        pltpu.VMEM((8, L), f32),
        pltpu.VMEM((D, width), bf16),
        pltpu.VMEM((D, width), bf16),
        pltpu.VMEM((D, width), bf16),
        pltpu.VMEM((width, D), bf16),
        pltpu.VMEM((1, D), f32),
        pltpu.VMEM((D, E), bf16),
    ]
    work = [
        pltpu.VMEM((2, L, L), f32),
        pltpu.VMEM((2, L, L), bf16),
        pltpu.SemaphoreType.DMA((32,)),
    ]
    return call(
        forward_kernel,
        outs,
        [ANY] * 6 + [HBM] * 6,
        tuple(HBM for _ in outs[:-1]) + (VMEM,),
        ins + [pltpu.VMEM(o.shape, o.dtype) for o in outs[:-1]] + work,
        flops=6 * 10**9,
        limit=52,
    )(keep, bias, *blocks, w_query, w_key, w_value, w_out, ln_gain[None], w_proj)


def sums_kernel(plane_ref, embed_ref, send_ref, sums_ref, weight_ref, keep_ref):
    keep_ref[...] = embed_ref[L:, :].astype(f32)
    for c in range(PLANE):
        total = jnp.zeros((8, CHUNK), f32)
        for b in range(4):
            rows = slice(b * ROWS, (b + 1) * ROWS)
            close = dot(embed_ref[rows, :], plane_ref[c, :CHUNK, :], NT)
            near = jnp.exp2(close * (LOG2E / TAU)) * keep_ref[rows, 0:1]
            total += jnp.sum(near.reshape(ROWS // 8, 8, CHUNK), 0)
        total = jnp.sum(total, 0, keepdims=True)
        for j in range(4):
            sums_ref[4 * c + j : 4 * c + j + 1, :] = total[:, j * E : (j + 1) * E]
    weights = jnp.concatenate([plane_ref[c, CHUNK : CHUNK + LINE, :] for c in range(PLANE)], 0)
    row, col = iota((QLEN, QSET), 0), iota((QLEN, QSET), 1)
    weight = jnp.zeros((QLEN, E), f32)
    for g in range(4):
        picked = dot((col == 4 * row + g).astype(bf16), weights)
        weight = jnp.where(col // QLEN == g, picked, weight)
    weight_ref[...] = weight
    parts = weight * TAU * jnp.log(sums_ref[...])
    source, place = iota((E, QSET), 0), iota((E, QSET), 1)
    table = select(parts, source // QLEN == place % 4)
    table = jnp.sum(jnp.where(col // 4 == row, table, 0.0), 0, keepdims=True)
    send_ref[...] = jnp.broadcast_to(table, (DOCS, QSET))


def sums_call(plane, embed):
    return call(
        sums_kernel,
        (shape((DOCS, QSET), f32), shape((QLEN, E), f32), shape((QLEN, E), f32)),
        [VMEM] * 2,
        (VMEM, VMEM, VMEM),
        [pltpu.VMEM((L, E), f32)],
        flops=10**9,
    )(plane, embed)


def grads_kernel(
    table_ref, sums_ref, weight_ref, plane_ref, embed_ref, out_ref, score_ref, couple_ref
):
    _, mine = position()
    table = table_ref[...]
    lse = jnp.log(jnp.sum(jnp.exp(table), 0, keepdims=True))
    targets = jnp.concatenate(
        [plane_ref[c, CHUNK + LINE :, :] for c in range(PLANE)], 0
    ).astype(f32)
    row, col = iota((QSET, QSET), 0), iota((QSET, QSET), 1)
    target = jnp.sum(jnp.where(row == col, targets, 0.0), 0, keepdims=True).astype(i32)
    hit = row == target
    gap = lse - jnp.sum(jnp.where(hit, table, 0.0), 0, keepdims=True)
    loss = jnp.sum(gap, -1, keepdims=True)
    own = jnp.sum(jnp.where(row == mine, table, 0.0), 0, keepdims=True)
    dscore = GRAD_SCALE * (jnp.exp(own - lse) - jnp.where(target == mine, 1.0, 0.0))
    group = iota((QLEN, QSET), 1) // 4 == iota((QLEN, QSET), 0)
    wide = select(jnp.where(group, dscore, 0.0), row % 4 == col // QLEN)
    coef = wide * weight_ref[...] / sums_ref[...]
    for c in range(PLANE):
        queries = plane_ref[c, :CHUNK, :]
        score_ref[c % 2] = dot(embed_ref[:L, :], queries, NT)
        factor = jnp.concatenate([coef[4 * c + j : 4 * c + j + 1, :] for j in range(4)], 1)
        for b in range(L // STRIP):
            rows = slice(b * STRIP, (b + 1) * STRIP)
            near = jnp.exp2(score_ref[c % 2, rows, :] * (LOG2E / TAU))
            couple_ref[c % 2, rows, :] = (near * factor).astype(bf16)
        part = dot(couple_ref[c % 2], queries)
        if c == 0:
            out_ref[:L, :] = part
        else:
            out_ref[:L, :] += part
    out_ref[:L, :] = out_ref[:L, :] * embed_ref[L:, :].astype(f32)
    out_ref[L:, :] = jnp.broadcast_to(loss, (8, E))


def grads_call(table, plane, embed, sums, weight):
    return call(
        grads_kernel,
        shape((L + 8, E), f32),
        [VMEM] * 5,
        VMEM,
        [pltpu.VMEM((2, L, CHUNK), f32), pltpu.VMEM((2, L, CHUNK), bf16)],
        flops=2 * 10**9,
    )(table, sums, weight, plane, embed)


def add_kernel(own_ref, got_ref, sum_ref, send_ref):
    for b in range(4):
        rows = slice(b * ROWS, (b + 1) * ROWS)
        other = (b ^ 1) * ROWS
        total = own_ref[rows, :] + got_ref[other : other + ROWS, :]
        sum_ref[rows, :] = total
        send_ref[rows, :] = total.astype(bf16)
    loss = own_ref[L:, :] + got_ref[L:, :]
    sum_ref[L:, :] = loss
    high = loss.astype(bf16).astype(f32)
    middle = (loss - high).astype(bf16).astype(f32)
    low = loss - high - middle
    send_ref[L : L + 16, :] = jnp.concatenate([high, middle], 0).astype(bf16)
    send_ref[L + 16 :, :] = jnp.concatenate([low, low], 0).astype(bf16)


def add_call(own, got):
    return call(add_kernel, (shape((L + 8, E), f32), shape((L + 32, E), bf16)), [VMEM] * 2, (VMEM, VMEM), limit=4)(own, got)


def backward_kernel(
    sum_ref,
    got_ref,
    proj_ref,
    wp_ref,
    inv_ref,
    gain_ref,
    unit_ref,
    wo_ref,
    att_ref,
    v_ref,
    k_ref,
    q_ref,
    prow_ref,
    pcol_ref,
    wq_ref,
    wk_ref,
    wv_ref,
    out_ref,
    loss_ref,
    wide_ref,
    mixed_ref,
    ag_ref,
    qg_ref,
    kg_ref,
    vg_ref,
    delta_ref,
    inner_ref,
    score_ref,
):
    tail = got_ref[L:, :].astype(f32)
    loss = sum_ref[L:, :] + (tail[0:8] + tail[8:16] + tail[16:24])
    loss_ref[0] = loss[0, 0]
    got = got_ref[:L, :].astype(f32)
    grad = sum_ref[:L, :] + jnp.concatenate([got[2 * ROWS :], got[: 2 * ROWS]], 0)
    proj = proj_ref[...]
    scale = lax.rsqrt(jnp.sum(proj * proj, -1, keepdims=True) + 1e-06)
    embed = proj * scale
    proj_grad = ((grad - embed * jnp.sum(embed * grad, -1, keepdims=True)) * scale).astype(bf16)
    wide_ref[...] = dot(proj_grad, wp_ref[...], NT)
    for c in range(L // THIN):
        rows = slice(c * THIN, (c + 1) * THIN)
        gained = wide_ref[rows, :] * gain_ref[...]
        unit = unit_ref[rows, :]
        along = jnp.mean(gained * unit, -1, keepdims=True)
        mixed = inv_ref[rows, 0:1] * (gained - jnp.mean(gained, -1, keepdims=True) - unit * along)
        if (c + 1) * THIN <= ROWS:
            wide_ref[rows, :] = mixed
        mixed_ref[rows, :] = mixed.astype(bf16)
    ag_ref[...] = dot(mixed_ref[...], wo_ref[...], NT).astype(bf16)
    product = ag_ref[...].astype(f32) * att_ref[...].astype(f32)
    high = product.astype(bf16)
    low = (product - high.astype(f32)).astype(bf16)
    heads = (iota((HEADS * HD, E), 0) // HD == iota((HEADS * HD, E), 1)).astype(bf16)
    delta = dot(high, heads) + dot(low, heads)
    delta_ref[...] = jnp.transpose(delta)
    first = iota((ROWS, 2 * HD), 1) < HD

    def halves(t):
        none = jnp.zeros_like(t)
        return jnp.concatenate([jnp.where(first, t, none), jnp.where(first, none, t)], 0)

    def joined(t):
        return jnp.where(first, t[:ROWS], t[ROWS:]).astype(bf16)

    for pair in range(HEADS // 2):
        lanes = slice(pair * 2 * HD, (pair + 1) * 2 * HD)
        kp, qp, vp, agp = k_ref[:, lanes], q_ref[:, lanes], v_ref[:, lanes], ag_ref[:, lanes]
        inner_ref[0] = dot(halves(vp[:ROWS]), agp, NT)
        inner_ref[1] = dot(halves(agp[:ROWS]), vp, NT)
        for half in range(2):
            head = 2 * pair + half
            for c in range(ROWS // STRIP):
                rows = slice(c * STRIP, (c + 1) * STRIP)
                place = slice(half * ROWS + c * STRIP, half * ROWS + (c + 1) * STRIP)
                off = inner_ref[0, place, :] - delta_ref[head : head + 1, :]
                prob = pcol_ref[head, rows, :].astype(f32)
                score_ref[0, place, :] = (prob * (off * HD**-0.5)).astype(bf16)
                off = inner_ref[1, place, :] - delta[rows, head : head + 1]
                prob = prow_ref[head, rows, :].astype(f32)
                score_ref[1, place, :] = (prob * (off * HD**-0.5)).astype(bf16)
        two = slice(2 * pair, 2 * pair + 2)
        kg_ref[:, lanes] = joined(dot(score_ref[0], qp))
        qg_ref[:, lanes] = joined(dot(score_ref[1], kp))
        vg_ref[:, lanes] = joined(dot(pcol_ref[two].reshape(2 * ROWS, L), agp))
    total = wide_ref[:ROWS, :]
    total += dot(qg_ref[...], wq_ref[...], NT)
    total += dot(kg_ref[...], wk_ref[...], NT)
    total += dot(vg_ref[...], wv_ref[...], NT)
    out_ref[...] = total.astype(bf16)


def backward(summed, got, kept, ln_gain, w_proj, w_out, w_query, w_key, w_value):
    q, k, v, att, prow, pcol, unit, inv, proj = kept
    width = HEADS * HD
    moved = (unit, w_out, att, v, k, q, prow, pcol, w_query, w_key, w_value)
    return call(
        backward_kernel,
        (shape((ROWS, D), bf16), shape((1,), f32)),
        [VMEM] * (6 + len(moved)),
        (VMEM, SMEM),
        [
            pltpu.VMEM((L, D), f32),
            pltpu.VMEM((L, D), bf16),
            pltpu.VMEM((L, width), bf16),
            pltpu.VMEM((ROWS, width), bf16),
            pltpu.VMEM((ROWS, width), bf16),
            pltpu.VMEM((ROWS, width), bf16),
            pltpu.VMEM((E, L), f32),
            pltpu.VMEM((2, 2 * ROWS, L), f32),
            pltpu.VMEM((2, 2 * ROWS, L), bf16),
        ],
        flops=3 * 10**9,
        limit=12,
    )(summed, got, proj, w_proj, inv, ln_gain[None], *moved)


def spread(x, axes):
    return lax.all_to_all(x, axes, 0, 0)


def body(
    hidden,
    doc_len,
    doc_keep,
    w_query,
    w_key,
    w_value,
    w_out,
    ln_gain,
    w_proj,
    queries,
    query_mask,
    positive,
):
    query_send, own = pack(positive, queries, query_mask, hidden, doc_keep)
    by_core = lax.ppermute(own, "core", SWAP)
    by_yhi = lax.ppermute(own, "yhi", SWAP)
    line = spread(query_send, "z")
    packed = repack(line, by_core)
    plane = spread(packed, ("ylo", "x"))
    by_yhi, _ = lax.optimization_barrier((by_yhi, packed))
    by_both = lax.ppermute(by_yhi, "core", SWAP)
    blocks = (own, by_core, by_yhi, by_both)
    keep, bias = marks_call(doc_len, blocks)
    *kept, embed = forward(
        keep, bias, blocks, w_query, w_key, w_value, w_out, ln_gain, w_proj
    )
    send, sums, weight = sums_call(plane, embed)
    table = spread(send, DP)
    partial = grads_call(table, plane, embed, sums, weight)
    summed, half = add_call(partial, lax.ppermute(partial, "core", SWAP))
    got = lax.ppermute(half, "yhi", SWAP)
    out, loss = backward(summed, got, kept, ln_gain, w_proj, w_out, w_query, w_key, w_value)
    return (out, loss[0])


def solution(mesh):
    fine = Mesh(np.asarray(mesh.devices).reshape(SIZES), AXES)
    placed = (
        P(AXES, None),
        P(DP),
        P(AXES),
        P(),
        P(),
        P(),
        P(),
        P(),
        P(),
        P(AXES, None, None),
        P(AXES, None),
        P(AXES),
    )
    return jax.shard_map(
        body, mesh=fine, in_specs=placed, out_specs=(P(AXES, None), P()), check_vma=False
    )
```

```python
import jax
import jax.numpy as jnp
import numpy as np
from jax import lax
from jax.experimental import pallas as pl
from jax.experimental.pallas import tpu as pltpu
from jax.sharding import Mesh, PartitionSpec as P

D = 1024
HEADS = 8
HD = 64
E = 128
QLEN = 32
L = 512
ROWS = 128
DOCS = 128
QSET = 128
AUX = 16
TAIL = 8
TAU = 0.05
GRAD_SCALE = 1024.0
NEG = -1e30
AXES = ("z", "ylo", "x", "yhi", "core")
SIZES = (16, 2, 4, 2, 2)
DP = ("z", "ylo", "x")
LINE = 16
PLANE = 8
CHUNK = LINE * QLEN
STRIP = 64
THIN = 32
MARKS_FLOPS = 10**8
LOG2E = 1.4426950408889634
SWAP = [(0, 1), (1, 0)]
bf16 = jnp.bfloat16
f32 = jnp.float32
i32 = jnp.int32
BLOCK = pl.BlockSpec()
VMEM = pl.BlockSpec(memory_space=pltpu.VMEM)
ANY = pl.BlockSpec(memory_space=pl.ANY)
HBM = pl.BlockSpec(memory_space=pltpu.MemorySpace.HBM)
SMEM = pl.BlockSpec(memory_space=pltpu.SMEM)
NN = (((1,), (0,)), ((), ()))
NT = (((1,), (1,)), ((), ()))
TN = (((0,), (0,)), ((), ()))


def dot(left, right, dims=NN):
    return lax.dot_general(left, right, dims, preferred_element_type=f32)


def iota(shape, dim):
    return lax.broadcasted_iota(i32, shape, dim)


def select(x, choice):
    choice = choice.astype(bf16)
    high = x.astype(bf16)
    rest = x - high.astype(f32)
    middle = rest.astype(bf16)
    low = (rest - middle.astype(f32)).astype(bf16)
    return dot(high, choice) + (dot(middle, choice) + dot(low, choice))


def position():
    return lax.axis_index("yhi") * 2 + lax.axis_index("core"), lax.axis_index(DP)


def call(kernel, outs, ins, out_specs=None, scratch=(), flops=0, limit=12):
    return pl.pallas_call(
        kernel,
        out_shape=outs,
        in_specs=ins,
        out_specs=jax.tree.map(lambda _: BLOCK, outs) if out_specs is None else out_specs,
        scratch_shapes=list(scratch),
        compiler_params=pltpu.CompilerParams(vmem_limit_bytes=limit * 2**20),
        cost_estimate=pl.CostEstimate(flops=flops, bytes_accessed=4 * 2**20, transcendentals=0),
    )


class Moves:
    def __init__(self, sems):
        self.sems, self.used = sems, 0

    def start(self, source, target):
        copy = pltpu.make_async_copy(source, target, self.sems.at[self.used])
        self.used += 1
        copy.start()
        return copy


def shape(dims, kind):
    return jax.ShapeDtypeStruct(dims, kind)


def pack_kernel(pos_ref, queries_ref, mask_ref, skip_ref, hidden_ref, query_out, own_out):
    own_out[:ROWS, :] = hidden_ref[...]
    own_out[ROWS:, :] = jnp.zeros((AUX, D), bf16)
    own_out[ROWS:, :ROWS] = jnp.broadcast_to(skip_ref[...], (AUX, ROWS)).astype(f32).astype(bf16)
    q = queries_ref[...].astype(f32)
    qn = q * lax.rsqrt(jnp.sum(q * q, -1, keepdims=True) + 1e-06)
    repeat = (iota((QLEN, E), 1) % QLEN == iota((QLEN, E), 0)).astype(bf16)
    weights = dot(jnp.broadcast_to(mask_ref[...], (16, QLEN)), repeat)[:TAIL]
    target = jnp.broadcast_to(pos_ref[...], (TAIL, E)).astype(f32)
    row = iota((TAIL, E), 0)
    tail = jnp.where(row == 0, weights, jnp.where(row == 1, target, 0.0))
    packet = jnp.concatenate([qn, tail], 0).astype(bf16)
    query_out[...] = jnp.broadcast_to(packet[None], (LINE, QLEN + TAIL, E))


def pack(positive, queries, query_mask, hidden, doc_keep):
    return call(
        pack_kernel,
        (shape((LINE, QLEN + TAIL, E), bf16), shape((ROWS + AUX, D), bf16)),
        [BLOCK] * 5,
        (VMEM, VMEM),
        limit=56,
    )(positive[None], queries[0], query_mask, doc_keep[None], hidden)


def repack_kernel(line_ref, after_ref, out_ref):
    line = line_ref[...].astype(f32)
    queries = line[:, :QLEN, :].reshape(CHUNK, E)
    packed = jnp.concatenate([queries, line[:, QLEN, :], line[:, QLEN + 1, :]], 0).astype(bf16)
    for p in range(PLANE):
        out_ref[p] = packed


def repack(line, after):
    out = shape((PLANE, CHUNK + 2 * LINE, E), bf16)
    return call(repack_kernel, out, [VMEM, ANY], VMEM, limit=8)(line, after)


def marks_kernel(length_ref, x0_any, x1_any, x2_any, x3_any, keep_ref, bias_ref, skip_ref, sems):
    moves = Moves(sems)
    skips = [
        moves.start(source.at[pl.ds(ROWS, AUX), pl.ds(0, ROWS)], skip_ref.at[b])
        for b, source in enumerate((x0_any, x1_any, x2_any, x3_any))
    ]
    length = length_ref[0]
    me, _ = position()
    for b in range(4):
        skips[b].wait()
        start = jnp.bitwise_xor(me, b) * ROWS
        skip = skip_ref[b].astype(f32)[0:1, :]
        place = start + iota((1, ROWS), 1)
        valid = place < length
        bias = jnp.where(valid, 0.0, NEG)
        bias_ref[:, b * ROWS : (b + 1) * ROWS] = jnp.broadcast_to(bias, (8, ROWS))
        kept = jnp.where(valid & ((skip == 1.0) | (place == 0)), 1.0, 0.0)
        diagonal = iota((ROWS, ROWS), 0) == iota((ROWS, ROWS), 1)
        column = jnp.sum(jnp.where(diagonal, kept, 0.0), -1, keepdims=True)
        keep_ref[b * ROWS : (b + 1) * ROWS, :] = jnp.broadcast_to(column, (ROWS, E)).astype(bf16)


def marks_call(doc_len, blocks):
    return call(
        marks_kernel,
        (shape((L, E), bf16), shape((8, L), f32)),
        [SMEM] + [ANY] * 4,
        scratch=[pltpu.VMEM((4, AUX, ROWS), bf16), pltpu.SemaphoreType.DMA((4,))],
        flops=MARKS_FLOPS,
        limit=4,
    )(doc_len, *blocks)


def forward_kernel(
    keep_any,
    bias_any,
    x0_any,
    x1_any,
    x2_any,
    x3_any,
    wq_any,
    wk_any,
    wv_any,
    wo_any,
    gain_any,
    wp_any,
    q_any,
    k_any,
    v_any,
    att_any,
    prow_any,
    pcol_any,
    unit_any,
    inv_any,
    proj_any,
    embed_ref,
    x_ref,
    bias_ref,
    wq_ref,
    wk_ref,
    wv_ref,
    wo_ref,
    gain_ref,
    wp_ref,
    q_ref,
    k_ref,
    v_ref,
    att_ref,
    prow_ref,
    pcol_ref,
    unit_ref,
    inv_ref,
    proj_ref,
    score_ref,
    prob_ref,
    sems,
):
    moves = Moves(sems)
    blocks = [
        moves.start(source.at[pl.ds(0, ROWS)], x_ref.at[pl.ds(b * ROWS, ROWS)])
        for b, source in enumerate((x0_any, x1_any, x2_any, x3_any))
    ]
    at_k = moves.start(wk_any, wk_ref)
    at_keep = moves.start(keep_any, embed_ref.at[pl.ds(L, L)])
    at_bias = moves.start(bias_any, bias_ref)
    at_q = moves.start(wq_any, wq_ref)
    at_v = moves.start(wv_any, wv_ref)
    at_o = moves.start(wo_any, wo_ref)
    at_gain = moves.start(gain_any, gain_ref)
    at_p = moves.start(wp_any, wp_ref)
    ends = []
    for copy in blocks:
        copy.wait()
    at_k.wait()
    k_ref[...] = dot(x_ref[...], wk_ref[...]).astype(bf16)
    ends.append(moves.start(k_ref, k_any))
    at_q.wait()
    q_ref[...] = dot(x_ref[...], wq_ref[...]).astype(bf16)
    ends.append(moves.start(q_ref, q_any))
    at_v.wait()
    v_ref[...] = dot(x_ref[...], wv_ref[...]).astype(bf16)
    ends.append(moves.start(v_ref, v_any))
    at_keep.wait()
    at_bias.wait()
    bias = bias_ref[0:1, :]
    first = iota((L, 2 * HD), 1) < HD
    for pair in range(HEADS // 2):
        lanes = slice(pair * 2 * HD, (pair + 1) * 2 * HD)
        qp = q_ref[:, lanes] * jnp.array(HD**-0.5, bf16)
        mixes = []
        for half in range(2):
            head = 2 * pair + half
            own = first if half == 0 else ~first
            score_ref[half] = dot(jnp.where(own, qp, jnp.zeros_like(qp)), k_ref[:, lanes], NT)
            for c in range(L // STRIP):
                rows = slice(c * STRIP, (c + 1) * STRIP)
                scores = score_ref[half, rows, :] + bias
                expo = jnp.exp(scores - jnp.max(scores, -1, keepdims=True))
                probs = expo * (1.0 / jnp.sum(expo, -1, keepdims=True))
                prob_ref[half, rows, :] = probs.astype(bf16)
            prow_ref[head] = prob_ref[half, :ROWS, :]
            pcol_ref[head] = prob_ref[half, :, :ROWS]
            mixes.append(dot(prob_ref[half], v_ref[:, lanes]))
        att_ref[:, lanes] = jnp.where(first, mixes[0], mixes[1]).astype(bf16)
        two = pl.ds(2 * pair, 2)
        ends.append(moves.start(prow_ref.at[two], prow_any.at[two]))
        ends.append(moves.start(pcol_ref.at[two], pcol_any.at[two]))
    ends.append(moves.start(att_ref, att_any))
    at_o.wait()
    unit_ref[...] = dot(att_ref[...], wo_ref[...])
    at_gain.wait()
    for c in range(L // THIN):
        rows = slice(c * THIN, (c + 1) * THIN)
        mixed = x_ref[rows, :].astype(f32) + unit_ref[rows, :]
        centred = mixed - jnp.mean(mixed, -1, keepdims=True)
        inv = lax.rsqrt(jnp.mean(centred * centred, -1, keepdims=True) + 1e-05)
        unit = centred * inv
        unit_ref[rows, :] = unit
        inv_ref[rows, :] = jnp.broadcast_to(inv, (THIN, E))
        x_ref[rows, :] = (unit * gain_ref[...]).astype(bf16)
        if (c + 1) * THIN % ROWS == 0:
            done = pl.ds((c + 1) * THIN - ROWS, ROWS)
            ends.append(moves.start(unit_ref.at[done], unit_any.at[done]))
    ends.append(moves.start(inv_ref, inv_any))
    at_p.wait()
    proj = dot(x_ref[...], wp_ref[...])
    proj_ref[...] = proj
    ends.append(moves.start(proj_ref, proj_any))
    scale = lax.rsqrt(jnp.sum(proj * proj, -1, keepdims=True) + 1e-06)
    embed_ref[:L, :] = (proj * scale).astype(bf16)
    for copy in ends:
        copy.wait()


def forward(keep, bias, blocks, w_query, w_key, w_value, w_out, ln_gain, w_proj):
    width = HEADS * HD
    square = shape((L, width), bf16)
    outs = (
        square,
        square,
        square,
        square,
        shape((HEADS, ROWS, L), bf16),
        shape((HEADS, L, ROWS), bf16),
        shape((L, D), f32),
        shape((L, E), f32),
        shape((L, E), f32),
        shape((2 * L, E), bf16),
    )
    ins = [
        pltpu.VMEM((L, D), bf16),
        pltpu.VMEM((8, L), f32),
        pltpu.VMEM((D, width), bf16),
        pltpu.VMEM((D, width), bf16),
        pltpu.VMEM((D, width), bf16),
        pltpu.VMEM((width, D), bf16),
        pltpu.VMEM((1, D), f32),
        pltpu.VMEM((D, E), bf16),
    ]
    work = [
        pltpu.VMEM((2, L, L), f32),
        pltpu.VMEM((2, L, L), bf16),
        pltpu.SemaphoreType.DMA((32,)),
    ]
    return call(
        forward_kernel,
        outs,
        [ANY] * 6 + [HBM] * 6,
        tuple(HBM for _ in outs[:-1]) + (VMEM,),
        ins + [pltpu.VMEM(o.shape, o.dtype) for o in outs[:-1]] + work,
        flops=6 * 10**9,
        limit=52,
    )(keep, bias, *blocks, w_query, w_key, w_value, w_out, ln_gain[None], w_proj)


def turn_kernel(in_ref, out_ref):
    for head in range(HEADS):
        out_ref[head] = jnp.transpose(in_ref[head])


def turn(pcol):
    return call(turn_kernel, shape((HEADS, ROWS, L), bf16), [BLOCK], flops=5 * 10**9, limit=56)(pcol)


def sums_kernel(plane_ref, embed_ref, send_ref, sums_ref, weight_ref, keep_ref):
    keep_ref[...] = embed_ref[L:, :].astype(f32)
    for c in range(PLANE):
        total = jnp.zeros((8, CHUNK), f32)
        for b in range(4):
            rows = slice(b * ROWS, (b + 1) * ROWS)
            close = dot(embed_ref[rows, :], plane_ref[c, :CHUNK, :], NT)
            near = jnp.exp2(close * (LOG2E / TAU)) * keep_ref[rows, 0:1]
            total += jnp.sum(near.reshape(ROWS // 8, 8, CHUNK), 0)
        total = jnp.sum(total, 0, keepdims=True)
        for j in range(4):
            sums_ref[4 * c + j : 4 * c + j + 1, :] = total[:, j * E : (j + 1) * E]
    weights = jnp.concatenate([plane_ref[c, CHUNK : CHUNK + LINE, :] for c in range(PLANE)], 0)
    row, col = iota((QLEN, QSET), 0), iota((QLEN, QSET), 1)
    weight = jnp.zeros((QLEN, E), f32)
    for g in range(4):
        picked = dot((col == 4 * row + g).astype(bf16), weights)
        weight = jnp.where(col // QLEN == g, picked, weight)
    weight_ref[...] = weight
    parts = weight * TAU * jnp.log(sums_ref[...])
    source, place = iota((E, QSET), 0), iota((E, QSET), 1)
    table = select(parts, source // QLEN == place % 4)
    table = jnp.sum(jnp.where(col // 4 == row, table, 0.0), 0, keepdims=True)
    send_ref[...] = jnp.broadcast_to(table, (DOCS, QSET))


def sums_call(plane, embed):
    return call(
        sums_kernel,
        (shape((DOCS, QSET), f32), shape((QLEN, E), f32), shape((QLEN, E), f32)),
        [VMEM] * 2,
        (VMEM, VMEM, VMEM),
        [pltpu.VMEM((L, E), f32)],
        flops=10**9,
    )(plane, embed)


def grads_kernel(
    table_ref, sums_ref, weight_ref, plane_ref, embed_ref, out_ref, score_ref, couple_ref
):
    _, mine = position()
    table = table_ref[...]
    lse = jnp.log(jnp.sum(jnp.exp(table), 0, keepdims=True))
    targets = jnp.concatenate(
        [plane_ref[c, CHUNK + LINE :, :] for c in range(PLANE)], 0
    ).astype(f32)
    row, col = iota((QSET, QSET), 0), iota((QSET, QSET), 1)
    target = jnp.sum(jnp.where(row == col, targets, 0.0), 0, keepdims=True).astype(i32)
    hit = row == target
    gap = lse - jnp.sum(jnp.where(hit, table, 0.0), 0, keepdims=True)
    loss = jnp.sum(gap, -1, keepdims=True)
    own = jnp.sum(jnp.where(row == mine, table, 0.0), 0, keepdims=True)
    dscore = GRAD_SCALE * (jnp.exp(own - lse) - jnp.where(target == mine, 1.0, 0.0))
    group = iota((QLEN, QSET), 1) // 4 == iota((QLEN, QSET), 0)
    wide = select(jnp.where(group, dscore, 0.0), row % 4 == col // QLEN)
    coef = wide * weight_ref[...] / sums_ref[...]
    for c in range(PLANE):
        queries = plane_ref[c, :CHUNK, :]
        score_ref[c % 2] = dot(embed_ref[:L, :], queries, NT)
        factor = jnp.concatenate([coef[4 * c + j : 4 * c + j + 1, :] for j in range(4)], 1)
        for b in range(L // STRIP):
            rows = slice(b * STRIP, (b + 1) * STRIP)
            near = jnp.exp2(score_ref[c % 2, rows, :] * (LOG2E / TAU))
            couple_ref[c % 2, rows, :] = (near * factor).astype(bf16)
        part = dot(couple_ref[c % 2], queries)
        if c == 0:
            out_ref[:L, :] = part
        else:
            out_ref[:L, :] += part
    out_ref[:L, :] = out_ref[:L, :] * embed_ref[L:, :].astype(f32)
    out_ref[L:, :] = jnp.broadcast_to(loss, (8, E))


def grads_call(table, plane, embed, sums, weight):
    return call(
        grads_kernel,
        shape((L + 8, E), f32),
        [VMEM] * 5,
        VMEM,
        [pltpu.VMEM((2, L, CHUNK), f32), pltpu.VMEM((2, L, CHUNK), bf16)],
        flops=2 * 10**9,
    )(table, sums, weight, plane, embed)


def add_kernel(own_ref, got_ref, sum_ref, send_ref):
    for b in range(4):
        rows = slice(b * ROWS, (b + 1) * ROWS)
        other = (b ^ 1) * ROWS
        total = own_ref[rows, :] + got_ref[other : other + ROWS, :]
        sum_ref[rows, :] = total
        send_ref[rows, :] = total.astype(bf16)
    loss = own_ref[L:, :] + got_ref[L:, :]
    sum_ref[L:, :] = loss
    high = loss.astype(bf16).astype(f32)
    middle = (loss - high).astype(bf16).astype(f32)
    low = loss - high - middle
    send_ref[L : L + 16, :] = jnp.concatenate([high, middle], 0).astype(bf16)
    send_ref[L + 16 :, :] = jnp.concatenate([low, low], 0).astype(bf16)


def add_call(own, got):
    return call(add_kernel, (shape((L + 8, E), f32), shape((L + 32, E), bf16)), [VMEM] * 2, (VMEM, VMEM), limit=4)(own, got)


def backward_kernel(
    sum_ref,
    got_ref,
    proj_ref,
    wp_ref,
    inv_ref,
    gain_ref,
    unit_ref,
    wo_ref,
    att_ref,
    v_ref,
    k_ref,
    q_ref,
    prow_ref,
    pcol_ref,
    wq_ref,
    wk_ref,
    wv_ref,
    out_ref,
    loss_ref,
    wide_ref,
    mixed_ref,
    ag_ref,
    qg_ref,
    kg_ref,
    vg_ref,
    delta_ref,
    inner_ref,
    score_ref,
):
    tail = got_ref[L:, :].astype(f32)
    loss = sum_ref[L:, :] + (tail[0:8] + tail[8:16] + tail[16:24])
    loss_ref[0] = loss[0, 0]
    got = got_ref[:L, :].astype(f32)
    grad = sum_ref[:L, :] + jnp.concatenate([got[2 * ROWS :], got[: 2 * ROWS]], 0)
    proj = proj_ref[...]
    scale = lax.rsqrt(jnp.sum(proj * proj, -1, keepdims=True) + 1e-06)
    embed = proj * scale
    proj_grad = ((grad - embed * jnp.sum(embed * grad, -1, keepdims=True)) * scale).astype(bf16)
    wide_ref[...] = dot(proj_grad, wp_ref[...], NT)
    for c in range(L // THIN):
        rows = slice(c * THIN, (c + 1) * THIN)
        gained = wide_ref[rows, :] * gain_ref[...]
        unit = unit_ref[rows, :]
        along = jnp.mean(gained * unit, -1, keepdims=True)
        mixed = inv_ref[rows, 0:1] * (gained - jnp.mean(gained, -1, keepdims=True) - unit * along)
        if (c + 1) * THIN <= ROWS:
            wide_ref[rows, :] = mixed
        mixed_ref[rows, :] = mixed.astype(bf16)
    ag_ref[...] = dot(mixed_ref[...], wo_ref[...], NT).astype(bf16)
    product = ag_ref[...].astype(f32) * att_ref[...].astype(f32)
    high = product.astype(bf16)
    low = (product - high.astype(f32)).astype(bf16)
    heads = (iota((HEADS * HD, E), 0) // HD == iota((HEADS * HD, E), 1)).astype(bf16)
    delta = dot(high, heads) + dot(low, heads)
    delta_ref[...] = jnp.transpose(delta)
    first = iota((ROWS, 2 * HD), 1) < HD

    def halves(t):
        none = jnp.zeros_like(t)
        return jnp.concatenate([jnp.where(first, t, none), jnp.where(first, none, t)], 0)

    def joined(t):
        return jnp.where(first, t[:ROWS], t[ROWS:]).astype(bf16)

    for pair in range(HEADS // 2):
        lanes = slice(pair * 2 * HD, (pair + 1) * 2 * HD)
        kp, qp, vp, agp = k_ref[:, lanes], q_ref[:, lanes], v_ref[:, lanes], ag_ref[:, lanes]
        inner_ref[0] = dot(halves(vp[:ROWS]), agp, NT)
        inner_ref[1] = dot(halves(agp[:ROWS]), vp, NT)
        for half in range(2):
            head = 2 * pair + half
            for c in range(ROWS // STRIP):
                rows = slice(c * STRIP, (c + 1) * STRIP)
                place = slice(half * ROWS + c * STRIP, half * ROWS + (c + 1) * STRIP)
                off = inner_ref[0, place, :] - delta_ref[head : head + 1, :]
                prob = pcol_ref[head, rows, :].astype(f32)
                score_ref[0, place, :] = (prob * (off * HD**-0.5)).astype(bf16)
                off = inner_ref[1, place, :] - delta[rows, head : head + 1]
                prob = prow_ref[head, rows, :].astype(f32)
                score_ref[1, place, :] = (prob * (off * HD**-0.5)).astype(bf16)
        two = slice(2 * pair, 2 * pair + 2)
        kg_ref[:, lanes] = joined(dot(score_ref[0], qp))
        qg_ref[:, lanes] = joined(dot(score_ref[1], kp))
        vg_ref[:, lanes] = joined(dot(pcol_ref[two].reshape(2 * ROWS, L), agp))
    total = wide_ref[:ROWS, :]
    total += dot(qg_ref[...], wq_ref[...], NT)
    total += dot(kg_ref[...], wk_ref[...], NT)
    total += dot(vg_ref[...], wv_ref[...], NT)
    out_ref[...] = total.astype(bf16)


def backward(summed, got, kept, ln_gain, w_proj, w_out, w_query, w_key, w_value):
    q, k, v, att, prow, pcol, unit, inv, proj = kept
    width = HEADS * HD
    moved = (unit, w_out, att, v, k, q, prow, pcol, w_query, w_key, w_value)
    return call(
        backward_kernel,
        (shape((ROWS, D), bf16), shape((1,), f32)),
        [VMEM] * (6 + len(moved)),
        (VMEM, SMEM),
        [
            pltpu.VMEM((L, D), f32),
            pltpu.VMEM((L, D), bf16),
            pltpu.VMEM((L, width), bf16),
            pltpu.VMEM((ROWS, width), bf16),
            pltpu.VMEM((ROWS, width), bf16),
            pltpu.VMEM((ROWS, width), bf16),
            pltpu.VMEM((E, L), f32),
            pltpu.VMEM((2, 2 * ROWS, L), f32),
            pltpu.VMEM((2, 2 * ROWS, L), bf16),
        ],
        flops=3 * 10**9,
        limit=12,
    )(summed, got, proj, w_proj, inv, ln_gain[None], *moved)


def spread(x, axes):
    return lax.all_to_all(x, axes, 0, 0)


def body(
    hidden,
    doc_len,
    doc_keep,
    w_query,
    w_key,
    w_value,
    w_out,
    ln_gain,
    w_proj,
    queries,
    query_mask,
    positive,
):
    query_send, own = pack(positive, queries, query_mask, hidden, doc_keep)
    by_core = lax.ppermute(own, "core", SWAP)
    by_yhi = lax.ppermute(own, "yhi", SWAP)
    line = spread(query_send, "z")
    packed = repack(line, by_core)
    plane = spread(packed, ("ylo", "x"))
    by_yhi, _ = lax.optimization_barrier((by_yhi, packed))
    by_both = lax.ppermute(by_yhi, "core", SWAP)
    blocks = (own, by_core, by_yhi, by_both)
    keep, bias = marks_call(doc_len, blocks)
    *kept, embed = forward(
        keep, bias, blocks, w_query, w_key, w_value, w_out, ln_gain, w_proj
    )
    send, sums, weight = sums_call(plane, embed)
    kept[5] = turn(kept[5])
    table = spread(send, DP)
    partial = grads_call(table, plane, embed, sums, weight)
    summed, half = add_call(partial, lax.ppermute(partial, "core", SWAP))
    got = lax.ppermute(half, "yhi", SWAP)
    out, loss = backward(summed, got, kept, ln_gain, w_proj, w_out, w_query, w_key, w_value)
    return (out, loss[0])


def solution(mesh):
    fine = Mesh(np.asarray(mesh.devices).reshape(SIZES), AXES)
    placed = (
        P(AXES, None),
        P(DP),
        P(AXES),
        P(),
        P(),
        P(),
        P(),
        P(),
        P(),
        P(AXES, None, None),
        P(AXES, None),
        P(AXES),
    )
    return jax.shard_map(
        body, mesh=fine, in_specs=placed, out_specs=(P(AXES, None), P()), check_vma=False
    )
```
